32 devices in a mesh: grp: 8 (over z, y), ep: 4 (over x, core).
Axes of the slice: x: 2, y: 2, z: 4, core: 2. Of those that a mesh axis runs over, the one named last changes fastest.
Arguments:
- tokens: bfloat16 [8192, 2048], P(('grp', 'ep')), may hold values from -6 to 6
- cotangent: bfloat16 [8192, 2048], P(('grp', 'ep')), may hold values from -6 to 6
- pack_order: int32 [8], replicated, may hold values from 0 to 7, each once
- doc_lengths: int32 [8, 4], P('grp'), may hold values from 1 to 512, 1024 in all within a row
- doc_sets: int32 [8, 4], P('grp'), may hold values from 0 to 7
- routes: int32 [8192, 8], P(('grp', 'ep')), may hold values from 0 to 15, all different within a row; in each aligned block of 256 rows (0 to 255, 256 to 511, ...) at most 144 rows name the same one
- attention_gain: bfloat16 [2048], replicated, may hold values from 0.5 to 1.5
- query_gain: bfloat16 [2048], replicated, may hold values from 0.5 to 1.5
- key_gain: bfloat16 [2048], replicated, may hold values from 0.5 to 1.5
- feed_gain: bfloat16 [2048], replicated, may hold values from 0.5 to 1.5
- qkv_weight: bfloat16 [3, 2048, 2048], P(None, None, 'ep'), may hold values from -0.125 to 0.125
- out_weight: bfloat16 [2048, 2048], P('ep'), may hold values from -0.5 to 0.5
- router_weight: bfloat16 [2048, 16], replicated, may hold values from -0.0625 to 0.0625
- gate_weight: bfloat16 [16, 2048, 1024], P('ep'), may hold values from -0.125 to 0.125
- up_weight: bfloat16 [16, 2048, 1024], P('ep'), may hold values from -0.125 to 0.125
- down_weight: bfloat16 [16, 1024, 2048], P('ep'), may hold values from -1.5 to 1.5
- qkv_enter: bfloat16 [3, 2048, 128], replicated, may hold values from -0.125 to 0.125
- qkv_leave: bfloat16 [3, 128, 2048], P(None, None, 'ep'), may hold values from -0.375 to 0.375
- out_enter: bfloat16 [2048, 128], P('ep'), may hold values from -0.5 to 0.5
- out_leave: bfloat16 [128, 2048], replicated, may hold values from -0.375 to 0.375
- router_enter: bfloat16 [2048, 128], replicated, may hold values from -0.125 to 0.125
- router_leave: bfloat16 [128, 16], replicated, may hold values from -0.1875 to 0.1875
- gate_enter: bfloat16 [16, 2048, 128], P('ep'), may hold values from -0.125 to 0.125
- gate_leave: bfloat16 [16, 128, 1024], P('ep'), may hold values from -0.375 to 0.375
- up_enter: bfloat16 [16, 2048, 128], P('ep'), may hold values from -0.125 to 0.125
- up_leave: bfloat16 [16, 128, 1024], P('ep'), may hold values from -0.375 to 0.375
- down_enter: bfloat16 [16, 1024, 128], P('ep'), may hold values from -0.1875 to 0.1875
- down_leave: bfloat16 [16, 128, 2048], P('ep'), may hold values from -0.375 to 0.375
Outputs:
- layer_output: bfloat16 [8192, 2048], P(('grp', 'ep'))
- input_grad: bfloat16 [8192, 2048], P(('grp', 'ep'))
- qkv_enter_grad: float32 [3, 2048, 128], P(None, 'ep', 'grp')
- qkv_leave_grad: float32 [3, 128, 2048], P(None, 'grp', 'ep')
- out_enter_grad: float32 [2048, 128], P('ep', 'grp')
- out_leave_grad: float32 [128, 2048], P('grp', 'ep')
- router_enter_grad: float32 [2048, 128], P('ep', 'grp')
- router_leave_grad: float32 [128, 16], P('ep', 'grp')
- gate_enter_grad: float32 [16, 2048, 128], P('ep', 'grp')
- gate_leave_grad: float32 [16, 128, 1024], P('ep', None, 'grp')
- up_enter_grad: float32 [16, 2048, 128], P('ep', 'grp')
- up_leave_grad: float32 [16, 128, 1024], P('ep', None, 'grp')
- down_enter_grad: float32 [16, 1024, 128], P('ep', 'grp')
- down_leave_grad: float32 [16, 128, 2048], P('ep', None, 'grp')
The draws below stay inside these ranges and needn't reach their ends.
Inputs may be any that keep to these rules, and one draw needn't show every extreme that they name: `doc_lengths`: each row holds the 4 document lengths of a slot, summing to 1024. `routes`: each row names 8 different experts; among the rows of one device no expert is named more than 144 times.
All inputs are finite; a program needn't handle non-finite values.
Results may differ from the reference program's by a relative error of at most 0.024.
Values may be sent and summed in bfloat16 or wider, within the bound.
No kernel may reach another device: no remote copies, remote signals or barrier semaphores. Data moves between devices by JAX's collectives and lax.ppermute only.
A program may use at most 384 MiB of HBM per device.

```python
import math
import jax
import jax.numpy as jnp
import numpy as np
from jax import lax

D = 2048
HEADS = 16
HEAD_DIM = 128
FF = 1024
EXPERTS = 16
TOP = 8
SETS = 8
RANK = 16
NDOC = 4
TOK_DEV = 256
SR = 128
GROUP_TOK = 1024
TOKENS = 8192
MOST = 512
CAP = 144
N_GRP = 8
N_EP = 4


def place_ends(entries, own_key, low, high):
    index_at = [jax.random.randint(jax.random.fold_in(own_key, axis), (), 0, length) for axis, length in enumerate(entries.shape)]
    widest = entries.shape.index(max(entries.shape))
    neighbour = index_at[:widest] + [(index_at[widest] + 1) % entries.shape[widest]] + index_at[widest + 1:]
    return entries.at[tuple(index_at)].set(low).at[tuple(neighbour)].set(high)


def shard_levels(rng, extent, split, low, largest):
    loudness = 1.0
    for dim, blocks in split:
        heights = jax.random.uniform(jax.random.fold_in(jax.random.fold_in(rng, 6), dim), (blocks,), jnp.float32, low / len(split), largest / len(split))
        loudness = loudness * jnp.repeat(jnp.exp(heights), extent[dim] // blocks).reshape((-1,) + (1,) * (len(extent) - 1 - dim))
    return loudness


def split_up(amount, total, most, skew):
    portions = [(1 << 20) // math.isqrt(grade ** skew) + 1 for grade in range(2, amount + 1)]
    spare, holding = total - most - (amount - 1), [1] * (amount - 1)
    while spare > 0:
        free = [i for i in range(amount - 1) if holding[i] < most]
        mass, left = sum([portions[i] for i in free]), spare
        for i in free:
            addition = min(most - holding[i], max(1, left * portions[i] // mass), spare)
            holding[i] = holding[i] + addition
            spare = spare - addition
    return np.array([most] + holding)


def ragged_sizes(own_key, count, total, bound, lean):
    if count == 2:
        one = jax.random.randint(own_key, (), max(1, total - bound), min(bound, total - 1) + 1)
        return jnp.stack([one, total - one])
    sizes = jnp.asarray(split_up(count, total, bound, lean), jnp.int32)
    twos = (count - 1) // 2
    source_of, sink = sizes[1:1 + 2 * twos:2], sizes[2:2 + 2 * twos:2]
    margin = jnp.minimum(source_of - 1, bound - sink)
    shifted = jax.random.randint(jax.random.fold_in(own_key, 1), (twos,), 0, 1 << 20) % (margin + 1)
    sizes = sizes.at[1:1 + 2 * twos:2].set(source_of - shifted).at[2:2 + 2 * twos:2].set(sink + shifted)
    return sizes[jax.random.permutation(jax.random.fold_in(own_key, 2), count)]


def routed_block(stream_key, own, number, rows, amount, top, limit, lean):
    sequence = jax.random.permutation(stream_key, amount)
    packed, usual = shares(amount, rows * top, limit, lean, True), shares(amount, rows * top, limit, lean, False)
    places = jnp.arange(amount)

    def named(tallies, turn):
        used = int((tallies > 0).sum())
        fixed = max(1, used // 4)
        passed = fixed + (places - fixed + turn * (used - fixed)) % max(1, amount - fixed)
        return jnp.zeros((amount,), jnp.int32).at[sequence[jnp.where(places < fixed, places, passed)]].set(jnp.asarray(tallies, jnp.int32))

    tallies = jnp.where(number % 4 == 0, named(packed, number // 4), named(usual, number - number // 4 - 1))
    mixed = jax.random.permutation(jax.random.fold_in(own, 3), amount)
    source_of, sink = mixed[0:amount // 2 * 2:2], mixed[1:amount // 2 * 2:2]
    room = jnp.minimum(tallies[source_of] - 1, limit - tallies[sink]) // 2
    room = jnp.where((source_of == sequence[0]) | (sink == sequence[0]) | (tallies[sink] == 0), 0, jnp.maximum(room, 0))
    passed = jax.random.randint(jax.random.fold_in(own, 4), (amount // 2,), 0, 1 << 20) % (room + 1)
    tallies = tallies.at[source_of].add(-passed).at[sink].add(passed)
    items = jnp.searchsorted(jnp.cumsum(tallies), jnp.arange(rows * top), side="right").astype(jnp.int32)
    grid = items.reshape(top, rows).T
    grid = grid[jax.random.permutation(jax.random.fold_in(own, 1), rows)]
    turn = jax.random.randint(jax.random.fold_in(own, 2), (rows, 1), 0, top)
    return jnp.take_along_axis(grid, (jnp.arange(top)[None, :] + turn) % top, axis=1)


def shares(number_of, total, reach, slope, full):
    weights = [(1 << 20) // math.isqrt(standing ** slope) + 1 for standing in range(1, number_of + 1)]
    largest = reach if full else min(reach, max(-(-total // number_of), total * weights[0] // sum(weights)))
    least = 1 if total - largest >= number_of - 1 else 0
    given, surplus = [largest] + [least] * (number_of - 1), total - largest - least * (number_of - 1)
    while surplus > 0:
        free = [i for i in range(1, number_of) if given[i] < largest] or [i for i in range(1, number_of) if given[i] < reach]
        whole, left = sum([weights[i] for i in free]), surplus
        for i in free:
            extra = min(reach - given[i], max(1, left * weights[i] // whole), surplus)
            given[i] = given[i] + extra
            surplus = surplus - extra
    return np.array(given)


def scatter_about(rng, extent, width, bound, cuts=(), kind=jnp.bfloat16):
    loudness = shard_levels(rng, extent, cuts, -0.22, 0.18) if cuts else 1.0
    values = jax.random.normal(rng, extent, jnp.float32) * width * loudness
    return jnp.minimum(jnp.maximum(values, -bound), bound).astype(kind)


def setup_inputs(seed: int = 0) -> dict:
    key_of = jax.random.split(jax.random.key(seed), 29)
    tokens = scatter_about(key_of[0], (TOKENS, D), 1.0, 6.0, ((0, 32),))
    cotangent = scatter_about(key_of[1], (TOKENS, D), 1.0, 6.0, ((0, 32),))
    pack_order = jax.random.permutation(key_of[2], N_GRP).astype(jnp.int32)
    doc_lengths = jax.vmap(lambda own: ragged_sizes(own, NDOC, GROUP_TOK, MOST, 2))(jax.random.split(key_of[3], N_GRP)).reshape((N_GRP, NDOC)).astype(jnp.int32)
    doc_sets = place_ends(jax.random.randint(key_of[4], (N_GRP, NDOC), 0, SETS), jax.random.fold_in(key_of[4], 1), 0, SETS - 1).astype(jnp.int32)
    routes_keys = jax.random.split(jax.random.fold_in(key_of[5], 1), TOKENS // TOK_DEV)
    routes_turns = jax.random.permutation(jax.random.fold_in(key_of[5], 3), TOKENS // TOK_DEV)
    routes = jax.vmap(lambda own, number: routed_block(jax.random.fold_in(key_of[5], 2), own, number, TOK_DEV, EXPERTS, TOP, CAP, 1))(routes_keys, routes_turns).reshape((TOKENS, TOP))
    attention_gain = jnp.clip(1.0 + 0.1 * jax.random.normal(key_of[6], (D,), jnp.float32), 0.5, 1.5).astype(jnp.bfloat16)
    query_gain = jnp.clip(1.0 + 0.1 * jax.random.normal(key_of[7], (D,), jnp.float32), 0.5, 1.5).astype(jnp.bfloat16)
    key_gain = jnp.clip(1.0 + 0.1 * jax.random.normal(key_of[8], (D,), jnp.float32), 0.5, 1.5).astype(jnp.bfloat16)
    feed_gain = jnp.clip(1.0 + 0.1 * jax.random.normal(key_of[9], (D,), jnp.float32), 0.5, 1.5).astype(jnp.bfloat16)
    qkv_weight = scatter_about(key_of[10], (3, D, D), D ** -0.5, 0.125, ((2, 4),))
    out_weight = scatter_about(key_of[11], (D, D), (D // 16) ** -0.5, 0.5, ((0, 4),))
    router_weight = scatter_about(key_of[12], (D, EXPERTS), (4 * D) ** -0.5, 0.0625)
    gate_weight = scatter_about(key_of[13], (EXPERTS, D, FF), D ** -0.5, 0.125, ((0, 4),))
    up_weight = scatter_about(key_of[14], (EXPERTS, D, FF), D ** -0.5, 0.125, ((0, 4),))
    down_weight = scatter_about(key_of[15], (EXPERTS, FF, D), (max(1, FF // 64)) ** -0.5, 1.5, ((0, 4),))
    qkv_enter = scatter_about(key_of[16], (3, D, SR), D ** -0.5, 0.125)
    qkv_leave = scatter_about(key_of[17], (3, SR, D), (16 * RANK) ** -0.5, 0.375, ((2, 4),))
    out_enter = scatter_about(key_of[18], (D, SR), (D // 16) ** -0.5, 0.5, ((0, 4),))
    out_leave = scatter_about(key_of[19], (SR, D), (16 * RANK) ** -0.5, 0.375)
    router_enter = scatter_about(key_of[20], (D, SR), D ** -0.5, 0.125)
    router_leave = scatter_about(key_of[21], (SR, EXPERTS), (64 * RANK) ** -0.5, 0.1875)
    gate_enter = scatter_about(key_of[22], (EXPERTS, D, SR), D ** -0.5, 0.125, ((0, 4),))
    gate_leave = scatter_about(key_of[23], (EXPERTS, SR, FF), (16 * RANK) ** -0.5, 0.375, ((0, 4),))
    up_enter = scatter_about(key_of[24], (EXPERTS, D, SR), D ** -0.5, 0.125, ((0, 4),))
    up_leave = scatter_about(key_of[25], (EXPERTS, SR, FF), (16 * RANK) ** -0.5, 0.375, ((0, 4),))
    down_enter = scatter_about(key_of[26], (EXPERTS, FF, SR), FF ** -0.5, 0.1875, ((0, 4),))
    down_leave = scatter_about(key_of[27], (EXPERTS, SR, D), (16 * RANK) ** -0.5, 0.375, ((0, 4),))
    return dict(tokens=tokens, cotangent=cotangent, pack_order=pack_order, doc_lengths=doc_lengths, doc_sets=doc_sets, routes=routes, attention_gain=attention_gain, query_gain=query_gain, key_gain=key_gain, feed_gain=feed_gain, qkv_weight=qkv_weight, out_weight=out_weight, router_weight=router_weight, gate_weight=gate_weight, up_weight=up_weight, down_weight=down_weight, qkv_enter=qkv_enter, qkv_leave=qkv_leave, out_enter=out_enter, out_leave=out_leave, router_enter=router_enter, router_leave=router_leave, gate_enter=gate_enter, gate_leave=gate_leave, up_enter=up_enter, up_leave=up_leave, down_enter=down_enter, down_leave=down_leave)


EPS = 1e-05
SCALE = 2.0
THETA = 10000.0
NEG = -1e+30
HIGH = lax.Precision.HIGHEST

@jax.custom_vjp
def low(v):
    return lax.optimization_barrier(v.astype(jnp.bfloat16)).astype(jnp.float32)

@jax.custom_vjp
def low_back(v):
    return v

def low_keep(v):
    return (low(v), None)

def low_pass(kept, grad):
    return (grad,)

def back_keep(v):
    return (v, None)

def back_low(kept, grad):
    return (low(grad),)
low.defvjp(low_keep, low_pass)
low_back.defvjp(back_keep, back_low)

def matmul(left, right):
    return jnp.dot(left, right, precision=HIGH, preferred_element_type=jnp.float32)

def rms_scale(value):
    return lax.rsqrt(lax.optimization_barrier(jnp.mean(value * value, axis=-1, keepdims=True)) + EPS)

def rotate(value, cosine, sine):
    half = value.shape[-1] // 2
    turned = jnp.concatenate([-value[..., half:], value[..., :half]], axis=-1)
    return value * cosine + turned * sine

def angles(position):
    half = HEAD_DIM // 2
    freq = THETA ** (-(jnp.arange(half, dtype=jnp.float32) * 2.0) / HEAD_DIM)
    phase = position.astype(jnp.float32)[:, None] * freq[None, :]
    cosine = jnp.concatenate([jnp.cos(phase), jnp.cos(phase)], axis=-1)
    sine = jnp.concatenate([jnp.sin(phase), jnp.sin(phase)], axis=-1)
    return (cosine[:, None, :], sine[:, None, :])

def documents(lengths, sets, count):
    ends = jnp.cumsum(lengths).astype(jnp.int32)
    starts = (ends - lengths).astype(jnp.int32)
    rows = jnp.arange(count, dtype=jnp.int32)
    doc_index = lax.optimization_barrier(jnp.sum((rows[:, None] >= ends[None, :]).astype(jnp.int32), axis=1)).astype(jnp.int32)
    member = doc_index[:, None] == jnp.arange(lengths.shape[0], dtype=jnp.int32)[None, :]
    position = (rows - lax.optimization_barrier(jnp.sum(jnp.where(member, starts[None, :], 0), axis=1))).astype(jnp.int32)
    chosen = lax.optimization_barrier(jnp.sum(jnp.where(member, sets[None, :], 0), axis=1)).astype(jnp.int32)
    columns = jnp.arange(SETS * RANK, dtype=jnp.int32) // RANK
    selector = (columns[None, :] == chosen[:, None]).astype(jnp.float32)
    return (doc_index, position, selector)

def attention(queries, keys, values, doc_index):
    count = queries.shape[0]
    block = min(512, count)
    key_rows = jnp.arange(count, dtype=jnp.int32)

    def one_block(index):
        start = (index * block).astype(jnp.int32)
        query_block = lax.dynamic_slice_in_dim(queries, start, block, 0)
        rows = start + jnp.arange(block, dtype=jnp.int32)
        doc_rows = lax.dynamic_slice_in_dim(doc_index, start, block, 0)
        allowed = (doc_rows[:, None] == doc_index[None, :]) & (key_rows[None, :] <= rows[:, None])
        raw = jnp.einsum('qhd,khd->hqk', query_block, keys, precision=HIGH)
        scores = low_back(raw) * HEAD_DIM ** (-0.5)
        scores = jnp.where(allowed[None], scores, NEG)
        probs = jax.nn.softmax(scores, axis=-1)
        return jnp.einsum('hqk,khd->qhd', low(probs), values, precision=HIGH)
    parts = lax.map(jax.checkpoint(one_block), jnp.arange(count // block, dtype=jnp.int32))
    return parts.reshape(count, -1)

def route_places(route):
    flat = route.reshape(N_EP, TOK_DEV * TOP)
    hot = (flat[:, :, None] == jnp.arange(EXPERTS, dtype=jnp.int32)[None, None, :]).astype(jnp.int32)
    rank = lax.optimization_barrier(jnp.sum((jnp.cumsum(hot, axis=1) - hot) * hot, axis=2)).astype(jnp.int32)
    source = jnp.arange(N_EP, dtype=jnp.int32)[:, None]
    return (flat * (N_EP * CAP) + source * CAP + rank).reshape(-1).astype(jnp.int32)

def one_expert(operands):
    rows, marks, g_enter, g_leave, u_enter, u_leave, d_enter, d_leave, w_gate, w_up, w_down = operands
    low_gate = low(low_back(matmul(rows, g_enter)) * marks)
    low_up = low(low_back(matmul(rows, u_enter)) * marks)
    gate = low_back(matmul(rows, w_gate) + SCALE * matmul(low_gate, g_leave))
    up = low_back(matmul(rows, w_up) + SCALE * matmul(low_up, u_leave))
    hidden = low(jax.nn.silu(gate) * up)
    low_down = low(low_back(matmul(hidden, d_enter)) * marks)
    return low(low_back(matmul(hidden, w_down) + SCALE * matmul(low_down, d_leave)))

def slot_layer(inputs, lengths, sets, route, frozen, adapters):
    attention_gain, query_gain, key_gain, feed_gain, qkv_weight, out_weight, router_weight, gate_weight, up_weight, down_weight = frozen
    qkv_enter, qkv_leave, out_enter, out_leave, router_enter, router_leave, gate_enter, gate_leave, up_enter, up_leave, down_enter, down_leave = adapters
    count = inputs.shape[0]
    doc_index, position, selector = documents(lengths, sets, count)
    cosine, sine = angles(position)
    normed_one = low(inputs * rms_scale(inputs) * attention_gain)
    low_in = low(low_back(jnp.einsum('td,kdc->ktc', normed_one, qkv_enter, precision=HIGH)) * selector[None])
    projected = low_back(jnp.einsum('td,kde->kte', normed_one, qkv_weight, precision=HIGH) + SCALE * jnp.einsum('ktc,kce->kte', low_in, qkv_leave, precision=HIGH))
    shape = (count, HEADS, HEAD_DIM)
    query_norm = (projected[0] * rms_scale(projected[0]) * query_gain).reshape(shape)
    key_norm = (projected[1] * rms_scale(projected[1]) * key_gain).reshape(shape)
    queries = low(rotate(query_norm, cosine, sine))
    keys = low(rotate(key_norm, cosine, sine))
    values = low(projected[2].reshape(shape))
    attended = low(low_back(attention(queries, keys, values, doc_index)))
    low_out = low(low_back(matmul(attended, out_enter)) * selector)
    hidden_state = inputs + low_back(matmul(attended, out_weight) + SCALE * matmul(low_out, out_leave))
    normed_two = low(hidden_state * rms_scale(hidden_state) * feed_gain)
    low_router = low(low_back(matmul(normed_two, router_enter)) * selector)
    logits = low_back(matmul(normed_two, router_weight) + SCALE * matmul(low_router, router_leave))
    probs = jax.nn.softmax(logits, axis=-1)
    route_hot = (route[:, :, None] == jnp.arange(EXPERTS, dtype=jnp.int32)[None, None, :]).astype(jnp.float32)
    weight = lax.optimization_barrier(jnp.sum(route_hot * probs[:, None, :], axis=-1))
    place = route_places(route)
    total = EXPERTS * N_EP * CAP
    route_ids = jnp.arange(count * TOP, dtype=jnp.int32)
    owner = jnp.zeros((total,), jnp.int32).at[place].set(route_ids // TOP)
    filled = jnp.zeros((total,), jnp.float32).at[place].set(1.0)
    rows_in = low_back(normed_two[owner] * filled[:, None]).reshape(EXPERTS, N_EP * CAP, -1)
    marks = (selector[owner] * filled[:, None]).reshape(EXPERTS, N_EP * CAP, -1)
    expert_out = lax.map(jax.checkpoint(one_expert), (rows_in, marks, gate_enter, gate_leave, up_enter, up_leave, down_enter, down_leave, gate_weight, up_weight, down_weight))
    route_out = expert_out.reshape(total, -1)[place].reshape(count, TOP, -1)
    return hidden_state + lax.optimization_barrier(jnp.sum(route_out * weight[:, :, None], axis=1))

def reference(tokens, cotangent, pack_order, doc_lengths, doc_sets, routes, attention_gain, query_gain, key_gain, feed_gain, qkv_weight, out_weight, router_weight, gate_weight, up_weight, down_weight, qkv_enter, qkv_leave, out_enter, out_leave, router_enter, router_leave, gate_enter, gate_leave, up_enter, up_leave, down_enter, down_leave):
    frozen = tuple((item.astype(jnp.float32) for item in (attention_gain, query_gain, key_gain, feed_gain, qkv_weight, out_weight, router_weight, gate_weight, up_weight, down_weight)))
    adapters = tuple((item.astype(jnp.float32) for item in (qkv_enter, qkv_leave, out_enter, out_leave, router_enter, router_leave, gate_enter, gate_leave, up_enter, up_leave, down_enter, down_leave)))
    group = TOK_DEV * N_EP
    slot_routes = routes.reshape(N_GRP, group, TOP)

    def forward(inputs, weights):
        stacked = inputs.reshape(N_GRP, group, -1)[pack_order]

        def per_slot(operands):
            rows, lengths, sets, route = operands
            return slot_layer(rows, lengths, sets, route, frozen, weights)
        results = lax.map(jax.checkpoint(per_slot), (stacked, doc_lengths, doc_sets, slot_routes))
        placed = jnp.zeros_like(results).at[pack_order].set(results)
        return placed.reshape(N_GRP * group, -1)
    result, pull = jax.vjp(forward, tokens.astype(jnp.float32), adapters)
    grad_tokens, grads = pull(cotangent.astype(jnp.float32))
    return (result.astype(jnp.bfloat16), grad_tokens.astype(jnp.bfloat16), grads[0], grads[1], grads[2], grads[3], grads[4], grads[5], grads[6], grads[7], grads[8], grads[9], grads[10], grads[11])
```

```python
import functools

import jax
import jax.numpy as jnp
from jax import lax
from jax.experimental import pallas as pl
from jax.experimental.pallas import tpu as pltpu
from jax.sharding import PartitionSpec as P

HEAD_DIM = 128
EXPERTS = 16
TOP = 8
SETS = 8
RANK = 16
CAP = 144


EPS = 1e-05
SCALE = 2.0
THETA = 10000.0
NEG = -1e30


def rms_scale(value):
    return lax.rsqrt(jnp.mean(value * value, axis=-1, keepdims=True) + EPS)


def rotate(value, cosine, sine):
    half = value.shape[-1] // 2
    turned = jnp.concatenate([-value[..., half:], value[..., :half]], axis=-1)
    return value * cosine + turned * sine


def rotate_back(grad, cosine, sine):
    half = grad.shape[-1] // 2
    moved = grad * sine
    turned = jnp.concatenate([moved[..., half:], -moved[..., :half]], axis=-1)
    return grad * cosine + turned


def angles(position):
    half = HEAD_DIM // 2
    freq = THETA ** (-(jnp.arange(half, dtype=jnp.float32) * 2.0) / HEAD_DIM)
    phase = position.astype(jnp.float32)[:, None] * freq[None, :]
    cosine = jnp.concatenate([jnp.cos(phase), jnp.cos(phase)], axis=-1)
    sine = jnp.concatenate([jnp.sin(phase), jnp.sin(phase)], axis=-1)
    return (cosine[:, None, :], sine[:, None, :])


LINE = 4
VMEM = 62 * 1024 * 1024


def swap(value, axis, bit):
    count = lax.axis_size(axis)
    return lax.ppermute(value, axis, [(i, i ^ bit) for i in range(count)])


def gather_parts(value, axis):
    parts, bit = ({0: value}, lax.axis_size(axis) // 2)
    while bit >= 1:
        for j in list(parts):
            parts[j ^ bit] = swap(parts[j], axis, bit)
        bit //= 2
    return [parts[j] for j in range(len(parts))]


def scatter_parts(parts, axis):
    parts, bit, count = (dict(enumerate(parts)), 1, lax.axis_size(axis))
    while bit < count:
        kept = {}
        for j in parts:
            if not j & bit:
                got = swap(parts[j ^ bit], axis, bit)
                kept[j] = parts[j].astype(jnp.float32) + got.astype(jnp.float32)
        bit *= 2
        if bit < count:
            kept = {j: part.astype(jnp.bfloat16) for j, part in kept.items()}
        parts = kept
    return parts[0]


def sum_relative(value, axis, local):
    count, bit = (lax.axis_size(axis), 1)
    while bit < count:
        got = swap(value, axis, bit)
        got = [got[..., (j ^ bit) * local : ((j ^ bit) + 1) * local] for j in range(count)]
        value = value + jnp.concatenate(got, axis=-1)
        bit *= 2
    return value


def line_scatter(parts, axis, length, stride):
    count = lax.axis_size(axis)
    place = lambda i: i // stride % length
    at = place(lax.axis_index(axis))
    up = [(i, i + stride) for i in range(count) if place(i) + 1 < length]
    down = [(i + stride, i) for i in range(count) if place(i) + 1 < length]
    total = [part.astype(jnp.float32) for part in parts]
    if length == 2:
        return total[0] + lax.ppermute(parts[1], axis, up + down).astype(jnp.float32)
    for step in range(1, length):
        from_below = lax.ppermute(total[length - step].astype(jnp.bfloat16), axis, up)
        from_above = lax.ppermute(total[step].astype(jnp.bfloat16), axis, down)
        low, high = (length - step - 1, (step + 1) % length)
        good = (at >= 1) & (at + length - step - 1 < length)
        total[low] = total[low] + jnp.where(good, from_below.astype(jnp.float32), 0.0)
        good = (at + 1 < length) & (at - (length - step - 1) >= 0)
        total[high] = total[high] + jnp.where(good, from_above.astype(jnp.float32), 0.0)
    return total[0]


def by_place(chunks):
    inner = chunks.shape[0] // LINE
    index = lax.axis_index("grp")
    parts = []
    for q in range(inner):
        group = []
        for p in range(LINE):
            chunk = (index // inner + p) % LINE * inner + (index % inner + q) % inner
            group.append(lax.dynamic_index_in_dim(chunks, chunk, 0, keepdims=False))
        parts.append(jnp.stack(group))
    return parts


def sum_packs(parts):
    inner = len(parts)
    mine = line_scatter(parts, "grp", inner, 1).astype(jnp.bfloat16) if inner > 1 else parts[0]
    return line_scatter([mine[p] for p in range(LINE)], "grp", LINE, inner)


def dot_nn(a, b):
    return jnp.dot(a, b, preferred_element_type=jnp.float32)


def dot_nt(a, b):
    return lax.dot_general(a, b, (((1,), (1,)), ((), ())), preferred_element_type=jnp.float32)


def dot_tn(a, b):
    return lax.dot_general(a, b, (((0,), (0,)), ((), ())), preferred_element_type=jnp.float32)


def expert_kernel(
    line,
    rank_ref,
    weight_ref,
    normed_ref,
    upstream_ref,
    mark_ref,
    gate_w,
    up_w,
    down_w,
    gate_enter,
    gate_leave,
    up_enter,
    up_leave,
    down_enter,
    down_leave,
    place_ref,
    mixed_ref,
    grad_ref,
    score_ref,
    *rest,
):
    inner = len(rest) - 9
    sums, (rows_in, grads_in, hidden, grad_gate, grad_up, marks, out_tile, back_tile, done) = (rest[:inner], rest[inner:])
    f32, bf16 = (jnp.float32, jnp.bfloat16)
    blocks, local, width = (rank_ref.shape[1], rank_ref.shape[3], normed_ref.shape[1])
    cap = mixed_ref.shape[2]
    expert, turn = (pl.program_id(0), pl.program_id(1))
    count = blocks * cap
    ff = hidden.shape[1]
    slots = lax.broadcasted_iota(jnp.int32, (cap, local), 0).astype(f32)
    weights = []
    for b in range(blocks):
        hit = rank_ref[0, b] == slots
        pick = hit.astype(bf16)
        weights.append(jnp.sum(jnp.where(hit, weight_ref[0, b], 0.0), axis=1, keepdims=True))
        here, there = (slice(b * cap, (b + 1) * cap), slice(b * local, (b + 1) * local))
        rows_in[here, :] = dot_nn(pick, normed_ref[there, :]).astype(bf16)
        grads_in[here, :] = dot_nn(pick, upstream_ref[there, :]).astype(bf16)
        marks[here, :] = dot_nn(pick, mark_ref[there, :])
    weight = jnp.concatenate(weights, axis=0)
    mark = marks[...]
    rank = mark.shape[1]
    low = dot_nn(rows_in[...], jnp.concatenate([gate_enter[0], up_enter[0]], axis=1))
    low_gate = (low[:, :rank] * mark).astype(bf16) * SCALE
    low_up = (low[:, rank:] * mark).astype(bf16) * SCALE
    grad_low_down = (dot_nt(grads_in[...], down_leave[0]) * (SCALE * weight) * mark).astype(bf16)
    step = min(256, ff)
    for at in range(0, ff, step):
        cut = slice(at, at + step)
        gate = dot_nn(rows_in[...], gate_w[0, :, cut]) + dot_nn(low_gate, gate_leave[0, :, cut])
        up = dot_nn(rows_in[...], up_w[0, :, cut]) + dot_nn(low_up, up_leave[0, :, cut])
        back = dot_nt(grads_in[...], down_w[0, cut, :]) * weight + dot_nt(grad_low_down, down_enter[0, cut, :])
        sigma = 1.0 / (1.0 + jnp.exp(-gate))
        silu = gate * sigma
        hidden[:, cut] = (silu * up).astype(bf16)
        grad_gate[:, cut] = (back * up * sigma * (1.0 + gate * (1.0 - sigma))).astype(bf16)
        grad_up[:, cut] = (back * silu).astype(bf16)
    low_down = (dot_nn(hidden[...], down_enter[0]) * mark).astype(bf16) * SCALE
    grad_low_gate = (dot_nt(grad_gate[...], gate_leave[0]) * SCALE * mark).astype(bf16)
    grad_low_up = (dot_nt(grad_up[...], up_leave[0]) * SCALE * mark).astype(bf16)
    grad_low = jnp.concatenate([grad_low_gate, grad_low_up], axis=1)
    step = out_tile.shape[3]
    sent = []

    def send(slot, cut):
        there = pl.ds(turn * blocks, blocks)
        copies = [
            pltpu.make_async_copy(out_tile.at[slot], mixed_ref.at[there, expert, :, cut], done.at[0, slot]),
            pltpu.make_async_copy(back_tile.at[slot], grad_ref.at[there, expert, :, cut], done.at[1, slot]),
        ]
        for copy in copies:
            copy.start()
        sent.append(copies)

    score = jnp.zeros((count, 1), f32)
    for at in range(0, width, step):
        cut = slice(at, at + step)
        out = dot_nn(hidden[...], down_w[0, :, cut]) + dot_nn(low_down, down_leave[0, :, cut])
        score = score + jnp.sum(out * grads_in[:, cut].astype(f32), axis=1, keepdims=True)
        back = dot_nt(grad_gate[...], gate_w[0, cut, :]) + dot_nt(grad_up[...], up_w[0, cut, :])
        back = back + dot_nt(grad_low, jnp.concatenate([gate_enter[0, cut, :], up_enter[0, cut, :]], axis=1))
        out = (out * weight).astype(bf16)
        back = back.astype(bf16)
        slot = len(sent) % 2
        if len(sent) >= 2:
            for copy in sent[-2]:
                copy.wait()
        for b in range(blocks):
            out_tile[slot, b] = out[b * cap : (b + 1) * cap]
            back_tile[slot, b] = back[b * cap : (b + 1) * cap]
        send(slot, pl.ds(at, step))
    for b in range(blocks):
        hit = rank_ref[0, b] == slots
        score_ref[0, b] = jnp.sum(jnp.where(hit, score[b * cap : (b + 1) * cap], 0.0), axis=0, keepdims=True)

    def keep(value, row, ref_at):
        piece = value.shape[1] // (line * inner)
        value = value.astype(bf16)
        for c in range(line * inner):
            part = value[:, c * piece : (c + 1) * piece]
            for q in range(inner):
                target = sums[q] if ref_at is None else sums[q]
                target = target.at[place_ref[0, c], 0, slice(row, row + value.shape[0]), slice(ref_at, ref_at + piece)]

                @pl.when((place_ref[1, c] == q) & (turn == 0))
                def _():
                    target[...] = part

                @pl.when((place_ref[1, c] == q) & (turn != 0))
                def _():
                    target[...] = (target[...].astype(f32) + part.astype(f32)).astype(bf16)

    wide = width // (line * inner)
    keep(dot_tn(grad_low, rows_in[...]), 0, 0)
    keep(dot_tn((low_down.astype(f32) * weight).astype(bf16), grads_in[...]), 2 * rank, 0)
    keep(dot_tn(low_gate, grad_gate[...]), 0, wide)
    keep(dot_tn(low_up, grad_up[...]), rank, wide)
    keep(dot_tn(grad_low_down, hidden[...]), 2 * rank, wide)
    for copies in sent[-2:]:
        for copy in copies:
            copy.wait()


def run_experts(rank, weight, normed, upstream, marks, place, inner, *params):
    experts, members, _, local = rank.shape
    group_len, width = normed.shape
    ff = params[0].shape[2]
    low = marks.shape[1]
    blocks = min(members, 4)
    turns = members // blocks
    packs = place.shape[1]
    line = packs // inner
    tokens = blocks * local
    bf16 = jnp.bfloat16
    by_turn = lambda e, r: (e, r, 0, 0)
    once = lambda shape: pl.BlockSpec(shape, lambda e, r: (r, 0), pipeline_mode=pl.Buffered(1))
    per_expert = lambda value: pl.BlockSpec((1,) + value.shape[1:], lambda e, r: (e, 0, 0))
    sums = jax.ShapeDtypeStruct((line, experts, 3 * low, (width + ff) // packs), bf16)
    rows_out = jax.ShapeDtypeStruct((members, experts, CAP, width), bf16)
    count = blocks * CAP
    tile = min(512, width)
    return pl.pallas_call(
        functools.partial(expert_kernel, line),
        grid=(experts, turns),
        out_shape=(rows_out, rows_out, jax.ShapeDtypeStruct(rank.shape, jnp.float32)) + (sums,) * inner,
        in_specs=[
            pl.BlockSpec((1, blocks, 1, local), by_turn),
            pl.BlockSpec((1, blocks, 1, local), by_turn),
            once((tokens, width)),
            once((tokens, width)),
            once((tokens, low)),
        ]
        + [per_expert(value) for value in params]
        + [pl.BlockSpec(memory_space=pltpu.SMEM)],
        out_specs=(
            pl.BlockSpec(memory_space=pl.ANY),
            pl.BlockSpec(memory_space=pl.ANY),
            pl.BlockSpec((1, blocks, 1, local), by_turn),
        )
        + (pl.BlockSpec((line, 1) + sums.shape[2:], lambda e, r: (0, e, 0, 0)),) * inner,
        scratch_shapes=[
            pltpu.VMEM((count, width), bf16),
            pltpu.VMEM((count, width), bf16),
            pltpu.VMEM((count, ff), bf16),
            pltpu.VMEM((count, ff), bf16),
            pltpu.VMEM((count, ff), bf16),
            pltpu.VMEM((count, low), jnp.float32),
            pltpu.VMEM((2, blocks, CAP, tile), bf16),
            pltpu.VMEM((2, blocks, CAP, tile), bf16),
            pltpu.SemaphoreType.DMA((2, 2)),
        ],
        compiler_params=pltpu.CompilerParams(vmem_limit_bytes=VMEM),
        cost_estimate=pl.CostEstimate(
            flops=2 * experts * members * CAP * (width * ff * 6 + 9 * low * (width + ff)),
            bytes_accessed=60_000_000,
            transcendentals=experts * members * CAP * ff,
        ),
        name="experts",
    )(rank, weight, normed, upstream, marks, *params, place)


def combine_kernel(rank_ref, rows_ref, out_ref):
    experts, cap, local = (rows_ref.shape[1], rows_ref.shape[2], rank_ref.shape[3])
    slots = lax.broadcasted_iota(jnp.int32, (cap, local), 0).astype(jnp.float32)
    pick = jnp.concatenate([(rank_ref[e, 0] == slots).astype(jnp.bfloat16) for e in range(experts)], axis=0)
    rows = jnp.concatenate([rows_ref[0, e] for e in range(experts)], axis=0)
    out_ref[0] = dot_tn(pick, rows).astype(out_ref.dtype)


def combine(rank, rows, name):
    experts, members, _, local = rank.shape
    width = rows.shape[3]
    half = width // 2
    return pl.pallas_call(
        combine_kernel,
        grid=(members, 2),
        out_shape=jax.ShapeDtypeStruct((members, local, width), jnp.bfloat16),
        in_specs=[
            pl.BlockSpec((experts, 1, 1, local), lambda b, n: (0, b, 0, 0)),
            pl.BlockSpec((1, experts, CAP, half), lambda b, n: (b, 0, 0, n)),
        ],
        out_specs=pl.BlockSpec((1, local, half), lambda b, n: (b, 0, n)),
        compiler_params=pltpu.CompilerParams(vmem_limit_bytes=VMEM),
        cost_estimate=pl.CostEstimate(
            flops=2 * members * local * experts * CAP * width, bytes_accessed=2 * rows.size, transcendentals=0
        ),
        name=name,
    )(rank, rows)


def rows_of(chunks):
    return chunks.reshape(chunks.shape[0], -1, 128)

def per_device(
    tokens,
    cotangent,
    pack_order,
    doc_lengths,
    doc_sets,
    routes,
    attention_gain,
    query_gain,
    key_gain,
    feed_gain,
    qkv_weight,
    out_weight,
    router_weight,
    gate_weight,
    up_weight,
    down_weight,
    qkv_enter,
    qkv_leave,
    out_enter,
    out_leave,
    router_enter,
    router_leave,
    gate_enter,
    gate_leave,
    up_enter,
    up_leave,
    down_enter,
    down_leave,
):
    members = lax.axis_size("ep")
    packs = lax.axis_size("grp")
    pack = lax.axis_index("grp")
    member = lax.axis_index("ep")
    local, width = tokens.shape
    group_len = local * members
    slice_width = width // members
    heads_here = slice_width // HEAD_DIM
    experts_here = gate_weight.shape[0]
    own_cols = member * slice_width
    f32, bf16 = (jnp.float32, jnp.bfloat16)
    slot = jnp.sum(jnp.where(pack_order == pack, jnp.arange(packs, dtype=jnp.int32), 0))
    named = jnp.sum(jnp.left_shift(jnp.int32(1), routes), axis=1)
    documents_here = jnp.concatenate([doc_lengths[0], doc_sets[0]])
    info = jnp.concatenate([named, jnp.pad(documents_here, (0, 128 - documents_here.shape[0]))])
    info = jnp.stack(gather_parts(info, "grp"))
    info = lax.dynamic_index_in_dim(info, slot ^ pack, 0, keepdims=False)
    blocks = [member ^ j for j in range(members)]
    info = jnp.stack(gather_parts(info, "ep"))
    named_all = info[:, :local]
    docs = doc_lengths.shape[1]
    lengths, sets = (info[0, local : local + docs], info[0, local + docs : local + 2 * docs])
    block_ids = jnp.stack(blocks)
    rows = (block_ids[:, None] * local + jnp.arange(local, dtype=jnp.int32)[None, :]).reshape(-1)
    ends = jnp.cumsum(lengths)
    doc_index = jnp.sum((rows[:, None] >= ends[None, :]).astype(jnp.int32), axis=1)
    member_of = doc_index[:, None] == jnp.arange(docs, dtype=jnp.int32)[None, :]
    position = rows - jnp.sum(jnp.where(member_of, (ends - lengths)[None, :], 0), axis=1)
    chosen = jnp.sum(jnp.where(member_of, sets[None, :], 0), axis=1)
    columns = jnp.arange(SETS * RANK, dtype=jnp.int32) // RANK
    selector = (columns[None, :] == chosen[:, None]).astype(f32)
    own_selector = selector[:local]
    cosine, sine = angles(position)

    token_parts = gather_parts(tokens, "ep")
    upstream_parts = gather_parts(cotangent, "ep")
    gain_one = attention_gain.astype(f32)
    resid = tokens.astype(f32)
    scale_one = rms_scale(resid)
    normed_all = jnp.concatenate(
        [(part.astype(f32) * rms_scale(part.astype(f32)) * gain_one).astype(bf16) for part in token_parts]
    )
    low_all = jnp.einsum("td,kdc->ktc", normed_all, qkv_enter, preferred_element_type=f32)
    low_all = (low_all * selector[None]).astype(bf16)
    projected = jnp.einsum("td,kde->kte", normed_all, qkv_weight, preferred_element_type=f32)
    projected = projected + SCALE * jnp.einsum("ktc,kce->kte", low_all, qkv_leave, preferred_element_type=f32)
    squares = sum_relative(jnp.sum(projected[:2] * projected[:2], axis=-1), "ep", local)
    inverse = lax.rsqrt(squares / width + EPS)[:, :, None]
    gain_query = lax.dynamic_slice_in_dim(query_gain, own_cols, slice_width, 0).astype(f32)
    gain_key = lax.dynamic_slice_in_dim(key_gain, own_cols, slice_width, 0).astype(f32)
    shape = (group_len, heads_here, HEAD_DIM)
    query_norm = (projected[0] * inverse[0] * gain_query).reshape(shape)
    key_norm = (projected[1] * inverse[1] * gain_key).reshape(shape)
    queries = rotate(query_norm, cosine, sine).astype(bf16)
    keys = rotate(key_norm, cosine, sine).astype(bf16)
    values = projected[2].reshape(shape).astype(bf16)
    scale_attn = HEAD_DIM ** (-0.5)
    allowed = (doc_index[:, None] == doc_index[None, :]) & (rows[None, :] <= rows[:, None])
    scores = jnp.einsum("qhd,khd->hqk", queries, keys, preferred_element_type=f32) * scale_attn
    probs = jax.nn.softmax(jnp.where(allowed[None], scores, NEG), axis=-1)
    rounded_probs = probs.astype(bf16)
    attended = jnp.einsum("hqk,khd->qhd", rounded_probs, values, preferred_element_type=f32)
    attended = attended.reshape(group_len, slice_width).astype(bf16)
    out_part = jnp.dot(attended, out_weight, preferred_element_type=f32).astype(bf16)
    low_part = jnp.dot(attended, out_enter, preferred_element_type=f32).astype(bf16)
    cut = lambda value: [value[j * local : (j + 1) * local] for j in range(members)]
    out_sum = scatter_parts(cut(out_part), "ep")
    low_sum = scatter_parts(cut(low_part), "ep")
    low_out = (low_sum * own_selector).astype(bf16)
    hidden_state = resid + out_sum + SCALE * jnp.dot(low_out, out_leave, preferred_element_type=f32)
    scale_two = rms_scale(hidden_state)
    gain_two = feed_gain.astype(f32)
    normed_two = (hidden_state * scale_two * gain_two).astype(bf16)

    normed_two_parts = gather_parts(normed_two, "ep")
    normed_two_all = jnp.concatenate(normed_two_parts)
    upstream_all = jnp.concatenate(upstream_parts)
    low_router = jnp.dot(normed_two_all, router_enter, preferred_element_type=f32)
    low_router = (low_router * selector).astype(bf16)
    logits = jnp.dot(normed_two_all, router_weight, preferred_element_type=f32)
    logits = logits + SCALE * jnp.dot(low_router, router_leave, preferred_element_type=f32)
    probs_router = jax.nn.softmax(logits, axis=-1)
    expert_ids = jnp.arange(EXPERTS, dtype=jnp.int32)[None, :, None]
    hot = (jnp.right_shift(named_all[:, None, :], expert_ids) & 1).astype(f32)
    before = jnp.triu(jnp.ones((local, local), bf16), 1)
    rank = jnp.where(hot > 0, dot_nn(hot.astype(bf16), before), -1.0)
    first = member * experts_here
    of_here = lambda value: lax.dynamic_slice_in_dim(value, first, experts_here, 1).transpose(1, 0, 2)[:, :, None, :]
    rank_here = of_here(rank)
    weight_here = of_here(probs_router.reshape(members, local, EXPERTS).transpose(0, 2, 1))
    inner = packs // LINE
    chunk_ids = jnp.arange(packs, dtype=jnp.int32)
    place = jnp.stack([(chunk_ids // inner - pack // inner) % LINE, (chunk_ids % inner - pack % inner) % inner])
    mixed_rows, grad_rows, row_scores, *expert_sums = run_experts(
        rank_here,
        weight_here,
        normed_two_all,
        upstream_all,
        selector.astype(bf16),
        place,
        inner,
        gate_weight,
        up_weight,
        down_weight,
        gate_enter,
        gate_leave,
        up_enter,
        up_leave,
        down_enter,
        down_leave,
    )
    grad_mixed = combine(rank_here, grad_rows, "combine_grad")
    mixed_out = combine(rank_here, mixed_rows, "combine_out")
    expert_sum = sum_packs(expert_sums)
    wide = width // packs

    mixed_sum = scatter_parts([mixed_out[j] for j in range(members)], "ep")
    layer_out = (hidden_state + mixed_sum).astype(bf16)

    dot = lambda spec, a, b: jnp.einsum(spec, a, b, preferred_element_type=f32)
    grad_probs_all = jnp.zeros((EXPERTS, group_len), f32)
    grad_probs_here = row_scores.reshape(experts_here, group_len)
    grad_probs_all = lax.dynamic_update_slice_in_dim(grad_probs_all, grad_probs_here, first, 0)
    grad_probs_all = sum_relative(grad_probs_all, "ep", local).T
    grad_logits = probs_router * (grad_probs_all - jnp.sum(probs_router * grad_probs_all, axis=-1, keepdims=True))
    grad_logits = grad_logits.astype(bf16)
    grad_low_router = (dot("te,ce->tc", grad_logits, router_leave) * SCALE * selector).astype(bf16)
    slice_of = lambda value: lax.dynamic_slice_in_dim(value, own_cols, slice_width, 1)
    grad_router_enter = dot("tc,td->cd", grad_low_router, slice_of(normed_two_all))
    grad_router_leave = SCALE * dot("tc,te->ce", low_router, grad_logits)
    grad_normed_two = scatter_parts([grad_mixed[j] for j in range(members)], "ep")
    grad_normed_two = grad_normed_two + dot("te,de->td", grad_logits[:local], router_weight)
    grad_normed_two = grad_normed_two + dot("tc,dc->td", grad_low_router[:local], router_enter)
    grad_out = cotangent.astype(f32)
    weighted_two = gain_two * grad_normed_two
    grad_hidden_state = (
        grad_out
        + scale_two * weighted_two
        - hidden_state * scale_two**3 * jnp.mean(hidden_state * weighted_two, axis=-1, keepdims=True)
    )
    grad_branch = grad_hidden_state.astype(bf16)
    branch_all = jnp.concatenate(gather_parts(grad_branch, "ep"))
    low_out_all = jnp.concatenate(gather_parts(low_out, "ep"))
    low_grad_all = (dot("td,cd->tc", branch_all, out_leave) * SCALE * selector).astype(bf16)
    grad_att = dot("td,ed->te", branch_all, out_weight) + dot("tc,ec->te", low_grad_all, out_enter)
    grad_att = grad_att.astype(bf16).reshape(shape)
    grad_out_enter = dot("tc,te->ce", low_grad_all, attended)
    grad_out_leave = SCALE * dot("tc,td->cd", low_out_all, slice_of(branch_all))

    grad_probs_att = dot("qhd,khd->hqk", grad_att, values)
    inner = jnp.sum(probs * grad_probs_att, axis=-1, keepdims=True)
    grad_scores = (probs * (grad_probs_att - inner) * scale_attn).astype(bf16)
    grad_queries = dot("hqk,khd->qhd", grad_scores, keys)
    grad_keys = dot("hqk,qhd->khd", grad_scores, queries)
    grad_values = dot("hqk,qhd->khd", rounded_probs, grad_att)
    grad_query_norm = rotate_back(grad_queries, cosine, sine).reshape(group_len, slice_width)
    grad_key_norm = rotate_back(grad_keys, cosine, sine).reshape(group_len, slice_width)
    terms = jnp.stack(
        [
            jnp.sum(projected[0] * gain_query * grad_query_norm, axis=-1),
            jnp.sum(projected[1] * gain_key * grad_key_norm, axis=-1),
        ]
    )
    terms = sum_relative(terms, "ep", local)
    grad_query_proj = inverse[0] * gain_query * grad_query_norm - projected[0] * inverse[0] ** 3 * (terms[0] / width)[:, None]
    grad_key_proj = inverse[1] * gain_key * grad_key_norm - projected[1] * inverse[1] ** 3 * (terms[1] / width)[:, None]
    grad_proj = jnp.stack([grad_query_proj, grad_key_proj, grad_values.reshape(group_len, slice_width)]).astype(bf16)
    grad_qkv_leave = SCALE * dot("ktc,kte->kce", low_all, grad_proj)
    part_input = dot("kte,kde->td", grad_proj, qkv_weight).astype(bf16)
    part_low = (SCALE * dot("kte,kce->tkc", grad_proj, qkv_leave) * selector[:, None, :]).astype(bf16)
    part_low = part_low.reshape(group_len, -1)
    low_own = scatter_parts(cut(part_low), "ep").astype(bf16)
    low_grads = jnp.concatenate(gather_parts(low_own, "ep"))
    grad_qkv_enter = dot("tc,te->ce", low_grads, slice_of(normed_all)).reshape(3, -1, slice_width)
    input_part = scatter_parts(cut(part_input), "ep")
    grad_normed_one = input_part + dot("tkc,kdc->td", low_own.reshape(local, 3, -1), qkv_enter)
    weighted_one = gain_one * grad_normed_one
    grad_input = (
        grad_hidden_state
        + scale_one * weighted_one
        - resid * scale_one**3 * jnp.mean(resid * weighted_one, axis=-1, keepdims=True)
    )
    grad_input = grad_input.astype(bf16)

    by_rows = lambda value: rows_of(value.astype(bf16).reshape(value.shape[0], packs, -1).transpose(1, 0, 2).reshape(packs, -1))
    leave_rows = lax.dynamic_slice_in_dim(grad_router_leave, member * (SETS * RANK // members), SETS * RANK // members, 0)
    leave_chunks = leave_rows.reshape(leave_rows.shape[0], packs, -1).transpose(1, 0, 2).reshape(packs, -1)
    leave_size = leave_chunks.shape[1]
    leave_chunks = jnp.pad(leave_chunks, ((0, 0), (0, 128 - leave_size))).astype(bf16)
    rest = [grad_out_enter[None], grad_out_leave[None], grad_router_enter[None], grad_qkv_enter, grad_qkv_leave]
    pieces = [by_rows(value.reshape(value.shape[0], -1)) for value in rest]
    pieces.append(leave_chunks[:, None, :])
    summed = sum_packs(by_place(jnp.concatenate(pieces, axis=1)))
    outs, at = ([], 0)
    for value, piece in zip(rest, pieces):
        size = piece.shape[1]
        outs.append(summed[at : at + size].reshape(value.shape[0], -1, slice_width))
        at += size
    router_leave_out = summed[at, :leave_size].reshape(SETS * RANK // members, -1)
    low = SETS * RANK
    turn = lambda value: jnp.swapaxes(value, -1, -2)
    return (
        layer_out,
        grad_input,
        turn(outs[3]),
        outs[4],
        turn(outs[0][0]),
        outs[1][0],
        turn(outs[2][0]),
        router_leave_out,
        turn(expert_sum[:, :low, :wide]),
        expert_sum[:, :low, wide:],
        turn(expert_sum[:, low : 2 * low, :wide]),
        expert_sum[:, low : 2 * low, wide:],
        turn(expert_sum[:, 2 * low :, wide:]),
        expert_sum[:, 2 * low :, :wide],
    )


def solution(mesh):
    in_specs = (
        P(("grp", "ep"), None),
        P(("grp", "ep"), None),
        P(),
        P("grp", None),
        P("grp", None),
        P(("grp", "ep"), None),
        P(),
        P(),
        P(),
        P(),
        P(None, None, "ep"),
        P("ep", None),
        P(),
        P("ep", None, None),
        P("ep", None, None),
        P("ep", None, None),
        P(),
        P(None, None, "ep"),
        P("ep", None),
        P(),
        P(),
        P(),
        P("ep", None, None),
        P("ep", None, None),
        P("ep", None, None),
        P("ep", None, None),
        P("ep", None, None),
        P("ep", None, None),
    )
    out_specs = (
        P(("grp", "ep"), None),
        P(("grp", "ep"), None),
        P(None, "ep", "grp"),
        P(None, "grp", "ep"),
        P("ep", "grp"),
        P("grp", "ep"),
        P("ep", "grp"),
        P("ep", "grp"),
        P("ep", "grp", None),
        P("ep", None, "grp"),
        P("ep", "grp", None),
        P("ep", None, "grp"),
        P("ep", "grp", None),
        P("ep", None, "grp"),
    )
    return jax.shard_map(
        per_device, mesh=mesh, in_specs=in_specs, out_specs=out_specs, check_vma=False
    )
```

```python
import functools

import jax
import jax.numpy as jnp
from jax import lax
from jax.experimental import pallas as pl
from jax.experimental.pallas import tpu as pltpu
from jax.sharding import PartitionSpec as P

HEAD_DIM = 128
EXPERTS = 16
TOP = 8
SETS = 8
RANK = 16
CAP = 144


EPS = 1e-05
SCALE = 2.0
THETA = 10000.0
NEG = -1e30


def rms_scale(value):
    return lax.rsqrt(jnp.mean(value * value, axis=-1, keepdims=True) + EPS)


def angles(position):
    half = HEAD_DIM // 2
    freq = THETA ** (-(jnp.arange(half, dtype=jnp.float32) * 2.0) / HEAD_DIM)
    phase = position.astype(jnp.float32)[:, None] * freq[None, :]
    cosine, sine = (jnp.cos(phase), jnp.sin(phase))
    return (jnp.concatenate([cosine, cosine], axis=-1), jnp.concatenate([-sine, sine], axis=-1))


LINE = 4
VMEM = 62 * 1024 * 1024


def swap(value, axis, bit):
    count = lax.axis_size(axis)
    return lax.ppermute(value, axis, [(i, i ^ bit) for i in range(count)])


def gather_parts(value, axis, bit=None):
    parts, bit = ({0: value}, (bit or lax.axis_size(axis)) // 2)
    while bit >= 1:
        for j in list(parts):
            parts[j ^ bit] = swap(parts[j], axis, bit)
        bit //= 2
    return [parts[j] for j in range(len(parts))]


def gather_near(value, axis):
    return gather_parts(value, axis, lax.axis_size(axis) // 2)


def gather_far(value, axis, *deps):
    far = swap(value, axis, lax.axis_size(axis) // 2)
    return gather_near(fence(far, *deps) if deps else far, axis)


def scatter_even(parts, axis):
    parts, bit = ({2 * i: part for i, part in enumerate(parts)}, 2)
    while bit < lax.axis_size(axis) // 2:
        got = {j: swap(parts[j ^ bit], axis, bit) for j in parts if not j & bit}
        parts = {j: (parts[j].astype(jnp.float32) + got[j].astype(jnp.float32)).astype(jnp.bfloat16) for j in got}
        bit *= 2
    return parts[0]


def reduce_scatter(make, axis, *deps):
    members = lax.axis_size(axis)
    top = members // 2
    odd = {}
    for j in range(members - 1, 0, -2):
        part, mark = make(j, None, *deps)
        odd[j - 1], deps = (swap(part, axis, 1), (mark,))
    sums = {}
    for j in range(members - 2, top - 1, -2):
        sums[j], mark = make(j, odd[j], *deps)
        deps = (mark,)
    far = scatter_even([sums[j] for j in range(top, members, 2)], axis)
    deps = (far,)
    for j in range(top - 2, -1, -2):
        sums[j], mark = make(j, odd[j], *deps)
        deps = (mark,)
    return scatter_even([sums[j] for j in range(0, top, 2)], axis), swap(far, axis, top)


def fence_kernel(*refs):
    pass


def fence(value, *deps):
    return pl.pallas_call(
        fence_kernel,
        out_shape=jax.ShapeDtypeStruct(value.shape, value.dtype),
        in_specs=[pl.BlockSpec(memory_space=pl.ANY)] * (1 + len(deps)),
        out_specs=pl.BlockSpec(memory_space=pl.ANY),
        input_output_aliases={0: 0},
        name="fence",
    )(value, *deps)


def sum_relative(value, axis, local):
    count, bit = (lax.axis_size(axis), 1)
    while bit < count:
        got = swap(value, axis, bit)
        got = [got[..., (j ^ bit) * local : ((j ^ bit) + 1) * local] for j in range(count)]
        value = value + jnp.concatenate(got, axis=-1)
        bit *= 2
    return value


class LineSum:
    def __init__(self, parts, axis, length, stride):
        count = lax.axis_size(axis)
        place = lambda i: i // stride % length
        self.axis, self.length, self.at = (axis, length, place(lax.axis_index(axis)))
        self.up = [(i, i + stride) for i in range(count) if place(i) + 1 < length]
        self.down = [(i + stride, i) for i in range(count) if place(i) + 1 < length]
        self.total = [part.astype(jnp.float32) for part in parts]

    def ready(self, step):
        return [self.total[p].astype(jnp.bfloat16) for p in (self.length - step, step)]

    def send(self, step, ready=None):
        up, down = ready or self.ready(step)
        return lax.ppermute(up, self.axis, self.up), lax.ppermute(down, self.axis, self.down)

    def add(self, step, got):
        left = self.length - step - 1
        below, above = (value.astype(jnp.float32) for value in got)
        good = (self.at >= 1) & (self.at + left < self.length)
        self.total[left] = self.total[left] + jnp.where(good, below, 0.0)
        good = (self.at + 1 < self.length) & (self.at - left >= 0)
        high = (step + 1) % self.length
        self.total[high] = self.total[high] + jnp.where(good, above, 0.0)


def line_scatter(parts, axis, length, stride):
    line = LineSum(parts, axis, length, stride)
    for step in range(1, length):
        line.add(step, line.send(step))
    return line.total[0]


def direct_scatter(parts, axis, length, stride, *deps):
    count = lax.axis_size(axis)
    got = []
    for p in range(1, length):
        moves = [(i, i + ((i // stride % length + p) % length - i // stride % length) * stride) for i in range(count)]
        got.append(lax.ppermute(parts[p], axis, moves))
    total = (fence(parts[0], *deps) if deps else parts[0]).astype(jnp.float32)
    for value in got:
        total = total + value.astype(jnp.float32)
    return total


def by_place(chunks):
    inner = chunks.shape[0] // LINE
    index = lax.axis_index("grp")
    parts = []
    for q in range(inner):
        group = []
        for p in range(LINE):
            chunk = (index // inner + p) % LINE * inner + (index % inner + q) % inner
            group.append(lax.dynamic_index_in_dim(chunks, chunk, 0, keepdims=False))
        parts.append(jnp.stack(group))
    return parts


def sum_packs(parts, *deps):
    inner = len(parts)
    mine = direct_scatter(parts, "grp", inner, 1).astype(jnp.bfloat16) if inner > 1 else parts[0]
    return direct_scatter([mine[p] for p in range(LINE)], "grp", LINE, inner, *deps)


def widen_kernel(docs, line, sets_ref, kept_ref, got_ref, *refs):
    f32 = jnp.float32
    out_refs = refs[-line:]
    experts, rows = got_ref.shape[1:3]
    for p in range(line):
        out_refs[p][...] = kept_ref[p]
        for e in range(experts):
            for g in range(rows // (docs * RANK)):
                for d in range(docs):
                    there = pl.ds(pl.multiple_of(g * SETS * RANK + sets_ref[d] * RANK, RANK), RANK)
                    piece = got_ref[p, e, (g * docs + d) * RANK : (g * docs + d + 1) * RANK]
                    out_refs[p][e, there] = (out_refs[p][e, there].astype(f32) + piece.astype(f32)).astype(kept_ref.dtype)


def widen(docs, sets, kept, got, *deps):
    line = kept.shape[0]
    return pl.pallas_call(
        functools.partial(widen_kernel, docs, line),
        out_shape=(jax.ShapeDtypeStruct(kept.shape[1:], kept.dtype),) * line,
        in_specs=[full(SMEM), full(), full()] + [full(pl.ANY)] * len(deps),
        out_specs=(full(),) * line,
        compiler_params=params(),
        name="widen",
    )(sets, kept, got, *deps)


def sum_experts(docs, sets, parts, *deps):
    inner = len(parts)
    if inner == 2:
        return widen(docs, sets, parts[0], swap(parts[1], "grp", 1), *deps)
    mine = line_scatter(parts, "grp", inner, 1).astype(jnp.bfloat16) if inner > 1 else parts[0]
    return [mine[p] for p in range(LINE)]


def dot_nn(a, b):
    return jnp.dot(a, b, preferred_element_type=jnp.float32)


def dot_nt(a, b):
    return lax.dot_general(a, b, (((1,), (1,)), ((), ())), preferred_element_type=jnp.float32)


def dot_tn(a, b):
    return lax.dot_general(a, b, (((0,), (0,)), ((), ())), preferred_element_type=jnp.float32)


def column(row):
    return jnp.broadcast_to(row, (128, row.shape[1])).T


def as_row(value):
    return jnp.broadcast_to(value, (value.shape[0], 128)).T[:1]


def doc_sum(scal_ref, rows, docs, at):
    value = jnp.full(rows.shape, scal_ref[at], jnp.int32)
    for k in range(1, docs):
        value = jnp.where(rows >= scal_ref[k], scal_ref[at + k], value)
    return value


def block_marks(scal_ref, docs, block, local):
    rows = block * local + lax.broadcasted_iota(jnp.int32, (local, SETS * RANK), 0)
    lanes = lax.broadcasted_iota(jnp.int32, (local, SETS * RANK), 1) // RANK
    return (doc_sum(scal_ref, rows, docs, 1 + docs) == lanes).astype(jnp.float32)


def params(**kinds):
    return pltpu.CompilerParams(vmem_limit_bytes=VMEM, **kinds)


def cost(flops, moved, exps=0):
    return pl.CostEstimate(flops=int(flops) // 8, bytes_accessed=int(moved) // 8, transcendentals=int(exps) // 8)


def full(memory=pltpu.VMEM):
    return pl.BlockSpec(memory_space=memory)


SMEM = pltpu.SMEM


def project_kernel(docs, half, parts, scal_ref, *refs):
    f32, bf16 = (jnp.float32, jnp.bfloat16)
    x_refs, (gain_ref, w_ref, enter_ref, leave_ref) = (refs[:parts], refs[parts : parts + 4])
    normed_ref, low_ref, p_ref, v_ref, square_ref = refs[-5:]
    local = x_refs[0].shape[0]
    rank = SETS * RANK
    which = pl.program_id(0)

    @pl.when(which == 0)
    def _():
        enter = jnp.concatenate([enter_ref[i] for i in range(3)], axis=1)
        for b in range(parts):
            x = x_refs[b][...].astype(f32)
            here = slice(b * local, (b + 1) * local)
            normed_ref[here] = (x * rms_scale(x) * gain_ref[...].astype(f32)).astype(bf16)
            mark = block_marks(scal_ref, docs, scal_ref[0] ^ (half * parts + b), local)
            low = dot_nn(normed_ref[here], enter)
            for i in range(3):
                low_ref[i, here] = (low[:, i * rank : (i + 1) * rank] * mark).astype(bf16) * SCALE

    value = dot_nn(normed_ref[...], w_ref[0]) + dot_nn(low_ref[which], leave_ref[0])

    @pl.when(which < 2)
    def _():
        p_ref[0] = value
        square_ref[pl.ds(which, 1)] = as_row(jnp.sum(value * value, axis=1, keepdims=True))

    @pl.when(which == 2)
    def _():
        v_ref[...] = value.astype(bf16)


def project(docs, half, scal, x_parts, gain, weight, enter, leave, kept):
    parts = len(x_parts)
    local, width = x_parts[0].shape
    slice_width = weight.shape[2]
    rows, rank = (parts * local, enter.shape[2])
    f32, bf16 = (jnp.float32, jnp.bfloat16)
    outs = (
        jax.ShapeDtypeStruct((2 * rows, width), bf16),
        jax.ShapeDtypeStruct((3, 2 * rows, rank), bf16),
        jax.ShapeDtypeStruct((2, 2 * rows, slice_width), f32),
        jax.ShapeDtypeStruct((2 * rows, slice_width), bf16),
        jax.ShapeDtypeStruct((2, 2 * rows), f32),
    )
    extra = () if kept is None else kept
    first = 5 + parts
    return pl.pallas_call(
        functools.partial(project_kernel, docs, half, parts),
        grid=(3,),
        out_shape=outs,
        in_specs=[full(SMEM)]
        + [full()] * parts
        + [
            full(),
            pl.BlockSpec((1, width, slice_width), lambda i: (i, 0, 0)),
            full(),
            pl.BlockSpec((1, rank, slice_width), lambda i: (i, 0, 0)),
        ]
        + [full(pl.ANY)] * len(extra),
        out_specs=(
            pl.BlockSpec((rows, width), lambda i: (half, 0)),
            pl.BlockSpec((3, rows, rank), lambda i: (0, half, 0)),
            pl.BlockSpec((1, rows, slice_width), lambda i: (jnp.minimum(i, 1), half, 0)),
            pl.BlockSpec((rows, slice_width), lambda i: (half, 0)),
            pl.BlockSpec((2, rows), lambda i: (0, half)),
        ),
        input_output_aliases={first + i: i for i in range(len(extra))},
        compiler_params=params(),
        cost_estimate=cost(2 * rows * width * (3 * slice_width + 3 * rank), 14_000_000),
        name="project",
    )(scal, *x_parts, gain, weight, enter, leave, *extra)


def prepare_kernel(width, p_ref, square_ref, gains_ref, cos_ref, sin_ref, q_ref, k_ref):
    inverse = lax.rsqrt(square_ref[...] / width + EPS)
    for i, out_ref in ((0, q_ref), (1, k_ref)):
        scale = column(inverse[i : i + 1])
        for at in range(0, p_ref.shape[2], HEAD_DIM):
            cut = slice(at, at + HEAD_DIM)
            value = p_ref[i, :, cut] * scale * gains_ref[i : i + 1, cut]
            value = value * cos_ref[...] + pltpu.roll(value, HEAD_DIM // 2, 1) * sin_ref[...]
            out_ref[:, cut] = value.astype(jnp.bfloat16)


def prepare(width, p, squares, gains, cosine, sine, local, *deps):
    _, rows, slice_width = p.shape
    out = jax.ShapeDtypeStruct((rows, slice_width), jnp.bfloat16)
    return pl.pallas_call(
        lambda *refs: prepare_kernel(width, *refs[:5], *refs[5 + len(deps) :]),
        grid=(rows // local,),
        out_shape=(out, out),
        in_specs=[
            pl.BlockSpec((2, local, slice_width), lambda i: (0, i, 0)),
            pl.BlockSpec((2, local), lambda i: (0, i)),
            full(),
            pl.BlockSpec((local, HEAD_DIM), lambda i: (i, 0)),
            pl.BlockSpec((local, HEAD_DIM), lambda i: (i, 0)),
        ]
        + [full(pl.ANY)] * len(deps),
        out_specs=(pl.BlockSpec((local, slice_width), lambda i: (i, 0)),) * 2,
        compiler_params=params(),
        cost_estimate=cost(10 * p.size, 8 * p.size),
        name="prepare",
    )(p, squares, gains, cosine, sine, *deps)


def attend_kernel(docs, place, local, added, scal_ref, q_ref, k_ref, v_ref, w_ref, enter_ref, *refs):
    f32, bf16 = (jnp.float32, jnp.bfloat16)
    att_ref, part_ref, log_ref = refs[-3:]
    members = q_ref.shape[0] // local
    heads = q_ref.shape[1] // HEAD_DIM
    width = w_ref.shape[1]
    member = scal_ref[0]
    block = member ^ place
    queries = slice(place * local, (place + 1) * local)

    def run(last):
        rows = last * local + lax.broadcasted_iota(jnp.int32, (local, local), 0)
        begin = doc_sum(scal_ref, rows, docs, 1 + 2 * docs)
        lanes = lax.broadcasted_iota(jnp.int32, (local, local), 1)
        logs = jnp.zeros((8, local), f32)
        for h in range(heads):
            cut = slice(h * HEAD_DIM, (h + 1) * HEAD_DIM)
            query = q_ref[queries, cut]
            scores, values = ([], [])
            for b in range(last + 1):
                there = pl.ds(pl.multiple_of((member ^ b) * local, local), local)
                score = dot_nt(query, k_ref[there, cut]) * HEAD_DIM ** (-0.5)
                good = lanes + b * local >= begin
                if b == last:
                    good = good & (lanes + b * local <= rows)
                scores.append(jnp.where(good, score, NEG))
                values.append(v_ref[there, cut])
            peak = functools.reduce(jnp.maximum, [jnp.max(score, axis=1, keepdims=True) for score in scores])
            expo = [jnp.exp(score - peak) for score in scores]
            total = functools.reduce(jnp.add, [jnp.sum(e, axis=1, keepdims=True) for e in expo])
            share = 1.0 / total
            mixed = functools.reduce(jnp.add, [dot_nn((e * share).astype(bf16), v) for e, v in zip(expo, values)])
            att_ref[:, cut] = mixed.astype(bf16)
            head_row = lax.broadcasted_iota(jnp.int32, (8, local), 0) == h
            logs = jnp.where(head_row, as_row(peak + jnp.log(total)), logs)
        log_ref[...] = logs

    for last in range(members):
        pl.when(block == last)(functools.partial(run, last))
    for cut, value_ref in ((slice(0, width), w_ref), (slice(width, None), enter_ref)):
        value = dot_nn(att_ref[...], value_ref[...])
        if added:
            value = value + refs[0][:, cut].astype(f32)
        part_ref[:, cut] = value.astype(bf16)


def attend(docs, place, local, scal, q, k, v, weight, enter, addend, *deps):
    slice_width = q.shape[1]
    width, rank = (weight.shape[1], enter.shape[1])
    f32, bf16 = (jnp.float32, jnp.bfloat16)
    assert slice_width // HEAD_DIM <= 8
    return pl.pallas_call(
        functools.partial(attend_kernel, docs, place, local, addend is not None),
        out_shape=(
            jax.ShapeDtypeStruct((local, slice_width), bf16),
            jax.ShapeDtypeStruct((local, width + rank), bf16),
            jax.ShapeDtypeStruct((8, local), f32),
        ),
        in_specs=[full(SMEM)] + [full()] * (5 + (addend is not None)) + [full(pl.ANY)] * len(deps),
        out_specs=(full(),) * 3,
        compiler_params=params(),
        cost_estimate=cost(2_200_000_000, 4_000_000, 350_000),
        name="attend",
    )(scal, q, k, v, weight, enter, *(() if addend is None else (addend,)), *deps)


def middle_kernel(
    docs, scal_ref, x_ref, oa_ref, ob_ref, leave_ref, gain_ref, route_ref, route_enter, route_leave, h_ref, normed_ref, route_low, probs_ref
):
    f32, bf16 = (jnp.float32, jnp.bfloat16)
    width = x_ref.shape[1]
    mark = block_marks(scal_ref, docs, scal_ref[0], x_ref.shape[0])
    low = ((oa_ref[:, width:].astype(f32) + ob_ref[:, width:].astype(f32)) * mark).astype(bf16)
    normed_ref[:, width:] = low
    h = x_ref[...].astype(f32) + (oa_ref[:, :width].astype(f32) + ob_ref[:, :width].astype(f32))
    h = h + SCALE * dot_nn(low, leave_ref[...])
    h_ref[...] = h
    normed = (h * rms_scale(h) * gain_ref[...].astype(f32)).astype(bf16)
    normed_ref[:, :width] = normed
    low, probs = router(normed, mark, route_ref, route_enter, route_leave)
    route_low[...] = low
    probs_ref[...] = probs


def router(normed, mark, route_ref, route_enter, route_leave):
    low = (dot_nn(normed, route_enter[...]) * mark).astype(jnp.bfloat16)
    logits = dot_nt(route_ref[...], normed) + SCALE * dot_nt(route_leave[...], low)
    expo = jnp.exp(logits - jnp.max(logits, axis=0, keepdims=True))
    return low, expo / jnp.sum(expo, axis=0, keepdims=True)


def middle(docs, scal, x, outs, leave, gain, route, route_enter, route_leave):
    local, width = x.shape
    rank = leave.shape[0]
    f32, bf16 = (jnp.float32, jnp.bfloat16)
    return pl.pallas_call(
        functools.partial(middle_kernel, docs),
        out_shape=(
            jax.ShapeDtypeStruct((local, width), f32),
            jax.ShapeDtypeStruct((local, width + rank), bf16),
            jax.ShapeDtypeStruct((local, rank), bf16),
            jax.ShapeDtypeStruct((route.shape[0], local), f32),
        ),
        in_specs=[full(SMEM)] + [full()] * 8,
        out_specs=(full(),) * 4,
        compiler_params=params(),
        cost_estimate=cost(4 * local * width * rank, 8_000_000),
        name="middle",
    )(scal, x, *outs, leave, gain, route, route_enter, route_leave)


def middle_back_kernel(
    docs, scal_ref, ga_ref, gb_ref, probs_ref, h_ref, up_ref, route_low, gain_ref, route_ref, route_enter, route_leave, dh_ref, dhb_ref, leave_ref
):
    f32, bf16 = (jnp.float32, jnp.bfloat16)
    width = h_ref.shape[1]
    mark = block_marks(scal_ref, docs, scal_ref[0], h_ref.shape[0])
    probs = probs_ref[...]
    experts = probs.shape[0]
    scores = (ga_ref[:, width:].astype(f32) + gb_ref[:, width:].astype(f32)).T
    dprobs = scores[:experts] + scores[experts : 2 * experts]
    dlogits = (probs * (dprobs - jnp.sum(probs * dprobs, axis=0, keepdims=True))).astype(bf16)
    dlow = (dot_tn(dlogits, route_leave[...]) * SCALE * mark).astype(bf16)
    dhb_ref[:, width:] = dlow
    leave_ref[...] = SCALE * dot_nn(dlogits, route_low[...])
    back = ga_ref[:, :width].astype(f32) + gb_ref[:, :width].astype(f32)
    back = back + dot_tn(dlogits, route_ref[...]) + dot_nt(dlow, route_enter[...])
    back = back * gain_ref[...].astype(f32)
    h = h_ref[...]
    scale = rms_scale(h)
    dh = up_ref[...].astype(f32) + scale * back - h * scale**3 * jnp.mean(h * back, axis=-1, keepdims=True)
    dh_ref[...] = dh
    dhb_ref[:, :width] = dh.astype(bf16)


def middle_back(docs, scal, grads, probs, h, upstream, route_low, gain, route, route_enter, route_leave):
    local, width = h.shape
    rank = route_enter.shape[1]
    f32, bf16 = (jnp.float32, jnp.bfloat16)
    return pl.pallas_call(
        functools.partial(middle_back_kernel, docs),
        out_shape=(
            jax.ShapeDtypeStruct((local, width), f32),
            jax.ShapeDtypeStruct((local, width + rank), bf16),
            jax.ShapeDtypeStruct((route.shape[0], rank), f32),
        ),
        in_specs=[full(SMEM)] + [full()] * 10,
        out_specs=(full(),) * 3,
        compiler_params=params(),
        cost_estimate=cost(4 * local * width * rank, 10_000_000),
        name="middle_back",
    )(scal, *grads, probs, h, upstream, route_low, gain, route, route_enter, route_leave)


def attend_back_kernel(docs, half, local, scal_ref, *refs):
    f32, bf16 = (jnp.float32, jnp.bfloat16)
    q_ref = refs[0]
    members = q_ref.shape[0] // local
    count = members // 2
    heads = q_ref.shape[1] // HEAD_DIM
    q_ref, k_ref, v_ref, w_ref, enter_ref, leave_ref = refs[:6]
    refs = refs[6:]
    grad_refs, att_refs, log_refs, normed_refs, refs = (*(refs[i * count : (i + 1) * count] for i in range(4)), refs[4 * count :])
    before, refs = (refs[: 5 * half], refs[5 * half + half :])
    dq_ref, dk_ref, dv_ref, enter_grad, leave_grad, route_grad, *rest = refs
    term_refs, (grad, datt, att, logs, normed) = (rest[:-5], rest[-5:])
    width = w_ref.shape[1]
    step = pl.program_id(0)
    place = half * count + step
    member = scal_ref[0]
    block = member ^ place
    queries = pl.ds(pl.multiple_of(place * local, local), local)
    mine = pl.ds(pl.multiple_of(member * q_ref.shape[1], 128), q_ref.shape[1])

    @pl.when(step == 0)
    def _():
        for i, ref in enumerate((dk_ref, dv_ref, enter_grad, leave_grad, route_grad)):
            ref[...] = before[i][...] if half else jnp.zeros_like(ref)

    for i in range(count):

        @pl.when(step == i)
        def _():
            grad[...] = grad_refs[i][...]
            att[...] = att_refs[i][...]
            logs[...] = log_refs[i][...]
            normed[:, : mine.size] = normed_refs[i][:, mine]
            normed[:, mine.size :] = normed_refs[i][:, width:]

    mark = block_marks(scal_ref, docs, block, local)
    low = (dot_nt(grad[:, :width], leave_ref[...]) * SCALE * mark).astype(bf16)
    datt[...] = (dot_nt(grad[:, :width], w_ref[...]) + dot_nt(low, enter_ref[...])).astype(bf16)
    enter_grad[...] += dot_tn(low, att[...])
    leave_grad[...] += SCALE * dot_tn(normed[:, mine.size :], grad[:, mine])
    route_grad[...] += dot_tn(grad[:, width:], normed[:, : mine.size])

    def run(last):
        rows = last * local + lax.broadcasted_iota(jnp.int32, (local, local), 1)
        begin = doc_sum(scal_ref, rows, docs, 1 + 2 * docs)
        down = lax.broadcasted_iota(jnp.int32, (local, local), 0)
        term = jnp.zeros((local, 1), f32)
        for h in range(heads):
            cut = slice(h * HEAD_DIM, (h + 1) * HEAD_DIM)
            query, dout = (q_ref[queries, cut], datt[:, cut])
            log = logs[h : h + 1]
            shares, pushes = ([], [])
            for b in range(last + 1):
                there = pl.ds(pl.multiple_of((member ^ b) * local, local), local)
                score = dot_nt(k_ref[there, cut], query) * HEAD_DIM ** (-0.5)
                good = down + b * local >= begin
                if b == last:
                    good = good & (down + b * local <= rows)
                share = jnp.where(good, jnp.exp(score - log), 0.0)
                shares.append(share)
                pushes.append(dot_nt(v_ref[there, cut], dout))
            inner = functools.reduce(jnp.add, [jnp.sum(s * d, axis=0, keepdims=True) for s, d in zip(shares, pushes)])
            dquery = jnp.zeros((local, HEAD_DIM), f32)
            for b in range(last + 1):
                there = pl.ds(pl.multiple_of((member ^ b) * local, local), local)
                dscore = (shares[b] * (pushes[b] - inner) * HEAD_DIM ** (-0.5)).astype(bf16)
                dquery = dquery + dot_tn(dscore, k_ref[there, cut])
                dk_ref[there, cut] += dot_nn(dscore, query)
                dv_ref[there, cut] += dot_nn(shares[b].astype(bf16), dout)
            dq_ref[:, cut] = dquery
            term = term + jnp.sum(dquery * query.astype(f32), axis=1, keepdims=True)
        term_refs[0][...] = as_row(term)

    for last in range(members):
        pl.when(block == last)(functools.partial(run, last))

    if half:

        @pl.when(step == count - 1)
        def _():
            for b in range(members):
                here = slice(b * local, (b + 1) * local)
                value = jnp.sum(dk_ref[here] * k_ref[here].astype(f32), axis=1, keepdims=True)
                term_refs[1][:, here] = as_row(value)


def attend_back(docs, half, scal, q, k, v, weight, enter, leave, grads, atts, logs, normed, before, *deps):
    group_len, slice_width = q.shape
    local = grads[0].shape[0]
    width, rank = (weight.shape[1], enter.shape[1])
    count = len(grads)
    f32, bf16 = (jnp.float32, jnp.bfloat16)
    low_grad = jax.ShapeDtypeStruct((rank, slice_width), f32)
    outs = (
        jax.ShapeDtypeStruct((count * local, slice_width), f32),
        jax.ShapeDtypeStruct((group_len, slice_width), f32),
        jax.ShapeDtypeStruct((group_len, slice_width), f32),
        low_grad,
        low_grad,
        low_grad,
        jax.ShapeDtypeStruct((1, count * local), f32),
    ) + ((jax.ShapeDtypeStruct((1, group_len), f32),) if half else ())
    return pl.pallas_call(
        functools.partial(attend_back_kernel, docs, half, local),
        grid=(count,),
        out_shape=outs,
        in_specs=[full(SMEM)] + [full()] * (6 + 4 * count + len(before)) + [full(pl.ANY)] * len(deps),
        out_specs=(pl.BlockSpec((local, slice_width), lambda i: (i, 0)),)
        + (full(),) * 5
        + (pl.BlockSpec((1, local), lambda i: (0, i)),)
        + ((full(),) if half else ()),
        scratch_shapes=[
            pltpu.VMEM((local, width + rank), bf16),
            pltpu.VMEM((local, slice_width), bf16),
            pltpu.VMEM((local, slice_width), bf16),
            pltpu.VMEM((8, local), f32),
            pltpu.VMEM((local, slice_width + rank), bf16),
        ],
        compiler_params=params(),
        cost_estimate=cost(8_000_000_000, 14_000_000, 700_000),
        name="attend_back",
    )(scal, q, k, v, weight, enter, leave, *grads, *atts, *logs, *normed, *before, *deps)


def project_back_kernel(docs, local, scal_ref, *refs):
    f32, bf16 = (jnp.float32, jnp.bfloat16)
    near_ref, far_ref, dk_ref, dv_ref, p_ref, square_ref, term_ref, gains_ref, cos_ref, sin_ref, normed_ref, low_ref = refs[:12]
    w_ref, enter_ref, leave_ref, route_ref, *refs = refs[12:]
    *dx_refs, enter_grad, leave_grad, dp_ref, dlow_ref, turned = refs
    rows, slice_width = near_ref.shape
    rank = SETS * RANK
    member = scal_ref[0]
    step = pl.program_id(0)
    members = pl.num_programs(0)
    width = slice_width * members
    count = rows // local

    @pl.when(step == 0)
    def _():
        inverse = lax.rsqrt(square_ref[...] / width + EPS)
        biases = inverse * inverse * term_ref[...] / width
        for i in range(2):
            for half in range(2):
                here = slice(half * rows, (half + 1) * rows)
                scale, bias = (column(inverse[i : i + 1, here]), column(biases[i : i + 1, here]))
                for at in range(0, slice_width, HEAD_DIM):
                    cut = slice(at, at + HEAD_DIM)
                    value = dk_ref[here, cut] if i else (far_ref if half else near_ref)[:, cut]
                    value = value * cos_ref[here] - pltpu.roll(value, HEAD_DIM // 2, 1) * sin_ref[here]
                    value = value * gains_ref[i : i + 1, cut] * scale - p_ref[i, here, cut] * bias
                    dp_ref[i, here, cut] = value.astype(bf16)
        dp_ref[2] = dv_ref[...].astype(bf16)
        for b in range(2 * count):
            here = slice(b * local, (b + 1) * local)
            mark = block_marks(scal_ref, docs, member ^ b, local)
            for i in range(3):
                value = dot_nt(dp_ref[i, here], leave_ref[i]) * SCALE * mark
                dlow_ref[here, i * rank : (i + 1) * rank] = value.astype(bf16)
                turned[i * rank : (i + 1) * rank, here] = value.T.astype(bf16)
        for i in range(3):
            leave_grad[i] = dot_tn(low_ref[i], dp_ref[i])

    enter_grad[0, : 3 * rank] = dot_nn(turned[...], normed_ref[...]).astype(bf16)
    enter_grad[0, 3 * rank :] = route_ref[0]
    spread_back(dx_refs, [dp_ref[i, rows:] for i in range(3)], dlow_ref[rows:], w_ref, enter_ref)


def spread_back(dx_refs, grads, low, w_ref, enter_ref):
    value = dot_nt(grads[0], w_ref[0]) + dot_nt(grads[1], w_ref[1]) + dot_nt(grads[2], w_ref[2])
    value = value + dot_nt(low, jnp.concatenate([enter_ref[i] for i in range(3)], axis=1))
    value = value.astype(jnp.bfloat16)
    local = dx_refs[0].shape[0]
    for b, dx_ref in enumerate(dx_refs):
        dx_ref[...] = value[b * local : (b + 1) * local]


def project_back(docs, local, scal, near, far, dk, dv, p, squares, terms, gains, cosine, sine, normed, low, weight, enter, leave, route_grad, *deps):
    rows, slice_width = near.shape
    width, rank = (normed.shape[1], enter.shape[2])
    members, count = (2 * rows // local, rows // local)
    tall = 3 * rank + route_grad.shape[1]
    f32, bf16 = (jnp.float32, jnp.bfloat16)
    pick = lambda i, scal: scal[0] ^ i
    sums = pl.BlockSpec((1, tall, slice_width), lambda i, scal: (i, 0, 0))
    in_specs = [full()] * 10 + [
        pl.BlockSpec((2 * rows, slice_width), lambda i, scal: (0, pick(i, scal))),
        full(),
        pl.BlockSpec((3, slice_width, slice_width), lambda i, scal: (0, pick(i, scal), 0)),
        pl.BlockSpec((3, slice_width, rank), lambda i, scal: (0, pick(i, scal), 0)),
        full(),
        pl.BlockSpec((1, tall - 3 * rank, slice_width), lambda i, scal: (i, 0, 0)),
    ] + [full(pl.ANY)] * len(deps)
    return pl.pallas_call(
        lambda *refs: project_back_kernel(docs, local, *refs[:17], *refs[17 + len(deps) :]),
        out_shape=(jax.ShapeDtypeStruct((local, width), bf16),) * count
        + (
            jax.ShapeDtypeStruct((members, tall, slice_width), bf16),
            jax.ShapeDtypeStruct((3, rank, slice_width), f32),
            jax.ShapeDtypeStruct((3, 2 * rows, slice_width), bf16),
            jax.ShapeDtypeStruct((2 * rows, 3 * rank), bf16),
        ),
        grid_spec=pltpu.PrefetchScalarGridSpec(
            num_scalar_prefetch=1,
            grid=(members,),
            in_specs=in_specs,
            out_specs=(pl.BlockSpec((local, slice_width), lambda i, scal: (0, pick(i, scal))),) * count
            + (sums, full(), full(), full()),
            scratch_shapes=[pltpu.VMEM((3 * rank, 2 * rows), bf16)],
        ),
        compiler_params=params(),
        cost_estimate=cost(2 * rows * (width * 3 * slice_width + 6 * rank * width), 20_000_000),
        name="project_back",
    )(scal, near, far, dk, dv, p, squares, terms, gains, cosine, sine, normed, low, weight, enter, leave, route_grad, *deps)


def project_near(local, grads, low, weight, enter, *deps):
    _, group_len, slice_width = grads.shape
    rows, width, rank = (group_len // 2, weight.shape[1], enter.shape[2])
    count = rows // local
    step = slice_width
    out = jax.ShapeDtypeStruct((local, width), jnp.bfloat16)

    def kernel(grads_ref, low_ref, w_ref, enter_ref, *refs):
        spread_back(refs[-count:], [grads_ref[i] for i in range(3)], low_ref[...], w_ref, enter_ref)

    return pl.pallas_call(
        kernel,
        grid=(width // step,),
        out_shape=(out,) * count,
        in_specs=[
            pl.BlockSpec((3, rows, slice_width), lambda i: (0, 0, 0)),
            pl.BlockSpec((rows, 3 * rank), lambda i: (0, 0)),
            pl.BlockSpec((3, step, slice_width), lambda i: (0, i, 0)),
            pl.BlockSpec((3, step, rank), lambda i: (0, i, 0)),
        ]
        + [full(pl.ANY)] * len(deps),
        out_specs=(pl.BlockSpec((local, step), lambda i: (0, i)),) * count,
        compiler_params=params(),
        cost_estimate=cost(2 * rows * (width * 3 * slice_width), 10_000_000),
        name="project_near",
    )(grads, low, weight, enter, *deps)


def finish_kernel(*refs):
    f32 = jnp.float32
    *parts, dh_ref, x_ref, gain_ref, out_ref = refs
    x = x_ref[...].astype(f32)
    back = functools.reduce(jnp.add, [part[...].astype(f32) for part in parts]) * gain_ref[...].astype(f32)
    scale = rms_scale(x)
    out = dh_ref[...] + scale * back - x * scale**3 * jnp.mean(x * back, axis=-1, keepdims=True)
    out_ref[...] = out.astype(out_ref.dtype)


def finish(grads, dh, x, gain):
    return pl.pallas_call(
        finish_kernel,
        out_shape=jax.ShapeDtypeStruct(x.shape, jnp.bfloat16),
        in_specs=[full()] * (3 + len(grads)),
        out_specs=full(),
        compiler_params=params(),
        cost_estimate=cost(10 * x.size, 12 * x.size),
        name="finish",
    )(*grads, dh, x, gain)


def upstream_kernel(scal_ref, named_ref, *refs):
    blocks = named_ref.shape[0]
    f32, bf16 = (jnp.float32, jnp.bfloat16)
    upstream_refs, (down_w, down_leave, rank_ref, rows_ref, back_ref, low_ref, places) = (refs[:blocks], refs[-7:])
    experts, local = places.shape[1:]
    cap = rows_ref.shape[1] // blocks

    @pl.when((pl.program_id(0) == 0) | (pl.num_programs(1) > 1))
    def _():
        earlier = lax.broadcasted_iota(jnp.int32, (local, local), 0) < lax.broadcasted_iota(jnp.int32, (local, local), 1)
        bits = lax.broadcasted_iota(jnp.int32, (experts, local), 0)
        for b in range(blocks):
            hot = (jnp.right_shift(named_ref[b], bits) & 1).astype(f32)
            rank = dot_nn(hot.astype(bf16), earlier.astype(f32).astype(bf16))
            places[b] = jnp.where(hot > 0.0, rank, -1.0)

    mine = pl.ds(scal_ref[0] * pl.num_programs(0) + pl.program_id(0), 1)
    slots = lax.broadcasted_iota(jnp.int32, (cap, local), 0).astype(f32)
    for b in range(blocks):
        rank_ref[0, b] = places[b, mine]
        pick = (places[b, mine] == slots).astype(bf16)
        rows_ref[0, b * cap : (b + 1) * cap] = dot_nn(pick, upstream_refs[b][...]).astype(bf16)
    back_ref[0] = dot_nt(rows_ref[0], down_w[0]).astype(bf16)
    low_ref[0] = dot_nt(rows_ref[0], down_leave[0])


def run_upstream(scal, named, upstream, down, down_leave, *deps):
    members, _, local = named.shape
    experts, ff, width = down.shape
    low = down_leave.shape[1]
    blocks = min(members, 4)
    turns = members // blocks
    count = blocks * CAP
    f32, bf16 = (jnp.float32, jnp.bfloat16)
    rows = lambda wide: pl.BlockSpec((1, count, wide), lambda e, r: (e, r, 0))
    return pl.pallas_call(
        lambda *refs: upstream_kernel(*refs[: 4 + blocks], *refs[4 + blocks + len(deps) :]),
        grid=(experts, turns),
        out_shape=(
            jax.ShapeDtypeStruct((experts, members, 1, local), f32),
            jax.ShapeDtypeStruct((experts, members * CAP, width), bf16),
            jax.ShapeDtypeStruct((experts, members * CAP, ff), bf16),
            jax.ShapeDtypeStruct((experts, members * CAP, low), f32),
        ),
        in_specs=[full(SMEM), pl.BlockSpec((blocks, 1, local), lambda e, r: (r, 0, 0))]
        + [pl.BlockSpec((local, width), lambda e, r: (r, 0), pipeline_mode=pl.Buffered(1))] * blocks
        + [pl.BlockSpec((1, ff, width), lambda e, r: (e, 0, 0)), pl.BlockSpec((1, low, width), lambda e, r: (e, 0, 0))]
        + [full(pl.ANY)] * len(deps),
        out_specs=(pl.BlockSpec((1, blocks, 1, local), lambda e, r: (e, r, 0, 0)), rows(width), rows(ff), rows(low)),
        scratch_shapes=[pltpu.VMEM((blocks, EXPERTS, local), f32)],
        compiler_params=params(),
        cost_estimate=cost(2 * experts * members * CAP * width * ff, 40_000_000),
        name="upstream",
    )(scal, named, *by_block(upstream, blocks), down, down_leave, *deps)


def by_block(parts, blocks):
    return [jnp.concatenate(parts[b::blocks]) if len(parts) > blocks else parts[b] for b in range(blocks)]


def expert_kernel(line, docs, scal_ref, rank_ref, grads_ref, back_ref, low_ref, route_ref, route_enter, route_leave, *refs):
    blocks = rank_ref.shape[1]
    normed_refs, refs, probs = (refs[:blocks], refs[blocks:-1], refs[-1])
    width = grads_ref.shape[2]
    turn = pl.program_id(1)
    local = rank_ref.shape[3]

    @pl.when((pl.program_id(0) == 0) | (pl.num_programs(1) > 1))
    def _():
        for b in range(blocks):
            mark = block_marks(scal_ref, docs, scal_ref[0] ^ (turn * blocks + b), local)
            probs[b] = router(normed_refs[b][:, :width], mark, route_ref, route_enter, route_leave)[1]

    mine = pl.ds(scal_ref[0] * pl.num_programs(0) + pl.program_id(0), 1)
    weights = [probs[b, mine] for b in range(blocks)]
    expert_rows(line, docs, scal_ref, rank_ref, weights, normed_refs, grads_ref.at[0], back_ref.at[0], low_ref.at[0], *refs)


def expert_rows(
    line,
    docs,
    scal_ref,
    rank_ref,
    weight_rows,
    normed_refs,
    grads_in,
    back_in,
    low_in,
    gate_w,
    up_w,
    down_w,
    gate_enter,
    gate_leave,
    up_enter,
    up_leave,
    down_enter,
    down_leave,
    place_ref,
    mixed_ref,
    grad_ref,
    score_ref,
    *rest,
):
    inner = len(rest) - 9
    sums, (rows_in, hidden, grad_gate, grad_up, marks, out_tile, back_tile, done, full_rows) = (rest[:inner], rest[inner:])
    f32, bf16 = (jnp.float32, jnp.bfloat16)
    blocks, local, width = (rank_ref.shape[1], rank_ref.shape[3], grads_in.shape[1])
    cap = mixed_ref.shape[2]
    expert, turn = (pl.program_id(0), pl.program_id(1))
    count = blocks * cap
    ff = hidden.shape[1]
    slots = lax.broadcasted_iota(jnp.int32, (cap, local), 0).astype(f32)
    weights = []
    for b in range(blocks):
        hit = rank_ref[0, b] == slots
        pick = hit.astype(bf16)
        weights.append(jnp.sum(jnp.where(hit, weight_rows[b], 0.0), axis=1, keepdims=True))
        here = slice(b * cap, (b + 1) * cap)
        mark = block_marks(scal_ref, docs, scal_ref[0] ^ (turn * blocks + b), local).astype(bf16)
        rows_in[here, :] = dot_nn(pick, normed_refs[b][:, :width]).astype(bf16)
        marks[here, :] = dot_nn(pick, mark)
    weight = jnp.concatenate(weights, axis=0)
    mark = marks[...]
    rank = mark.shape[1]
    low = dot_nn(rows_in[...], jnp.concatenate([gate_enter[0], up_enter[0]], axis=1))
    low_gate = (low[:, :rank] * mark).astype(bf16) * SCALE
    low_up = (low[:, rank:] * mark).astype(bf16) * SCALE
    grad_low_down = (low_in[...] * (SCALE * weight) * mark).astype(bf16)
    step = min(256, ff)
    for at in range(0, ff, step):
        cut = slice(at, at + step)
        gate = dot_nn(rows_in[...], gate_w[0, :, cut]) + dot_nn(low_gate, gate_leave[0, :, cut])
        up = dot_nn(rows_in[...], up_w[0, :, cut]) + dot_nn(low_up, up_leave[0, :, cut])
        back = back_in[:, cut].astype(f32) * weight + dot_nt(grad_low_down, down_enter[0, cut, :])
        sigma = 1.0 / (1.0 + jnp.exp(-gate))
        silu = gate * sigma
        hidden[:, cut] = (silu * up).astype(bf16)
        grad_gate[:, cut] = (back * up * sigma * (1.0 + gate * (1.0 - sigma))).astype(bf16)
        grad_up[:, cut] = (back * silu).astype(bf16)
    low_down = (dot_nn(hidden[...], down_enter[0]) * mark).astype(bf16) * SCALE
    grad_low_gate = (dot_nt(grad_gate[...], gate_leave[0]) * SCALE * mark).astype(bf16)
    grad_low_up = (dot_nt(grad_up[...], up_leave[0]) * SCALE * mark).astype(bf16)
    grad_low = jnp.concatenate([grad_low_gate, grad_low_up], axis=1)
    step = out_tile.shape[3]
    sent = []

    def send(slot, cut):
        there = pl.ds(turn * blocks, blocks)
        copies = [
            pltpu.make_async_copy(out_tile.at[slot], mixed_ref.at[there, expert, :, cut], done.at[0, slot]),
            pltpu.make_async_copy(back_tile.at[slot], grad_ref.at[there, expert, :, cut], done.at[1, slot]),
        ]
        for copy in copies:
            copy.start()
        sent.append(copies)

    score = jnp.zeros((count, 1), f32)
    for at in range(0, width, step):
        cut = slice(at, at + step)
        out = dot_nn(hidden[...], down_w[0, :, cut]) + dot_nn(low_down, down_leave[0, :, cut])
        score = score + jnp.sum(out * grads_in[:, cut].astype(f32), axis=1, keepdims=True)
        back = dot_nt(grad_gate[...], gate_w[0, cut, :]) + dot_nt(grad_up[...], up_w[0, cut, :])
        back = back + dot_nt(grad_low, jnp.concatenate([gate_enter[0, cut, :], up_enter[0, cut, :]], axis=1))
        out = (out * weight).astype(bf16)
        back = back.astype(bf16)
        slot = len(sent) % 2
        if len(sent) >= 2:
            for copy in sent[-2]:
                copy.wait()
        for b in range(blocks):
            out_tile[slot, b] = out[b * cap : (b + 1) * cap]
            back_tile[slot, b] = back[b * cap : (b + 1) * cap]
        send(slot, pl.ds(at, step))
    for b in range(blocks):
        hit = rank_ref[0, b] == slots
        score_ref[0, b] = jnp.sum(jnp.where(hit, score[b * cap : (b + 1) * cap], 0.0), axis=0, keepdims=True)

    def keep(value, row, ref_at):
        piece = value.shape[1] // (line * inner)
        value = value.astype(bf16)
        full_rows[: value.shape[0], : value.shape[1]] = value
        columns = slice(ref_at, ref_at + piece)
        for c in range(line * inner):
            part = slice(c * piece, (c + 1) * piece)
            for q in range(inner):

                @pl.when(place_ref[1, c] == q)
                def _():
                    for at in range(0, value.shape[0], rank):
                        if inner != 2 or q == 0:
                            source = full_rows[at : at + rank, part]
                            target = sums[q].at[place_ref[0, c], 0, slice(row + at, row + at + rank), columns]
                            if pl.num_programs(1) > 1:
                                old = jnp.where(turn > 0, target[...].astype(f32), 0.0)
                                source = (old + source.astype(f32)).astype(bf16)
                            target[...] = source
                            continue
                        for d in range(docs):
                            there = pl.ds(pl.multiple_of(at + scal_ref[1 + docs + d] * RANK, RANK), RANK)
                            source = full_rows[there, part]
                            for d2 in range(d):
                                repeated = scal_ref[1 + docs + d2] == scal_ref[1 + docs + d]
                                source = jnp.where(repeated, jnp.zeros_like(source), source)
                            to = ((row + at) // rank * docs + d) * RANK
                            target = sums[q].at[place_ref[0, c], 0, slice(to, to + RANK), columns]
                            if pl.num_programs(1) > 1:
                                old = jnp.where(turn > 0, target[...].astype(f32), 0.0)
                                source = (old + source.astype(f32)).astype(bf16)
                            target[...] = source

    wide = width // (line * inner)
    keep(dot_tn(grad_low, rows_in[...]), 0, 0)
    keep(dot_tn((low_down.astype(f32) * weight).astype(bf16), grads_in[...]), 2 * rank, 0)
    keep(dot_tn(low_gate, grad_gate[...]), 0, wide)
    keep(dot_tn(low_up, grad_up[...]), rank, wide)
    keep(dot_tn(grad_low_down, hidden[...]), 2 * rank, wide)
    for copies in sent[-2:]:
        for copy in copies:
            copy.wait()


def run_experts(docs, scal, ranks, grads, back, low_back, route, route_enter, route_leave, normed, place, inner, *weights):
    experts, members, _, local = ranks.shape
    width = grads.shape[2]
    ff = back.shape[2]
    low = SETS * RANK
    blocks = min(members, 4)
    turns = members // blocks
    packs = place.shape[1]
    line = packs // inner
    bf16 = jnp.bfloat16
    count = blocks * CAP
    tile = min(512, width)
    by_turn = lambda e, r: (e, r, 0, 0)
    rows = lambda wide: pl.BlockSpec((1, count, wide), lambda e, r: (e, r, 0))
    once = lambda wide: [pl.BlockSpec((local, wide), lambda e, r: (r, 0), pipeline_mode=pl.Buffered(1))] * blocks
    per_expert = lambda value: pl.BlockSpec((1,) + value.shape[1:], lambda e, r: (e, 0, 0))
    packed = docs * RANK if inner == 2 else low
    sums = [jax.ShapeDtypeStruct((line, experts, 3 * (packed if q else low), (width + ff) // packs), bf16) for q in range(inner)]
    rows_out = jax.ShapeDtypeStruct((members, experts, CAP, width), bf16)
    return pl.pallas_call(
        functools.partial(expert_kernel, line, docs),
        grid=(experts, turns),
        out_shape=(rows_out, rows_out, jax.ShapeDtypeStruct(ranks.shape, jnp.float32), *sums),
        in_specs=[full(SMEM), pl.BlockSpec((1, blocks, 1, local), by_turn), rows(width), rows(ff), rows(low)]
        + [full()] * 3
        + once(width + low)
        + [per_expert(value) for value in weights]
        + [full(SMEM)],
        out_specs=(full(pl.ANY), full(pl.ANY), pl.BlockSpec((1, blocks, 1, local), by_turn))
        + tuple(pl.BlockSpec((line, 1) + value.shape[2:], lambda e, r: (0, e, 0, 0)) for value in sums),
        scratch_shapes=[
            pltpu.VMEM((count, width), bf16),
            pltpu.VMEM((count, ff), bf16),
            pltpu.VMEM((count, ff), bf16),
            pltpu.VMEM((count, ff), bf16),
            pltpu.VMEM((count, low), jnp.float32),
            pltpu.VMEM((2, blocks, CAP, tile), bf16),
            pltpu.VMEM((2, blocks, CAP, tile), bf16),
            pltpu.SemaphoreType.DMA((2, 2)),
            pltpu.VMEM((2 * low, width), bf16),
            pltpu.VMEM((blocks, EXPERTS, local), jnp.float32),
        ],
        compiler_params=params(),
        cost_estimate=cost(2 * experts * members * CAP * (width * ff * 5 + 9 * low * (width + ff)), 60_000_000),
        name="experts",
    )(scal, ranks, grads, back, low_back, route, route_enter, route_leave, *by_block(normed, blocks), *weights, place)


def mix(rank_ref, rows_ref, pick_ref, step):
    experts, cap, local = (rows_ref.shape[1], rows_ref.shape[2], rank_ref.shape[3])

    @pl.when(step == 0)
    def _():
        slots = lax.broadcasted_iota(jnp.int32, (cap, local), 0).astype(jnp.float32)
        pick = jnp.concatenate([(rank_ref[e, 0] == slots).astype(jnp.float32) for e in range(experts)], axis=0)
        pick_ref[...] = pick.T.astype(jnp.bfloat16)

    rows = jnp.concatenate([rows_ref[0, e] for e in range(experts)], axis=0)
    return dot_nn(pick_ref[...], rows)


def mix_grads(scal_ref, rank_ref, score_ref, rows_ref, added_ref, back_ref, pick_ref, step):
    f32, bf16 = (jnp.float32, jnp.bfloat16)
    experts, local = (rows_ref.shape[1], rank_ref.shape[3])
    piece, low = (rows_ref.shape[3], SETS * RANK)
    width = back_ref.shape[1] - low
    columns = pl.ds(pl.multiple_of(step * piece, 128), piece)
    value = mix(rank_ref, rows_ref, pick_ref, step)
    if added_ref is not None:
        value = value + added_ref[:, columns].astype(f32)
    back_ref[:, columns] = value.astype(bf16)

    @pl.when(step == 0)
    def _():
        lines = lax.broadcasted_iota(jnp.int32, (low, local), 0)
        table = jnp.zeros((low, local), f32)
        for e in range(experts):
            score = score_ref[e, 0]
            whole = score.astype(bf16).astype(f32)
            at = scal_ref[0] * experts + e
            table = jnp.where(lines == at, whole, table)
            table = jnp.where(lines == at + EXPERTS, score - whole, table)
        table = table.T
        if added_ref is not None:
            table = table + added_ref[:, width:].astype(f32)
        back_ref[:, width:] = table.astype(bf16)


def combine_kernel(added, scal_ref, rank_ref, score_ref, rows_ref, *refs):
    back_ref, pick_ref = refs[-2:]
    mix_grads(scal_ref, rank_ref, score_ref, rows_ref, refs[0] if added else None, back_ref, pick_ref, pl.program_id(0))


def combine(scal, ranks, scores, rows, place, addend, *deps):
    experts, members, _, local = ranks.shape
    width = rows.shape[3]
    piece = width // 2
    low = SETS * RANK
    one = pl.BlockSpec((experts, 1, 1, local), lambda n: (0, place, 0, 0))
    more = () if addend is None else (addend,)
    return pl.pallas_call(
        functools.partial(combine_kernel, addend is not None),
        grid=(2,),
        out_shape=jax.ShapeDtypeStruct((local, width + low), jnp.bfloat16),
        in_specs=[full(SMEM), one, one, pl.BlockSpec((1, experts, CAP, piece), lambda n: (place, 0, 0, n))]
        + [full()] * len(more)
        + [full(pl.ANY)] * len(deps),
        out_specs=full(),
        scratch_shapes=[pltpu.VMEM((local, experts * CAP), jnp.bfloat16)],
        compiler_params=params(),
        cost_estimate=cost(2 * local * experts * CAP * width, 2 * experts * CAP * width),
        name="combine",
    )(scal, ranks, scores, rows, *more, *deps)


def combine_last_kernel(scal_ref, rank_ref, score_ref, grads_ref, rows_ref, added_ref, *refs):
    members = pl.num_programs(0)
    out_refs, (back_ref, pick_ref) = (refs[-2 - members : -2], refs[-2:])
    block, step = (pl.program_id(0), pl.program_id(1))
    piece = rows_ref.shape[3]
    columns = pl.ds(pl.multiple_of(step * piece, 128), piece)
    value = mix(rank_ref, rows_ref, pick_ref, step).astype(jnp.bfloat16)
    for b in range(members):

        @pl.when(block == b)
        def _():
            out_refs[b][:, columns] = value

    @pl.when(block == 0)
    def _():
        mix_grads(scal_ref, rank_ref, score_ref, grads_ref, added_ref, back_ref, pick_ref, step)


def combine_last(scal, ranks, scores, grads, mixed, addend, *deps):
    experts, members, _, local = ranks.shape
    width = grads.shape[3]
    piece = width // 2
    low = SETS * RANK
    out = jax.ShapeDtypeStruct((local, width), jnp.bfloat16)
    one = pl.BlockSpec((experts, 1, 1, local), lambda b, n: (0, b, 0, 0))
    first = lambda b, n: (0, 0, 0, jnp.where(b == 0, n, 1))
    return pl.pallas_call(
        lambda *refs: combine_last_kernel(*refs[:6], *refs[6 + len(deps) :]),
        grid=(members, 2),
        out_shape=(out,) * members + (jax.ShapeDtypeStruct((local, width + low), jnp.bfloat16),),
        in_specs=[full(SMEM), one, one]
        + [pl.BlockSpec((1, experts, CAP, piece), first), pl.BlockSpec((1, experts, CAP, piece), lambda b, n: (b, 0, 0, n))]
        + [full()]
        + [full(pl.ANY)] * len(deps),
        out_specs=(full(),) * (members + 1),
        scratch_shapes=[pltpu.VMEM((local, experts * CAP), jnp.bfloat16)],
        compiler_params=params(),
        cost_estimate=cost(2 * 5 * local * experts * CAP * width, 10 * experts * CAP * width),
        name="combine_last",
    )(scal, ranks, scores, grads, mixed, addend, *deps)


def per_device(
    tokens,
    cotangent,
    pack_order,
    doc_lengths,
    doc_sets,
    routes,
    attention_gain,
    query_gain,
    key_gain,
    feed_gain,
    qkv_weight,
    out_weight,
    router_weight,
    gate_weight,
    up_weight,
    down_weight,
    qkv_enter,
    qkv_leave,
    out_enter,
    out_leave,
    router_enter,
    router_leave,
    gate_enter,
    gate_leave,
    up_enter,
    up_leave,
    down_enter,
    down_leave,
):
    members = lax.axis_size("ep")
    packs = lax.axis_size("grp")
    pack = lax.axis_index("grp")
    member = lax.axis_index("ep")
    local, width = tokens.shape
    slice_width = width // members
    experts_here = gate_weight.shape[0]
    own_cols = member * slice_width
    count = members // 2
    low = SETS * RANK
    f32, bf16 = (jnp.float32, jnp.bfloat16)
    slot = jnp.sum(jnp.where(pack_order == pack, jnp.arange(packs, dtype=jnp.int32), 0))
    named = jnp.sum(jnp.left_shift(jnp.int32(1), routes), axis=1)
    documents_here = jnp.concatenate([doc_lengths[0], doc_sets[0]])
    info = jnp.concatenate([named, jnp.pad(documents_here, (0, 128 - documents_here.shape[0]))])
    info = jnp.stack(gather_parts(info, "grp"))
    other = jnp.sum(jnp.where(pack_order == pack ^ 1, jnp.arange(packs, dtype=jnp.int32), 0))
    other = lax.dynamic_index_in_dim(info, other ^ pack, 0, keepdims=False)
    info = lax.dynamic_index_in_dim(info, slot ^ pack, 0, keepdims=False)
    blocks = [member ^ j for j in range(members)]
    named = info[:local]
    docs = doc_lengths.shape[1]
    lengths, sets = (info[local : local + docs], info[local + docs : local + 2 * docs])
    ends = jnp.cumsum(lengths)
    starts = ends - lengths
    scal = jnp.concatenate([member[None].astype(jnp.int32), ends, sets, starts])
    gain_one, gain_two = (attention_gain[None], feed_gain[None])
    route, route_leave = (router_weight.T, router_leave.T)
    adapters = (gain_one, qkv_weight, qkv_enter, qkv_leave)
    kept = project(docs, 0, scal, gather_near(tokens, "ep"), *adapters, None)
    token_parts = gather_far(tokens, "ep", kept[4])
    named_all = jnp.stack(gather_parts(named.reshape(1, local), "ep"))
    kept = project(docs, 1, scal, token_parts, *adapters, kept)
    normed_all, low_all, projected, values, squares = kept
    late = fence(scal, values)
    ends, starts = (late[1 : 1 + docs], late[1 + 2 * docs :])
    rows = (jnp.stack(blocks)[:, None] * local + jnp.arange(local, dtype=jnp.int32)[None, :]).reshape(-1)
    begin = starts[0]
    for k in range(1, docs):
        begin = jnp.where(rows >= ends[k - 1], starts[k], begin)
    cosine, sine = angles(rows - begin)
    upstream_far = gather_near(swap(fence(cotangent, token_parts[0], named_all), "ep", members // 2), "ep")
    upstream_parts = gather_near(cotangent, "ep") + upstream_far
    squares = sum_relative(squares, "ep", local)
    own_gain = lambda gain: lax.dynamic_slice_in_dim(gain, own_cols, slice_width, 0)
    gains = jnp.stack([own_gain(query_gain), own_gain(key_gain)]).astype(f32)
    queries, keys = prepare(width, projected, squares, gains, cosine, sine, local, upstream_parts[-1], named_all)
    heads = [None] * members

    def attend_place(place, addend, *deps):
        heads[place] = attend(docs, place, local, scal, queries, keys, values, out_weight, out_enter, addend, *deps)
        return heads[place][1], heads[place][2]

    top = members // 2
    outs = reduce_scatter(attend_place, "ep")
    hidden_state, normed_two, low_router, probs = middle(
        docs, scal, tokens, outs, out_leave, gain_two, route, router_enter, route_leave
    )

    upstream_rows = run_upstream(scal, named_all, upstream_parts, down_weight, down_leave, normed_two)
    normed_two_parts = gather_near(normed_two, "ep") + gather_far(normed_two, "ep", upstream_rows[0])
    inner = packs // LINE
    chunk_ids = jnp.arange(packs, dtype=jnp.int32)
    place = jnp.stack([(chunk_ids // inner - pack // inner) % LINE, (chunk_ids % inner - pack % inner) % inner])
    ranks = upstream_rows[0]
    mixed_rows, grad_rows, scores, *expert_sums = run_experts(
        docs,
        scal,
        *upstream_rows,
        route,
        router_enter,
        route_leave,
        normed_two_parts,
        place,
        inner,
        gate_weight,
        up_weight,
        down_weight,
        gate_enter,
        gate_leave,
        up_enter,
        up_leave,
        down_enter,
        down_leave,
    )
    mixed = []

    def combine_place(place, addend, *deps):
        if place:
            part = combine(scal, ranks, scores, grad_rows, place, addend, *deps)
        else:
            *parts, part = combine_last(scal, ranks, scores, grad_rows, mixed_rows, addend, *deps)
            mixed.extend(parts)
        return part, part

    grads = reduce_scatter(combine_place, "ep")
    grad_hidden, grad_branch, grad_router_leave = middle_back(
        docs, scal, grads, probs, hidden_state, cotangent, low_router, gain_two, route, router_enter, route_leave
    )
    pair = lambda a, b: (a.astype(f32) + b.astype(f32)).astype(bf16)
    mixed = [pair(mixed[j], swap(mixed[j + 1], "ep", 1)) for j in range(0, members, 2)]
    mixed_near, mixed_far = (scatter_even(mixed[: top // 2], "ep"), scatter_even(mixed[top // 2 :], "ep"))

    inside = (queries, keys, values, out_weight, out_enter, out_leave)

    def attend_half_back(half, branch, before, *deps):
        part = slice(half * count, (half + 1) * count)
        atts, logs = ([head[i] for head in heads[part]] for i in (0, 2))
        return attend_back(docs, half, scal, *inside, branch, atts, logs, normed_two_parts[part], before, *deps)

    near = attend_half_back(0, gather_near(grad_branch, "ep"), ())
    branch_far = gather_far(grad_branch, "ep", near[6])
    other_sets = other[local + docs : local + 2 * docs]
    line_sums = sum_experts(docs, other_sets, expert_sums, near[6])
    far = attend_half_back(1, branch_far, near[1:6], line_sums[0])
    mixed_got = swap(fence(mixed_far, branch_far[0]), "ep", top)
    grad_keys, grad_values, *low_grads = far[1:6]
    terms = jnp.concatenate([jnp.concatenate([near[6], far[6]], axis=1), far[7]])
    line = LineSum(line_sums, "grp", LINE, inner)
    got = line.send(1)
    terms = sum_relative(fence(terms, *got, mixed_got), "ep", local)
    line.add(1, got)
    leave_rows = low // members
    leave_parts = jnp.stack([lax.dynamic_slice_in_dim(grad_router_leave, b * leave_rows, leave_rows, 1) for b in blocks])
    leave_parts = jnp.pad(leave_parts.astype(bf16), ((0, 0), (0, 0), (0, slice_width - leave_rows)))
    shared = (projected, squares, terms, gains, cosine, sine, normed_all, low_all, qkv_weight, qkv_enter, qkv_leave)
    ready = line.ready(2)
    *far_parts, enter_sums, leave_sums, projected_grads, low_grad = project_back(
        docs, local, scal, near[0], far[0], grad_keys, grad_values, *shared, leave_parts, *ready
    )
    got = line.send(2, ready)
    line.add(2, got)
    *far_parts, enter_sums, leave_sums = (fence(value, *got) for value in (*far_parts, enter_sums, leave_sums))
    input_far = scatter_even([pair(far_parts[j], swap(far_parts[j + 1], "ep", 1)) for j in range(0, count, 2)], "ep")
    near_parts = project_near(local, projected_grads, low_grad, qkv_weight, qkv_enter, input_far)
    input_got = swap(input_far, "ep", top)
    if count == 2:
        inputs = (near_parts[0], swap(near_parts[1], "ep", 1), input_got)
    else:
        inputs = [pair(near_parts[j], swap(near_parts[j + 1], "ep", 1)) for j in range(0, count, 2)]
        inputs = (scatter_even(inputs, "ep"), input_got)
    grad_input = finish(inputs, grad_hidden, tokens, gain_one)
    layer_out = (hidden_state + (mixed_near.astype(f32) + mixed_got.astype(f32))).astype(bf16)

    got = line.send(3)
    line.add(3, got)
    expert_sum = line.total[0]
    by_rows = lambda value: value.astype(bf16).reshape(-1, packs, value.shape[-2] // packs, slice_width).transpose(1, 0, 2, 3)
    joined = jnp.concatenate([by_rows(value) for value in (*low_grads, leave_sums)], axis=1)
    joined = sum_packs(by_place(fence(joined, input_far)), input_got)
    enter_sums = [pair(enter_sums[j], swap(enter_sums[j + 1], "ep", 1)) for j in range(0, members, 2)]
    enter_far = swap(scatter_even(enter_sums[top // 2 :], "ep"), "ep", top)
    enter_sum = fence(pair(scatter_even(enter_sums[: top // 2], "ep"), enter_far), input_got, *got, joined)
    enter_chunks = by_rows(enter_sum[: 3 * low].reshape(3, low, slice_width)).reshape(packs, -1, slice_width)
    leave_chunks = by_rows(enter_sum[3 * low :]).reshape(packs, -1, slice_width)
    enter_sum = sum_packs(by_place(jnp.concatenate([enter_chunks, leave_chunks], axis=1)))
    enter_rows = 3 * low // packs
    wide = width // packs
    turn = lambda value: jnp.swapaxes(value, -1, -2)
    return (
        layer_out,
        grad_input,
        turn(enter_sum[:enter_rows].reshape(3, -1, slice_width)),
        joined[3:],
        turn(joined[0]),
        joined[1],
        turn(joined[2]),
        turn(enter_sum[enter_rows:, :leave_rows]),
        turn(expert_sum[:, :low, :wide]),
        expert_sum[:, :low, wide:],
        turn(expert_sum[:, low : 2 * low, :wide]),
        expert_sum[:, low : 2 * low, wide:],
        turn(expert_sum[:, 2 * low :, wide:]),
        expert_sum[:, 2 * low :, :wide],
    )


def solution(mesh):
    in_specs = (
        P(("grp", "ep"), None),
        P(("grp", "ep"), None),
        P(),
        P("grp", None),
        P("grp", None),
        P(("grp", "ep"), None),
        P(),
        P(),
        P(),
        P(),
        P(None, None, "ep"),
        P("ep", None),
        P(),
        P("ep", None, None),
        P("ep", None, None),
        P("ep", None, None),
        P(),
        P(None, None, "ep"),
        P("ep", None),
        P(),
        P(),
        P(),
        P("ep", None, None),
        P("ep", None, None),
        P("ep", None, None),
        P("ep", None, None),
        P("ep", None, None),
        P("ep", None, None),
    )
    out_specs = (
        P(("grp", "ep"), None),
        P(("grp", "ep"), None),
        P(None, "ep", "grp"),
        P(None, "grp", "ep"),
        P("ep", "grp"),
        P("grp", "ep"),
        P("ep", "grp"),
        P("ep", "grp"),
        P("ep", "grp", None),
        P("ep", None, "grp"),
        P("ep", "grp", None),
        P("ep", None, "grp"),
        P("ep", "grp", None),
        P("ep", None, "grp"),
    )
    return jax.shard_map(
        per_device, mesh=mesh, in_specs=in_specs, out_specs=out_specs, check_vma=False
    )
```

```python
import functools

import jax
import jax.numpy as jnp
from jax import lax
from jax.experimental import pallas as pl
from jax.experimental.pallas import tpu as pltpu
from jax.sharding import PartitionSpec as P

HEAD_DIM = 128
EXPERTS = 16
TOP = 8
SETS = 8
RANK = 16
CAP = 144


EPS = 1e-05
SCALE = 2.0
THETA = 10000.0
NEG = -1e30


def rms_scale(value):
    return lax.rsqrt(jnp.mean(value * value, axis=-1, keepdims=True) + EPS)


def angles(position):
    half = HEAD_DIM // 2
    freq = THETA ** (-(jnp.arange(half, dtype=jnp.float32) * 2.0) / HEAD_DIM)
    phase = position.astype(jnp.float32)[:, None] * freq[None, :]
    cosine, sine = (jnp.cos(phase), jnp.sin(phase))
    return (jnp.concatenate([cosine, cosine], axis=-1), jnp.concatenate([-sine, sine], axis=-1))


LINE = 4
VMEM = 62 * 1024 * 1024


def swap(value, axis, bit):
    count = lax.axis_size(axis)
    return lax.ppermute(value, axis, [(i, i ^ bit) for i in range(count)])


def gather_parts(value, axis, bit=None):
    parts, bit = ({0: value}, (bit or lax.axis_size(axis)) // 2)
    while bit >= 1:
        for j in list(parts):
            parts[j ^ bit] = swap(parts[j], axis, bit)
        bit //= 2
    return [parts[j] for j in range(len(parts))]


def gather_near(value, axis):
    return gather_parts(value, axis, lax.axis_size(axis) // 2)


def gather_far(value, axis, *deps):
    far = swap(value, axis, lax.axis_size(axis) // 2)
    return gather_near(fence(far, *deps) if deps else far, axis)


def scatter_even(parts, axis):
    parts, bit = ({2 * i: part for i, part in enumerate(parts)}, 2)
    while bit < lax.axis_size(axis) // 2:
        got = {j: swap(parts[j ^ bit], axis, bit) for j in parts if not j & bit}
        parts = {j: (parts[j].astype(jnp.float32) + got[j].astype(jnp.float32)).astype(jnp.bfloat16) for j in got}
        bit *= 2
    return parts[0]


def reduce_scatter(make, axis, *deps):
    members = lax.axis_size(axis)
    top = members // 2
    odd = {}
    for j in range(members - 1, 0, -2):
        part, mark = make(j, None, *deps)
        odd[j - 1], deps = (swap(part, axis, 1), (mark,))
    sums = {}
    for j in range(members - 2, top - 1, -2):
        sums[j], mark = make(j, odd[j], *deps)
        deps = (mark,)
    far = scatter_even([sums[j] for j in range(top, members, 2)], axis)
    deps = (far,)
    for j in range(top - 2, -1, -2):
        sums[j], mark = make(j, odd[j], *deps)
        deps = (mark,)
    return scatter_even([sums[j] for j in range(0, top, 2)], axis), swap(far, axis, top)


def fence_kernel(*refs):
    pass


def fence(value, *deps):
    return pl.pallas_call(
        fence_kernel,
        out_shape=jax.ShapeDtypeStruct(value.shape, value.dtype),
        in_specs=[pl.BlockSpec(memory_space=pl.ANY)] * (1 + len(deps)),
        out_specs=pl.BlockSpec(memory_space=pl.ANY),
        input_output_aliases={0: 0},
        name="fence",
    )(value, *deps)


def sum_relative(value, axis, local):
    count, bit = (lax.axis_size(axis), 1)
    while bit < count:
        got = swap(value, axis, bit)
        got = [got[..., (j ^ bit) * local : ((j ^ bit) + 1) * local] for j in range(count)]
        value = value + jnp.concatenate(got, axis=-1)
        bit *= 2
    return value


class LineSum:
    def __init__(self, parts, axis, length, stride):
        count = lax.axis_size(axis)
        place = lambda i: i // stride % length
        self.axis, self.length, self.at = (axis, length, place(lax.axis_index(axis)))
        self.up = [(i, i + stride) for i in range(count) if place(i) + 1 < length]
        self.down = [(i + stride, i) for i in range(count) if place(i) + 1 < length]
        self.total = [part.astype(jnp.float32) for part in parts]

    def ready(self, step):
        return [self.total[p].astype(jnp.bfloat16) for p in (self.length - step, step)]

    def send(self, step, ready=None):
        up, down = ready or self.ready(step)
        return lax.ppermute(up, self.axis, self.up), lax.ppermute(down, self.axis, self.down)

    def add(self, step, got):
        left = self.length - step - 1
        below, above = (value.astype(jnp.float32) for value in got)
        good = (self.at >= 1) & (self.at + left < self.length)
        self.total[left] = self.total[left] + jnp.where(good, below, 0.0)
        good = (self.at + 1 < self.length) & (self.at - left >= 0)
        high = (step + 1) % self.length
        self.total[high] = self.total[high] + jnp.where(good, above, 0.0)


def line_scatter(parts, axis, length, stride):
    line = LineSum(parts, axis, length, stride)
    for step in range(1, length):
        line.add(step, line.send(step))
    return line.total[0]


def direct_scatter(parts, axis, length, stride, *deps):
    count = lax.axis_size(axis)
    got = []
    for p in range(1, length):
        moves = [(i, i + ((i // stride % length + p) % length - i // stride % length) * stride) for i in range(count)]
        got.append(lax.ppermute(parts[p], axis, moves))
    total = (fence(parts[0], *deps) if deps else parts[0]).astype(jnp.float32)
    for value in got:
        total = total + value.astype(jnp.float32)
    return total


def by_place(chunks):
    inner = chunks.shape[0] // LINE
    index = lax.axis_index("grp")
    parts = []
    for q in range(inner):
        group = []
        for p in range(LINE):
            chunk = (index // inner + p) % LINE * inner + (index % inner + q) % inner
            group.append(lax.dynamic_index_in_dim(chunks, chunk, 0, keepdims=False))
        parts.append(jnp.stack(group))
    return parts


def sum_packs(parts, *deps):
    inner = len(parts)
    mine = direct_scatter(parts, "grp", inner, 1).astype(jnp.bfloat16) if inner > 1 else parts[0]
    return direct_scatter([mine[p] for p in range(LINE)], "grp", LINE, inner, *deps)


def widen_kernel(docs, line, sets_ref, kept_ref, got_ref, *refs):
    f32 = jnp.float32
    out_refs = refs[-line:]
    experts, rows = got_ref.shape[1:3]
    for p in range(line):
        out_refs[p][...] = kept_ref[p]
        for e in range(experts):
            for g in range(rows // (docs * RANK)):
                for d in range(docs):
                    there = pl.ds(pl.multiple_of(g * SETS * RANK + sets_ref[d] * RANK, RANK), RANK)
                    piece = got_ref[p, e, (g * docs + d) * RANK : (g * docs + d + 1) * RANK]
                    out_refs[p][e, there] = (out_refs[p][e, there].astype(f32) + piece.astype(f32)).astype(kept_ref.dtype)


def widen(docs, sets, kept, got, *deps):
    line = kept.shape[0]
    return pl.pallas_call(
        functools.partial(widen_kernel, docs, line),
        out_shape=(jax.ShapeDtypeStruct(kept.shape[1:], kept.dtype),) * line,
        in_specs=[full(SMEM), full(), full()] + [full(pl.ANY)] * len(deps),
        out_specs=(full(),) * line,
        compiler_params=params(),
        name="widen",
    )(sets, kept, got, *deps)


def sum_experts(docs, sets, parts, *deps):
    inner = len(parts)
    if inner == 2:
        return widen(docs, sets, parts[0], swap(parts[1], "grp", 1), *deps)
    mine = line_scatter(parts, "grp", inner, 1).astype(jnp.bfloat16) if inner > 1 else parts[0]
    return [mine[p] for p in range(LINE)]


def dot_nn(a, b):
    return jnp.dot(a, b, preferred_element_type=jnp.float32)


def dot_nt(a, b):
    return lax.dot_general(a, b, (((1,), (1,)), ((), ())), preferred_element_type=jnp.float32)


def dot_tn(a, b):
    return lax.dot_general(a, b, (((0,), (0,)), ((), ())), preferred_element_type=jnp.float32)


def column(row):
    return jnp.broadcast_to(row, (128, row.shape[1])).T


def as_row(value):
    return jnp.broadcast_to(value, (value.shape[0], 128)).T[:1]


def doc_sum(scal_ref, rows, docs, at):
    value = jnp.full(rows.shape, scal_ref[at], jnp.int32)
    for k in range(1, docs):
        value = jnp.where(rows >= scal_ref[k], scal_ref[at + k], value)
    return value


def block_marks(scal_ref, docs, block, local):
    rows = block * local + lax.broadcasted_iota(jnp.int32, (local, SETS * RANK), 0)
    lanes = lax.broadcasted_iota(jnp.int32, (local, SETS * RANK), 1) // RANK
    return (doc_sum(scal_ref, rows, docs, 1 + docs) == lanes).astype(jnp.float32)


def params(**kinds):
    return pltpu.CompilerParams(vmem_limit_bytes=VMEM, **kinds)


def cost(flops, moved, exps=0):
    return pl.CostEstimate(flops=int(flops) // 8, bytes_accessed=int(moved) // 8, transcendentals=int(exps) // 8)


def full(memory=pltpu.VMEM):
    return pl.BlockSpec(memory_space=memory)


SMEM = pltpu.SMEM


def project_kernel(docs, half, parts, scal_ref, *refs):
    f32, bf16 = (jnp.float32, jnp.bfloat16)
    x_refs, (gain_ref, w_ref, enter_ref, leave_ref) = (refs[:parts], refs[parts : parts + 4])
    normed_ref, low_ref, p_ref, v_ref, square_ref = refs[-5:]
    local = x_refs[0].shape[0]
    rank = SETS * RANK
    which = pl.program_id(0)

    @pl.when(which == 0)
    def _():
        enter = jnp.concatenate([enter_ref[i] for i in range(3)], axis=1)
        for b in range(parts):
            x = x_refs[b][...].astype(f32)
            here = slice(b * local, (b + 1) * local)
            normed_ref[here] = (x * rms_scale(x) * gain_ref[...].astype(f32)).astype(bf16)
            mark = block_marks(scal_ref, docs, scal_ref[0] ^ (half * parts + b), local)
            low = dot_nn(normed_ref[here], enter)
            for i in range(3):
                low_ref[i, here] = (low[:, i * rank : (i + 1) * rank] * mark).astype(bf16) * SCALE

    value = dot_nn(normed_ref[...], w_ref[0]) + dot_nn(low_ref[which], leave_ref[0])

    @pl.when(which < 2)
    def _():
        p_ref[0] = value
        square_ref[pl.ds(which, 1)] = as_row(jnp.sum(value * value, axis=1, keepdims=True))

    @pl.when(which == 2)
    def _():
        v_ref[...] = value.astype(bf16)


def project(docs, half, scal, x_parts, gain, weight, enter, leave, kept, *deps):
    parts = len(x_parts)
    local, width = x_parts[0].shape
    slice_width = weight.shape[2]
    rows, rank = (parts * local, enter.shape[2])
    f32, bf16 = (jnp.float32, jnp.bfloat16)
    outs = (
        jax.ShapeDtypeStruct((2 * rows, width), bf16),
        jax.ShapeDtypeStruct((3, 2 * rows, rank), bf16),
        jax.ShapeDtypeStruct((2, 2 * rows, slice_width), f32),
        jax.ShapeDtypeStruct((2 * rows, slice_width), bf16),
        jax.ShapeDtypeStruct((2, 2 * rows), f32),
    )
    extra = () if kept is None else kept
    first = 5 + parts
    return pl.pallas_call(
        functools.partial(project_kernel, docs, half, parts),
        grid=(3,),
        out_shape=outs,
        in_specs=[full(SMEM)]
        + [full()] * parts
        + [
            full(),
            pl.BlockSpec((1, width, slice_width), lambda i: (i, 0, 0)),
            full(),
            pl.BlockSpec((1, rank, slice_width), lambda i: (i, 0, 0)),
        ]
        + [full(pl.ANY)] * (len(extra) + len(deps)),
        out_specs=(
            pl.BlockSpec((rows, width), lambda i: (half, 0)),
            pl.BlockSpec((3, rows, rank), lambda i: (0, half, 0)),
            pl.BlockSpec((1, rows, slice_width), lambda i: (jnp.minimum(i, 1), half, 0)),
            pl.BlockSpec((rows, slice_width), lambda i: (half, 0)),
            pl.BlockSpec((2, rows), lambda i: (0, half)),
        ),
        input_output_aliases={first + i: i for i in range(len(extra))},
        compiler_params=params(),
        cost_estimate=cost(2 * rows * width * (3 * slice_width + 3 * rank), 14_000_000),
        name="project",
    )(scal, *x_parts, gain, weight, enter, leave, *extra, *deps)


def prepare_kernel(width, p_ref, square_ref, gains_ref, cos_ref, sin_ref, q_ref, k_ref):
    inverse = lax.rsqrt(square_ref[...] / width + EPS)
    for i, out_ref in ((0, q_ref), (1, k_ref)):
        scale = column(inverse[i : i + 1])
        for at in range(0, p_ref.shape[2], HEAD_DIM):
            cut = slice(at, at + HEAD_DIM)
            value = p_ref[i, :, cut] * scale * gains_ref[i : i + 1, cut]
            value = value * cos_ref[...] + pltpu.roll(value, HEAD_DIM // 2, 1) * sin_ref[...]
            out_ref[:, cut] = value.astype(jnp.bfloat16)


def prepare(width, p, squares, gains, cosine, sine, local, *deps):
    _, rows, slice_width = p.shape
    out = jax.ShapeDtypeStruct((rows, slice_width), jnp.bfloat16)
    return pl.pallas_call(
        lambda *refs: prepare_kernel(width, *refs[:5], *refs[5 + len(deps) :]),
        grid=(rows // local,),
        out_shape=(out, out),
        in_specs=[
            pl.BlockSpec((2, local, slice_width), lambda i: (0, i, 0)),
            pl.BlockSpec((2, local), lambda i: (0, i)),
            full(),
            pl.BlockSpec((local, HEAD_DIM), lambda i: (i, 0)),
            pl.BlockSpec((local, HEAD_DIM), lambda i: (i, 0)),
        ]
        + [full(pl.ANY)] * len(deps),
        out_specs=(pl.BlockSpec((local, slice_width), lambda i: (i, 0)),) * 2,
        compiler_params=params(),
        cost_estimate=cost(10 * p.size, 8 * p.size),
        name="prepare",
    )(p, squares, gains, cosine, sine, *deps)


def attend_kernel(docs, place, local, added, scal_ref, q_ref, k_ref, v_ref, w_ref, enter_ref, *refs):
    f32, bf16 = (jnp.float32, jnp.bfloat16)
    att_ref, part_ref, log_ref = refs[-3:]
    members = q_ref.shape[0] // local
    heads = q_ref.shape[1] // HEAD_DIM
    width = w_ref.shape[1]
    member = scal_ref[0]
    block = member ^ place
    queries = slice(place * local, (place + 1) * local)

    def run(last):
        rows = last * local + lax.broadcasted_iota(jnp.int32, (local, local), 0)
        begin = doc_sum(scal_ref, rows, docs, 1 + 2 * docs)
        lanes = lax.broadcasted_iota(jnp.int32, (local, local), 1)
        logs = jnp.zeros((8, local), f32)
        for h in range(heads):
            cut = slice(h * HEAD_DIM, (h + 1) * HEAD_DIM)
            query = q_ref[queries, cut]
            scores, values = ([], [])
            for b in range(last + 1):
                there = pl.ds(pl.multiple_of((member ^ b) * local, local), local)
                score = dot_nt(query, k_ref[there, cut]) * HEAD_DIM ** (-0.5)
                good = lanes + b * local >= begin
                if b == last:
                    good = good & (lanes + b * local <= rows)
                scores.append(jnp.where(good, score, NEG))
                values.append(v_ref[there, cut])
            peak = functools.reduce(jnp.maximum, [jnp.max(score, axis=1, keepdims=True) for score in scores])
            expo = [jnp.exp(score - peak) for score in scores]
            total = functools.reduce(jnp.add, [jnp.sum(e, axis=1, keepdims=True) for e in expo])
            share = 1.0 / total
            mixed = functools.reduce(jnp.add, [dot_nn((e * share).astype(bf16), v) for e, v in zip(expo, values)])
            att_ref[:, cut] = mixed.astype(bf16)
            head_row = lax.broadcasted_iota(jnp.int32, (8, local), 0) == h
            logs = jnp.where(head_row, as_row(peak + jnp.log(total)), logs)
        log_ref[...] = logs

    for last in range(members):
        pl.when(block == last)(functools.partial(run, last))
    for cut, value_ref in ((slice(0, width), w_ref), (slice(width, None), enter_ref)):
        value = dot_nn(att_ref[...], value_ref[...])
        if added:
            value = value + refs[0][:, cut].astype(f32)
        part_ref[:, cut] = value.astype(bf16)


def attend(docs, place, local, scal, q, k, v, weight, enter, addend, *deps):
    slice_width = q.shape[1]
    width, rank = (weight.shape[1], enter.shape[1])
    f32, bf16 = (jnp.float32, jnp.bfloat16)
    assert slice_width // HEAD_DIM <= 8
    return pl.pallas_call(
        functools.partial(attend_kernel, docs, place, local, addend is not None),
        out_shape=(
            jax.ShapeDtypeStruct((local, slice_width), bf16),
            jax.ShapeDtypeStruct((local, width + rank), bf16),
            jax.ShapeDtypeStruct((8, local), f32),
        ),
        in_specs=[full(SMEM)] + [full()] * (5 + (addend is not None)) + [full(pl.ANY)] * len(deps),
        out_specs=(full(),) * 3,
        compiler_params=params(),
        cost_estimate=cost(2_200_000_000, 4_000_000, 350_000),
        name="attend",
    )(scal, q, k, v, weight, enter, *(() if addend is None else (addend,)), *deps)


def middle_kernel(
    docs, scal_ref, x_ref, oa_ref, ob_ref, leave_ref, gain_ref, route_ref, route_enter, route_leave, h_ref, normed_ref, route_low, probs_ref
):
    f32, bf16 = (jnp.float32, jnp.bfloat16)
    width = x_ref.shape[1]
    mark = block_marks(scal_ref, docs, scal_ref[0], x_ref.shape[0])
    low = ((oa_ref[:, width:].astype(f32) + ob_ref[:, width:].astype(f32)) * mark).astype(bf16)
    normed_ref[:, width:] = low
    h = x_ref[...].astype(f32) + (oa_ref[:, :width].astype(f32) + ob_ref[:, :width].astype(f32))
    h = h + SCALE * dot_nn(low, leave_ref[...])
    h_ref[...] = h
    normed = (h * rms_scale(h) * gain_ref[...].astype(f32)).astype(bf16)
    normed_ref[:, :width] = normed
    low, probs = router(normed, mark, route_ref, route_enter, route_leave)
    route_low[...] = low
    probs_ref[...] = probs


def router(normed, mark, route_ref, route_enter, route_leave):
    low = (dot_nn(normed, route_enter[...]) * mark).astype(jnp.bfloat16)
    logits = dot_nt(route_ref[...], normed) + SCALE * dot_nt(route_leave[...], low)
    expo = jnp.exp(logits - jnp.max(logits, axis=0, keepdims=True))
    return low, expo / jnp.sum(expo, axis=0, keepdims=True)


def middle(docs, scal, x, outs, leave, gain, route, route_enter, route_leave, *deps):
    local, width = x.shape
    rank = leave.shape[0]
    f32, bf16 = (jnp.float32, jnp.bfloat16)
    return pl.pallas_call(
        lambda *refs: middle_kernel(docs, *refs[:9], *refs[9 + len(deps) :]),
        out_shape=(
            jax.ShapeDtypeStruct((local, width), f32),
            jax.ShapeDtypeStruct((local, width + rank), bf16),
            jax.ShapeDtypeStruct((local, rank), bf16),
            jax.ShapeDtypeStruct((route.shape[0], local), f32),
        ),
        in_specs=[full(SMEM)] + [full()] * 8 + [full(pl.ANY)] * len(deps),
        out_specs=(full(),) * 4,
        compiler_params=params(),
        cost_estimate=cost(4 * local * width * rank, 8_000_000),
        name="middle",
    )(scal, x, *outs, leave, gain, route, route_enter, route_leave, *deps)


def middle_back_kernel(
    docs, scal_ref, ga_ref, gb_ref, probs_ref, h_ref, up_ref, route_low, gain_ref, route_ref, route_enter, route_leave, dh_ref, dhb_ref, leave_ref
):
    f32, bf16 = (jnp.float32, jnp.bfloat16)
    width = h_ref.shape[1]
    mark = block_marks(scal_ref, docs, scal_ref[0], h_ref.shape[0])
    probs = probs_ref[...]
    experts = probs.shape[0]
    scores = (ga_ref[:, width:].astype(f32) + gb_ref[:, width:].astype(f32)).T
    dprobs = scores[:experts] + scores[experts : 2 * experts]
    dlogits = (probs * (dprobs - jnp.sum(probs * dprobs, axis=0, keepdims=True))).astype(bf16)
    dlow = (dot_tn(dlogits, route_leave[...]) * SCALE * mark).astype(bf16)
    dhb_ref[:, width:] = dlow
    leave_ref[...] = SCALE * dot_nn(dlogits, route_low[...])
    back = ga_ref[:, :width].astype(f32) + gb_ref[:, :width].astype(f32)
    back = back + dot_tn(dlogits, route_ref[...]) + dot_nt(dlow, route_enter[...])
    back = back * gain_ref[...].astype(f32)
    h = h_ref[...]
    scale = rms_scale(h)
    dh = up_ref[...].astype(f32) + scale * back - h * scale**3 * jnp.mean(h * back, axis=-1, keepdims=True)
    dh_ref[...] = dh
    dhb_ref[:, :width] = dh.astype(bf16)


def middle_back(docs, scal, grads, probs, h, upstream, route_low, gain, route, route_enter, route_leave):
    local, width = h.shape
    rank = route_enter.shape[1]
    f32, bf16 = (jnp.float32, jnp.bfloat16)
    return pl.pallas_call(
        functools.partial(middle_back_kernel, docs),
        out_shape=(
            jax.ShapeDtypeStruct((local, width), f32),
            jax.ShapeDtypeStruct((local, width + rank), bf16),
            jax.ShapeDtypeStruct((route.shape[0], rank), f32),
        ),
        in_specs=[full(SMEM)] + [full()] * 10,
        out_specs=(full(),) * 3,
        compiler_params=params(),
        cost_estimate=cost(4 * local * width * rank, 10_000_000),
        name="middle_back",
    )(scal, *grads, probs, h, upstream, route_low, gain, route, route_enter, route_leave)


def attend_back_kernel(docs, half, local, scal_ref, *refs):
    f32, bf16 = (jnp.float32, jnp.bfloat16)
    q_ref = refs[0]
    members = q_ref.shape[0] // local
    count = members // 2
    heads = q_ref.shape[1] // HEAD_DIM
    q_ref, k_ref, v_ref, w_ref, enter_ref, leave_ref = refs[:6]
    refs = refs[6:]
    grad_refs, att_refs, log_refs, normed_refs, refs = (*(refs[i * count : (i + 1) * count] for i in range(4)), refs[4 * count :])
    before, refs = (refs[: 5 * half], refs[5 * half + half :])
    dq_ref, dk_ref, dv_ref, enter_grad, leave_grad, route_grad, *rest = refs
    term_refs, (grad, datt, att, logs, normed) = (rest[:-5], rest[-5:])
    width = w_ref.shape[1]
    step = pl.program_id(0)
    place = half * count + step
    member = scal_ref[0]
    block = member ^ place
    queries = pl.ds(pl.multiple_of(place * local, local), local)
    mine = pl.ds(pl.multiple_of(member * q_ref.shape[1], 128), q_ref.shape[1])

    @pl.when(step == 0)
    def _():
        for i, ref in enumerate((dk_ref, dv_ref, enter_grad, leave_grad, route_grad)):
            ref[...] = before[i][...] if half else jnp.zeros_like(ref)

    for i in range(count):

        @pl.when(step == i)
        def _():
            grad[...] = grad_refs[i][...]
            att[...] = att_refs[i][...]
            logs[...] = log_refs[i][...]
            normed[:, : mine.size] = normed_refs[i][:, mine]
            normed[:, mine.size :] = normed_refs[i][:, width:]

    mark = block_marks(scal_ref, docs, block, local)
    low = (dot_nt(grad[:, :width], leave_ref[...]) * SCALE * mark).astype(bf16)
    datt[...] = (dot_nt(grad[:, :width], w_ref[...]) + dot_nt(low, enter_ref[...])).astype(bf16)
    enter_grad[...] += dot_tn(low, att[...])
    leave_grad[...] += SCALE * dot_tn(normed[:, mine.size :], grad[:, mine])
    route_grad[...] += dot_tn(grad[:, width:], normed[:, : mine.size])

    def run(last):
        rows = last * local + lax.broadcasted_iota(jnp.int32, (local, local), 1)
        begin = doc_sum(scal_ref, rows, docs, 1 + 2 * docs)
        down = lax.broadcasted_iota(jnp.int32, (local, local), 0)
        term = jnp.zeros((local, 1), f32)
        for h in range(heads):
            cut = slice(h * HEAD_DIM, (h + 1) * HEAD_DIM)
            query, dout = (q_ref[queries, cut], datt[:, cut])
            log = logs[h : h + 1]
            shares, pushes = ([], [])
            for b in range(last + 1):
                there = pl.ds(pl.multiple_of((member ^ b) * local, local), local)
                score = dot_nt(k_ref[there, cut], query) * HEAD_DIM ** (-0.5)
                good = down + b * local >= begin
                if b == last:
                    good = good & (down + b * local <= rows)
                share = jnp.where(good, jnp.exp(score - log), 0.0)
                shares.append(share)
                pushes.append(dot_nt(v_ref[there, cut], dout))
            inner = functools.reduce(jnp.add, [jnp.sum(s * d, axis=0, keepdims=True) for s, d in zip(shares, pushes)])
            dquery = jnp.zeros((local, HEAD_DIM), f32)
            for b in range(last + 1):
                there = pl.ds(pl.multiple_of((member ^ b) * local, local), local)
                dscore = (shares[b] * (pushes[b] - inner) * HEAD_DIM ** (-0.5)).astype(bf16)
                dquery = dquery + dot_tn(dscore, k_ref[there, cut])
                dk_ref[there, cut] += dot_nn(dscore, query)
                dv_ref[there, cut] += dot_nn(shares[b].astype(bf16), dout)
            dq_ref[:, cut] = dquery
            term = term + jnp.sum(dquery * query.astype(f32), axis=1, keepdims=True)
        term_refs[0][...] = as_row(term)

    for last in range(members):
        pl.when(block == last)(functools.partial(run, last))

    if half:

        @pl.when(step == count - 1)
        def _():
            for b in range(members):
                here = slice(b * local, (b + 1) * local)
                value = jnp.sum(dk_ref[here] * k_ref[here].astype(f32), axis=1, keepdims=True)
                term_refs[1][:, here] = as_row(value)


def attend_back(docs, half, scal, q, k, v, weight, enter, leave, grads, atts, logs, normed, before, *deps):
    group_len, slice_width = q.shape
    local = grads[0].shape[0]
    width, rank = (weight.shape[1], enter.shape[1])
    count = len(grads)
    f32, bf16 = (jnp.float32, jnp.bfloat16)
    low_grad = jax.ShapeDtypeStruct((rank, slice_width), f32)
    outs = (
        jax.ShapeDtypeStruct((count * local, slice_width), f32),
        jax.ShapeDtypeStruct((group_len, slice_width), f32),
        jax.ShapeDtypeStruct((group_len, slice_width), f32),
        low_grad,
        low_grad,
        low_grad,
        jax.ShapeDtypeStruct((1, count * local), f32),
    ) + ((jax.ShapeDtypeStruct((1, group_len), f32),) if half else ())
    return pl.pallas_call(
        functools.partial(attend_back_kernel, docs, half, local),
        grid=(count,),
        out_shape=outs,
        in_specs=[full(SMEM)] + [full()] * (6 + 4 * count + len(before)) + [full(pl.ANY)] * len(deps),
        out_specs=(pl.BlockSpec((local, slice_width), lambda i: (i, 0)),)
        + (full(),) * 5
        + (pl.BlockSpec((1, local), lambda i: (0, i)),)
        + ((full(),) if half else ()),
        scratch_shapes=[
            pltpu.VMEM((local, width + rank), bf16),
            pltpu.VMEM((local, slice_width), bf16),
            pltpu.VMEM((local, slice_width), bf16),
            pltpu.VMEM((8, local), f32),
            pltpu.VMEM((local, slice_width + rank), bf16),
        ],
        compiler_params=params(),
        cost_estimate=cost(8_000_000_000, 14_000_000, 700_000),
        name="attend_back",
    )(scal, q, k, v, weight, enter, leave, *grads, *atts, *logs, *normed, *before, *deps)


def project_back_kernel(docs, local, scal_ref, *refs):
    f32, bf16 = (jnp.float32, jnp.bfloat16)
    near_ref, far_ref, dk_ref, dv_ref, p_ref, square_ref, term_ref, gains_ref, cos_ref, sin_ref, normed_ref, low_ref = refs[:12]
    w_ref, enter_ref, leave_ref, route_ref, *refs = refs[12:]
    *dx_refs, enter_grad, leave_grad, dp_ref, dlow_ref, turned = refs
    rows, slice_width = near_ref.shape
    rank = SETS * RANK
    member = scal_ref[0]
    step = pl.program_id(0)
    members = pl.num_programs(0)
    width = slice_width * members
    count = rows // local

    @pl.when(step == 0)
    def _():
        inverse = lax.rsqrt(square_ref[...] / width + EPS)
        biases = inverse * inverse * term_ref[...] / width
        for i in range(2):
            for half in range(2):
                here = slice(half * rows, (half + 1) * rows)
                scale, bias = (column(inverse[i : i + 1, here]), column(biases[i : i + 1, here]))
                for at in range(0, slice_width, HEAD_DIM):
                    cut = slice(at, at + HEAD_DIM)
                    value = dk_ref[here, cut] if i else (far_ref if half else near_ref)[:, cut]
                    value = value * cos_ref[here] - pltpu.roll(value, HEAD_DIM // 2, 1) * sin_ref[here]
                    value = value * gains_ref[i : i + 1, cut] * scale - p_ref[i, here, cut] * bias
                    dp_ref[i, here, cut] = value.astype(bf16)
        dp_ref[2] = dv_ref[...].astype(bf16)
        for b in range(2 * count):
            here = slice(b * local, (b + 1) * local)
            mark = block_marks(scal_ref, docs, member ^ b, local)
            for i in range(3):
                value = dot_nt(dp_ref[i, here], leave_ref[i]) * SCALE * mark
                dlow_ref[here, i * rank : (i + 1) * rank] = value.astype(bf16)
                turned[i * rank : (i + 1) * rank, here] = value.T.astype(bf16)
        for i in range(3):
            leave_grad[i] = dot_tn(low_ref[i], dp_ref[i])

    enter_grad[0, : 3 * rank] = dot_nn(turned[...], normed_ref[...]).astype(bf16)
    enter_grad[0, 3 * rank :] = route_ref[0]
    spread_back(dx_refs, [dp_ref[i, rows:] for i in range(3)], dlow_ref[rows:], w_ref, enter_ref)


def spread_back(dx_refs, grads, low, w_ref, enter_ref):
    value = dot_nt(grads[0], w_ref[0]) + dot_nt(grads[1], w_ref[1]) + dot_nt(grads[2], w_ref[2])
    value = value + dot_nt(low, jnp.concatenate([enter_ref[i] for i in range(3)], axis=1))
    value = value.astype(jnp.bfloat16)
    local = dx_refs[0].shape[0]
    for b, dx_ref in enumerate(dx_refs):
        dx_ref[...] = value[b * local : (b + 1) * local]


def project_back(docs, local, scal, near, far, dk, dv, p, squares, terms, gains, cosine, sine, normed, low, weight, enter, leave, route_grad, *deps):
    rows, slice_width = near.shape
    width, rank = (normed.shape[1], enter.shape[2])
    members, count = (2 * rows // local, rows // local)
    tall = 3 * rank + route_grad.shape[1]
    f32, bf16 = (jnp.float32, jnp.bfloat16)
    pick = lambda i, scal: scal[0] ^ i
    sums = pl.BlockSpec((1, tall, slice_width), lambda i, scal: (i, 0, 0))
    in_specs = [full()] * 10 + [
        pl.BlockSpec((2 * rows, slice_width), lambda i, scal: (0, pick(i, scal))),
        full(),
        pl.BlockSpec((3, slice_width, slice_width), lambda i, scal: (0, pick(i, scal), 0)),
        pl.BlockSpec((3, slice_width, rank), lambda i, scal: (0, pick(i, scal), 0)),
        full(),
        pl.BlockSpec((1, tall - 3 * rank, slice_width), lambda i, scal: (i, 0, 0)),
    ] + [full(pl.ANY)] * len(deps)
    return pl.pallas_call(
        lambda *refs: project_back_kernel(docs, local, *refs[:17], *refs[17 + len(deps) :]),
        out_shape=(jax.ShapeDtypeStruct((local, width), bf16),) * count
        + (
            jax.ShapeDtypeStruct((members, tall, slice_width), bf16),
            jax.ShapeDtypeStruct((3, rank, slice_width), f32),
            jax.ShapeDtypeStruct((3, 2 * rows, slice_width), bf16),
            jax.ShapeDtypeStruct((2 * rows, 3 * rank), bf16),
        ),
        grid_spec=pltpu.PrefetchScalarGridSpec(
            num_scalar_prefetch=1,
            grid=(members,),
            in_specs=in_specs,
            out_specs=(pl.BlockSpec((local, slice_width), lambda i, scal: (0, pick(i, scal))),) * count
            + (sums, full(), full(), full()),
            scratch_shapes=[pltpu.VMEM((3 * rank, 2 * rows), bf16)],
        ),
        compiler_params=params(),
        cost_estimate=cost(2 * rows * (width * 3 * slice_width + 6 * rank * width), 20_000_000),
        name="project_back",
    )(scal, near, far, dk, dv, p, squares, terms, gains, cosine, sine, normed, low, weight, enter, leave, route_grad, *deps)


def project_near(local, grads, low, weight, enter, *deps):
    _, group_len, slice_width = grads.shape
    rows, width, rank = (group_len // 2, weight.shape[1], enter.shape[2])
    count = rows // local
    step = slice_width
    out = jax.ShapeDtypeStruct((local, width), jnp.bfloat16)

    def kernel(grads_ref, low_ref, w_ref, enter_ref, *refs):
        spread_back(refs[-count:], [grads_ref[i] for i in range(3)], low_ref[...], w_ref, enter_ref)

    return pl.pallas_call(
        kernel,
        grid=(width // step,),
        out_shape=(out,) * count,
        in_specs=[
            pl.BlockSpec((3, rows, slice_width), lambda i: (0, 0, 0)),
            pl.BlockSpec((rows, 3 * rank), lambda i: (0, 0)),
            pl.BlockSpec((3, step, slice_width), lambda i: (0, i, 0)),
            pl.BlockSpec((3, step, rank), lambda i: (0, i, 0)),
        ]
        + [full(pl.ANY)] * len(deps),
        out_specs=(pl.BlockSpec((local, step), lambda i: (0, i)),) * count,
        compiler_params=params(),
        cost_estimate=cost(2 * rows * (width * 3 * slice_width), 10_000_000),
        name="project_near",
    )(grads, low, weight, enter, *deps)


def finish_kernel(*refs):
    f32 = jnp.float32
    *parts, dh_ref, x_ref, gain_ref, out_ref = refs
    x = x_ref[...].astype(f32)
    back = functools.reduce(jnp.add, [part[...].astype(f32) for part in parts]) * gain_ref[...].astype(f32)
    scale = rms_scale(x)
    out = dh_ref[...] + scale * back - x * scale**3 * jnp.mean(x * back, axis=-1, keepdims=True)
    out_ref[...] = out.astype(out_ref.dtype)


def finish(grads, dh, x, gain):
    return pl.pallas_call(
        finish_kernel,
        out_shape=jax.ShapeDtypeStruct(x.shape, jnp.bfloat16),
        in_specs=[full()] * (3 + len(grads)),
        out_specs=full(),
        compiler_params=params(),
        cost_estimate=cost(10 * x.size, 12 * x.size),
        name="finish",
    )(*grads, dh, x, gain)


def upstream_kernel(scal_ref, named_ref, *refs):
    blocks = named_ref.shape[0]
    f32, bf16 = (jnp.float32, jnp.bfloat16)
    upstream_refs, (down_w, down_leave, rank_ref, rows_ref, back_ref, low_ref, places) = (refs[:blocks], refs[-7:])
    experts, local = places.shape[1:]
    cap = rows_ref.shape[1] // blocks

    @pl.when((pl.program_id(0) == 0) | (pl.num_programs(1) > 1))
    def _():
        earlier = lax.broadcasted_iota(jnp.int32, (local, local), 0) < lax.broadcasted_iota(jnp.int32, (local, local), 1)
        bits = lax.broadcasted_iota(jnp.int32, (experts, local), 0)
        for b in range(blocks):
            hot = (jnp.right_shift(named_ref[b], bits) & 1).astype(f32)
            rank = dot_nn(hot.astype(bf16), earlier.astype(f32).astype(bf16))
            places[b] = jnp.where(hot > 0.0, rank, -1.0)

    mine = pl.ds(scal_ref[0] * pl.num_programs(0) + pl.program_id(0), 1)
    slots = lax.broadcasted_iota(jnp.int32, (cap, local), 0).astype(f32)
    for b in range(blocks):
        rank_ref[0, b] = places[b, mine]
        pick = (places[b, mine] == slots).astype(bf16)
        rows_ref[0, b * cap : (b + 1) * cap] = dot_nn(pick, upstream_refs[b][...]).astype(bf16)
    back_ref[0] = dot_nt(rows_ref[0], down_w[0]).astype(bf16)
    low_ref[0] = dot_nt(rows_ref[0], down_leave[0])


def run_upstream(scal, named, upstream, down, down_leave, *deps):
    members, _, local = named.shape
    experts, ff, width = down.shape
    low = down_leave.shape[1]
    blocks = min(members, 4)
    turns = members // blocks
    count = blocks * CAP
    f32, bf16 = (jnp.float32, jnp.bfloat16)
    rows = lambda wide: pl.BlockSpec((1, count, wide), lambda e, r: (e, r, 0))
    return pl.pallas_call(
        lambda *refs: upstream_kernel(*refs[: 4 + blocks], *refs[4 + blocks + len(deps) :]),
        grid=(experts, turns),
        out_shape=(
            jax.ShapeDtypeStruct((experts, members, 1, local), f32),
            jax.ShapeDtypeStruct((experts, members * CAP, width), bf16),
            jax.ShapeDtypeStruct((experts, members * CAP, ff), bf16),
            jax.ShapeDtypeStruct((experts, members * CAP, low), f32),
        ),
        in_specs=[full(SMEM), pl.BlockSpec((blocks, 1, local), lambda e, r: (r, 0, 0))]
        + [pl.BlockSpec((local, width), lambda e, r: (r, 0), pipeline_mode=pl.Buffered(1))] * blocks
        + [pl.BlockSpec((1, ff, width), lambda e, r: (e, 0, 0)), pl.BlockSpec((1, low, width), lambda e, r: (e, 0, 0))]
        + [full(pl.ANY)] * len(deps),
        out_specs=(pl.BlockSpec((1, blocks, 1, local), lambda e, r: (e, r, 0, 0)), rows(width), rows(ff), rows(low)),
        scratch_shapes=[pltpu.VMEM((blocks, EXPERTS, local), f32)],
        compiler_params=params(),
        cost_estimate=cost(2 * experts * members * CAP * width * ff, 40_000_000),
        name="upstream",
    )(scal, named, *by_block(upstream, blocks), down, down_leave, *deps)


def by_block(parts, blocks):
    return [jnp.concatenate(parts[b::blocks]) if len(parts) > blocks else parts[b] for b in range(blocks)]


def dispatch(docs, scal_ref, place, rank_rows, weight_rows, normed_refs, rows_in, marks):
    local, low = (rank_rows[0].shape[1], marks.shape[1])
    cap = rows_in.shape[0] // len(rank_rows)
    slots = lax.broadcasted_iota(jnp.int32, (cap, local), 0).astype(jnp.float32)
    weights = []
    for b, rank_row in enumerate(rank_rows):
        hit = rank_row == slots
        pick = hit.astype(jnp.bfloat16)
        weights.append(jnp.sum(jnp.where(hit, weight_rows[b], 0.0), axis=1, keepdims=True))
        here = slice(b * cap, (b + 1) * cap)
        mark = block_marks(scal_ref, docs, scal_ref[0] ^ (place + b), local).astype(jnp.bfloat16)
        rows_in[here, :] = dot_nn(pick, normed_refs[b][:, : rows_in.shape[1]]).astype(jnp.bfloat16)
        marks[here, :] = dot_nn(pick, mark)
    return jnp.concatenate(weights, axis=0)


def inner_rows(
    first, rows_in, mark, weight, low_in, back_in, gate_w, up_w, gate_enter, gate_leave, up_enter, up_leave, down_enter, hidden, grad_gate, grad_up
):
    f32, bf16 = (jnp.float32, jnp.bfloat16)
    rank, ff = (mark.shape[1], hidden.shape[1])
    rows = rows_in[first:]
    low = dot_nn(rows, jnp.concatenate([gate_enter[0], up_enter[0]], axis=1))
    low_gate = (low[:, :rank] * mark).astype(bf16) * SCALE
    low_up = (low[:, rank:] * mark).astype(bf16) * SCALE
    grad_low_down = (low_in[...] * (SCALE * weight) * mark).astype(bf16)
    step = min(256, ff)
    for at in range(0, ff, step):
        cut = slice(at, at + step)
        gate = dot_nn(rows, gate_w[0, :, cut]) + dot_nn(low_gate, gate_leave[0, :, cut])
        up = dot_nn(rows, up_w[0, :, cut]) + dot_nn(low_up, up_leave[0, :, cut])
        back = back_in[:, cut].astype(f32) * weight + dot_nt(grad_low_down, down_enter[0, cut, :])
        sigma = 1.0 / (1.0 + jnp.exp(-gate))
        silu = gate * sigma
        hidden[first:, cut] = (silu * up).astype(bf16)
        grad_gate[first:, cut] = (back * up * sigma * (1.0 + gate * (1.0 - sigma))).astype(bf16)
        grad_up[first:, cut] = (back * silu).astype(bf16)
    return low_gate, low_up, grad_low_down


def near_kernel(docs, scal_ref, rank_ref, back_ref, low_ref, route_ref, route_enter, route_leave, *refs):
    count = len(refs) - 14
    normed_refs, refs = (refs[:count], refs[count:])
    weights, (hidden, grad_gate, grad_up, lows, rows_in, marks, probs) = (refs[:7], refs[7:])
    width = rows_in.shape[1]
    local = rank_ref.shape[3]

    @pl.when(pl.program_id(0) == 0)
    def _():
        for b in range(count):
            mark = block_marks(scal_ref, docs, scal_ref[0] ^ b, local)
            probs[b] = router(normed_refs[b][:, :width], mark, route_ref, route_enter, route_leave)[1]

    mine = pl.ds(scal_ref[0] * pl.num_programs(0) + pl.program_id(0), 1)
    rank_rows, weight_rows = ([rank_ref[0, b] for b in range(count)], [probs[b, mine] for b in range(count)])
    weight = dispatch(docs, scal_ref, 0, rank_rows, weight_rows, normed_refs, rows_in, marks)
    made = inner_rows(
        0, rows_in, marks[...], weight, low_ref.at[0], back_ref.at[0], *weights, hidden.at[0], grad_gate.at[0], grad_up.at[0]
    )
    lows[0] = jnp.concatenate(made, axis=1)


def run_near(docs, scal, ranks, back, low_back, route, route_enter, route_leave, normed, *weights):
    experts, members, _, local = ranks.shape
    ff, low = (back.shape[2], low_back.shape[2])
    width = normed[0].shape[1] - low
    rows = len(normed) * CAP
    bf16 = jnp.bfloat16
    near = lambda wide: pl.BlockSpec((1, rows, wide), lambda e: (e, 0, 0))
    hidden = jax.ShapeDtypeStruct((experts, rows, ff), bf16)
    return pl.pallas_call(
        functools.partial(near_kernel, docs),
        grid=(experts,),
        out_shape=(hidden, hidden, hidden, jax.ShapeDtypeStruct((experts, rows, 3 * low), bf16)),
        in_specs=[full(SMEM), pl.BlockSpec((1, members, 1, local), lambda e: (e, 0, 0, 0)), near(ff), near(low)]
        + [full()] * (3 + len(normed))
        + [pl.BlockSpec((1,) + value.shape[1:], lambda e: (e, 0, 0)) for value in weights],
        out_specs=(near(ff), near(ff), near(ff), near(3 * low)),
        scratch_shapes=[
            pltpu.VMEM((rows, width), bf16),
            pltpu.VMEM((rows, low), jnp.float32),
            pltpu.VMEM((len(normed), EXPERTS, local), jnp.float32),
        ],
        compiler_params=params(),
        cost_estimate=cost(4 * experts * rows * width * ff, 40_000_000),
        name="near",
    )(scal, ranks, back, low_back, route, route_enter, route_leave, *normed, *weights)


def expert_kernel(line, docs, made, scal_ref, rank_ref, grads_ref, back_ref, low_ref, route_ref, route_enter, route_leave, *refs):
    blocks = rank_ref.shape[1]
    ahead, refs = (refs[:made], refs[made:])
    normed_refs, refs, probs = (refs[:blocks], refs[blocks:-1], refs[-1])
    width = grads_ref.shape[2]
    turn = pl.program_id(1)
    local = rank_ref.shape[3]

    @pl.when((pl.program_id(0) == 0) | (pl.num_programs(1) > 1))
    def _():
        for b in range(blocks):
            mark = block_marks(scal_ref, docs, scal_ref[0] ^ (turn * blocks + b), local)
            probs[b] = router(normed_refs[b][:, :width], mark, route_ref, route_enter, route_leave)[1]

    mine = pl.ds(scal_ref[0] * pl.num_programs(0) + pl.program_id(0), 1)
    weights = [probs[b, mine] for b in range(blocks)]
    expert_rows(line, docs, ahead, scal_ref, rank_ref, weights, normed_refs, grads_ref.at[0], back_ref.at[0], low_ref.at[0], *refs)


def expert_rows(
    line,
    docs,
    ahead,
    scal_ref,
    rank_ref,
    weight_rows,
    normed_refs,
    grads_in,
    back_in,
    low_in,
    gate_w,
    up_w,
    down_w,
    gate_enter,
    gate_leave,
    up_enter,
    up_leave,
    down_enter,
    down_leave,
    place_ref,
    mixed_ref,
    grad_ref,
    score_ref,
    *rest,
):
    inner = len(rest) - 9
    sums, (rows_in, hidden, grad_gate, grad_up, marks, out_tile, back_tile, done, full_rows) = (rest[:inner], rest[inner:])
    f32, bf16 = (jnp.float32, jnp.bfloat16)
    blocks, local, width = (rank_ref.shape[1], rank_ref.shape[3], grads_in.shape[1])
    cap = mixed_ref.shape[2]
    expert, turn = (pl.program_id(0), pl.program_id(1))
    count = blocks * cap
    ff = hidden.shape[1]
    slots = lax.broadcasted_iota(jnp.int32, (cap, local), 0).astype(f32)
    rank_rows = [rank_ref[0, b] for b in range(blocks)]
    weight = dispatch(docs, scal_ref, turn * blocks, rank_rows, weight_rows, normed_refs, rows_in, marks)
    mark = marks[...]
    rank = mark.shape[1]
    first = ahead[0].shape[1] if ahead else 0
    lows = inner_rows(
        first, rows_in, mark[first:], weight[first:], low_in, back_in, gate_w, up_w, gate_enter, gate_leave, up_enter, up_leave, down_enter,
        hidden, grad_gate, grad_up
    )
    if ahead:
        for to, of in zip((hidden, grad_gate, grad_up), ahead):
            to[:first] = of[0]
        lows = [jnp.concatenate([ahead[3][0, :, i * rank : (i + 1) * rank], value], axis=0) for i, value in enumerate(lows)]
    low_gate, low_up, grad_low_down = lows
    low_down = (dot_nn(hidden[...], down_enter[0]) * mark).astype(bf16) * SCALE
    grad_low_gate = (dot_nt(grad_gate[...], gate_leave[0]) * SCALE * mark).astype(bf16)
    grad_low_up = (dot_nt(grad_up[...], up_leave[0]) * SCALE * mark).astype(bf16)
    grad_low = jnp.concatenate([grad_low_gate, grad_low_up], axis=1)
    step = out_tile.shape[3]
    sent = []

    def send(slot, cut):
        there = pl.ds(turn * blocks, blocks)
        copies = [
            pltpu.make_async_copy(out_tile.at[slot], mixed_ref.at[there, expert, :, cut], done.at[0, slot]),
            pltpu.make_async_copy(back_tile.at[slot], grad_ref.at[there, expert, :, cut], done.at[1, slot]),
        ]
        for copy in copies:
            copy.start()
        sent.append(copies)

    score = jnp.zeros((count, 1), f32)
    for at in range(0, width, step):
        cut = slice(at, at + step)
        out = dot_nn(hidden[...], down_w[0, :, cut]) + dot_nn(low_down, down_leave[0, :, cut])
        score = score + jnp.sum(out * grads_in[:, cut].astype(f32), axis=1, keepdims=True)
        back = dot_nt(grad_gate[...], gate_w[0, cut, :]) + dot_nt(grad_up[...], up_w[0, cut, :])
        back = back + dot_nt(grad_low, jnp.concatenate([gate_enter[0, cut, :], up_enter[0, cut, :]], axis=1))
        out = (out * weight).astype(bf16)
        back = back.astype(bf16)
        slot = len(sent) % 2
        if len(sent) >= 2:
            for copy in sent[-2]:
                copy.wait()
        for b in range(blocks):
            out_tile[slot, b] = out[b * cap : (b + 1) * cap]
            back_tile[slot, b] = back[b * cap : (b + 1) * cap]
        send(slot, pl.ds(at, step))
    for b in range(blocks):
        hit = rank_ref[0, b] == slots
        score_ref[0, b] = jnp.sum(jnp.where(hit, score[b * cap : (b + 1) * cap], 0.0), axis=0, keepdims=True)

    def keep(value, row, ref_at):
        piece = value.shape[1] // (line * inner)
        value = value.astype(bf16)
        full_rows[: value.shape[0], : value.shape[1]] = value
        columns = slice(ref_at, ref_at + piece)
        for c in range(line * inner):
            part = slice(c * piece, (c + 1) * piece)
            for q in range(inner):

                @pl.when(place_ref[1, c] == q)
                def _():
                    for at in range(0, value.shape[0], rank):
                        if inner != 2 or q == 0:
                            source = full_rows[at : at + rank, part]
                            target = sums[q].at[place_ref[0, c], 0, slice(row + at, row + at + rank), columns]
                            if pl.num_programs(1) > 1:
                                old = jnp.where(turn > 0, target[...].astype(f32), 0.0)
                                source = (old + source.astype(f32)).astype(bf16)
                            target[...] = source
                            continue
                        for d in range(docs):
                            there = pl.ds(pl.multiple_of(at + scal_ref[1 + docs + d] * RANK, RANK), RANK)
                            source = full_rows[there, part]
                            for d2 in range(d):
                                repeated = scal_ref[1 + docs + d2] == scal_ref[1 + docs + d]
                                source = jnp.where(repeated, jnp.zeros_like(source), source)
                            to = ((row + at) // rank * docs + d) * RANK
                            target = sums[q].at[place_ref[0, c], 0, slice(to, to + RANK), columns]
                            if pl.num_programs(1) > 1:
                                old = jnp.where(turn > 0, target[...].astype(f32), 0.0)
                                source = (old + source.astype(f32)).astype(bf16)
                            target[...] = source

    wide = width // (line * inner)
    keep(dot_tn(grad_low, rows_in[...]), 0, 0)
    keep(dot_tn((low_down.astype(f32) * weight).astype(bf16), grads_in[...]), 2 * rank, 0)
    keep(dot_tn(low_gate, grad_gate[...]), 0, wide)
    keep(dot_tn(low_up, grad_up[...]), rank, wide)
    keep(dot_tn(grad_low_down, hidden[...]), 2 * rank, wide)
    for copies in sent[-2:]:
        for copy in copies:
            copy.wait()


def run_experts(docs, scal, ranks, grads, back, low_back, route, route_enter, route_leave, ahead, normed, place, inner, *weights):
    experts, members, _, local = ranks.shape
    width = grads.shape[2]
    ff = back.shape[2]
    low = SETS * RANK
    blocks = min(members, 4)
    turns = members // blocks
    packs = place.shape[1]
    line = packs // inner
    bf16 = jnp.bfloat16
    count = blocks * CAP
    tile = min(512, width)
    by_turn = lambda e, r: (e, r, 0, 0)
    rows = lambda wide: pl.BlockSpec((1, count, wide), lambda e, r: (e, r, 0))
    half = count // 2
    back_rows = lambda wide: pl.BlockSpec((1, half, wide), lambda e, r: (e, 1, 0)) if ahead else rows(wide)
    once = lambda wide: [pl.BlockSpec((local, wide), lambda e, r: (r, 0), pipeline_mode=pl.Buffered(1))] * blocks
    per_expert = lambda value: pl.BlockSpec((1,) + value.shape[1:], lambda e, r: (e, 0, 0))
    packed = docs * RANK if inner == 2 else low
    sums = [jax.ShapeDtypeStruct((line, experts, 3 * (packed if q else low), (width + ff) // packs), bf16) for q in range(inner)]
    rows_out = jax.ShapeDtypeStruct((members, experts, CAP, width), bf16)
    return pl.pallas_call(
        functools.partial(expert_kernel, line, docs, len(ahead)),
        grid=(experts, turns),
        out_shape=(rows_out, rows_out, jax.ShapeDtypeStruct(ranks.shape, jnp.float32), *sums),
        in_specs=[full(SMEM), pl.BlockSpec((1, blocks, 1, local), by_turn), rows(width), back_rows(ff), back_rows(low)]
        + [full()] * 3
        + [pl.BlockSpec((1,) + value.shape[1:], lambda e, r: (e, 0, 0)) for value in ahead]
        + once(width + low)
        + [per_expert(value) for value in weights]
        + [full(SMEM)],
        out_specs=(full(pl.ANY), full(pl.ANY), pl.BlockSpec((1, blocks, 1, local), by_turn))
        + tuple(pl.BlockSpec((line, 1) + value.shape[2:], lambda e, r: (0, e, 0, 0)) for value in sums),
        scratch_shapes=[
            pltpu.VMEM((count, width), bf16),
            pltpu.VMEM((count, ff), bf16),
            pltpu.VMEM((count, ff), bf16),
            pltpu.VMEM((count, ff), bf16),
            pltpu.VMEM((count, low), jnp.float32),
            pltpu.VMEM((2, blocks, CAP, tile), bf16),
            pltpu.VMEM((2, blocks, CAP, tile), bf16),
            pltpu.SemaphoreType.DMA((2, 2)),
            pltpu.VMEM((2 * low, width), bf16),
            pltpu.VMEM((blocks, EXPERTS, local), jnp.float32),
        ],
        compiler_params=params(),
        cost_estimate=cost(2 * experts * members * CAP * (width * ff * 5 + 9 * low * (width + ff)), 60_000_000),
        name="experts",
    )(scal, ranks, grads, back, low_back, route, route_enter, route_leave, *ahead, *by_block(normed, blocks), *weights, place)


def mix(rank_ref, rows_ref, pick_ref, step):
    experts, cap, local = (rows_ref.shape[1], rows_ref.shape[2], rank_ref.shape[3])

    @pl.when(step == 0)
    def _():
        slots = lax.broadcasted_iota(jnp.int32, (cap, local), 0).astype(jnp.float32)
        pick = jnp.concatenate([(rank_ref[e, 0] == slots).astype(jnp.float32) for e in range(experts)], axis=0)
        pick_ref[...] = pick.T.astype(jnp.bfloat16)

    rows = jnp.concatenate([rows_ref[0, e] for e in range(experts)], axis=0)
    return dot_nn(pick_ref[...], rows)


def mix_grads(scal_ref, rank_ref, score_ref, rows_ref, added_ref, back_ref, pick_ref, step):
    f32, bf16 = (jnp.float32, jnp.bfloat16)
    experts, local = (rows_ref.shape[1], rank_ref.shape[3])
    piece, low = (rows_ref.shape[3], SETS * RANK)
    width = back_ref.shape[1] - low
    columns = pl.ds(pl.multiple_of(step * piece, 128), piece)
    value = mix(rank_ref, rows_ref, pick_ref, step)
    if added_ref is not None:
        value = value + added_ref[:, columns].astype(f32)
    back_ref[:, columns] = value.astype(bf16)

    @pl.when(step == 0)
    def _():
        lines = lax.broadcasted_iota(jnp.int32, (low, local), 0)
        table = jnp.zeros((low, local), f32)
        for e in range(experts):
            score = score_ref[e, 0]
            whole = score.astype(bf16).astype(f32)
            at = scal_ref[0] * experts + e
            table = jnp.where(lines == at, whole, table)
            table = jnp.where(lines == at + EXPERTS, score - whole, table)
        table = table.T
        if added_ref is not None:
            table = table + added_ref[:, width:].astype(f32)
        back_ref[:, width:] = table.astype(bf16)


def combine_kernel(added, scal_ref, rank_ref, score_ref, rows_ref, *refs):
    back_ref, pick_ref = refs[-2:]
    mix_grads(scal_ref, rank_ref, score_ref, rows_ref, refs[0] if added else None, back_ref, pick_ref, pl.program_id(0))


def combine(scal, ranks, scores, rows, place, addend, *deps):
    experts, members, _, local = ranks.shape
    width = rows.shape[3]
    piece = width // 2
    low = SETS * RANK
    one = pl.BlockSpec((experts, 1, 1, local), lambda n: (0, place, 0, 0))
    more = () if addend is None else (addend,)
    return pl.pallas_call(
        functools.partial(combine_kernel, addend is not None),
        grid=(2,),
        out_shape=jax.ShapeDtypeStruct((local, width + low), jnp.bfloat16),
        in_specs=[full(SMEM), one, one, pl.BlockSpec((1, experts, CAP, piece), lambda n: (place, 0, 0, n))]
        + [full()] * len(more)
        + [full(pl.ANY)] * len(deps),
        out_specs=full(),
        scratch_shapes=[pltpu.VMEM((local, experts * CAP), jnp.bfloat16)],
        compiler_params=params(),
        cost_estimate=cost(2 * local * experts * CAP * width, 2 * experts * CAP * width),
        name="combine",
    )(scal, ranks, scores, rows, *more, *deps)


def combine_last_kernel(scal_ref, rank_ref, score_ref, grads_ref, rows_ref, added_ref, *refs):
    members = pl.num_programs(0)
    out_refs, (back_ref, pick_ref) = (refs[-2 - members : -2], refs[-2:])
    block, step = (pl.program_id(0), pl.program_id(1))
    piece = rows_ref.shape[3]
    columns = pl.ds(pl.multiple_of(step * piece, 128), piece)
    value = mix(rank_ref, rows_ref, pick_ref, step).astype(jnp.bfloat16)
    for b in range(members):

        @pl.when(block == b)
        def _():
            out_refs[b][:, columns] = value

    @pl.when(block == 0)
    def _():
        mix_grads(scal_ref, rank_ref, score_ref, grads_ref, added_ref, back_ref, pick_ref, step)


def combine_last(scal, ranks, scores, grads, mixed, addend, *deps):
    experts, members, _, local = ranks.shape
    width = grads.shape[3]
    piece = width // 2
    low = SETS * RANK
    out = jax.ShapeDtypeStruct((local, width), jnp.bfloat16)
    one = pl.BlockSpec((experts, 1, 1, local), lambda b, n: (0, b, 0, 0))
    first = lambda b, n: (0, 0, 0, jnp.where(b == 0, n, 1))
    return pl.pallas_call(
        lambda *refs: combine_last_kernel(*refs[:6], *refs[6 + len(deps) :]),
        grid=(members, 2),
        out_shape=(out,) * members + (jax.ShapeDtypeStruct((local, width + low), jnp.bfloat16),),
        in_specs=[full(SMEM), one, one]
        + [pl.BlockSpec((1, experts, CAP, piece), first), pl.BlockSpec((1, experts, CAP, piece), lambda b, n: (b, 0, 0, n))]
        + [full()]
        + [full(pl.ANY)] * len(deps),
        out_specs=(full(),) * (members + 1),
        scratch_shapes=[pltpu.VMEM((local, experts * CAP), jnp.bfloat16)],
        compiler_params=params(),
        cost_estimate=cost(2 * 5 * local * experts * CAP * width, 10 * experts * CAP * width),
        name="combine_last",
    )(scal, ranks, scores, grads, mixed, addend, *deps)


def per_device(
    tokens,
    cotangent,
    pack_order,
    doc_lengths,
    doc_sets,
    routes,
    attention_gain,
    query_gain,
    key_gain,
    feed_gain,
    qkv_weight,
    out_weight,
    router_weight,
    gate_weight,
    up_weight,
    down_weight,
    qkv_enter,
    qkv_leave,
    out_enter,
    out_leave,
    router_enter,
    router_leave,
    gate_enter,
    gate_leave,
    up_enter,
    up_leave,
    down_enter,
    down_leave,
):
    members = lax.axis_size("ep")
    packs = lax.axis_size("grp")
    pack = lax.axis_index("grp")
    member = lax.axis_index("ep")
    local, width = tokens.shape
    slice_width = width // members
    experts_here = gate_weight.shape[0]
    own_cols = member * slice_width
    count = members // 2
    low = SETS * RANK
    f32, bf16 = (jnp.float32, jnp.bfloat16)
    slot = jnp.sum(jnp.where(pack_order == pack, jnp.arange(packs, dtype=jnp.int32), 0))
    named = jnp.sum(jnp.left_shift(jnp.int32(1), routes), axis=1)
    documents_here = jnp.concatenate([doc_lengths[0], doc_sets[0]])
    info = jnp.concatenate([named, jnp.pad(documents_here, (0, 128 - documents_here.shape[0]))])
    info = jnp.stack(gather_parts(info, "grp"))
    other = jnp.sum(jnp.where(pack_order == pack ^ 1, jnp.arange(packs, dtype=jnp.int32), 0))
    other = lax.dynamic_index_in_dim(info, other ^ pack, 0, keepdims=False)
    info = lax.dynamic_index_in_dim(info, slot ^ pack, 0, keepdims=False)
    blocks = [member ^ j for j in range(members)]
    named = info[:local]
    docs = doc_lengths.shape[1]
    lengths, sets = (info[local : local + docs], info[local + docs : local + 2 * docs])
    ends = jnp.cumsum(lengths)
    starts = ends - lengths
    scal = jnp.concatenate([member[None].astype(jnp.int32), ends, sets, starts])
    gain_one, gain_two = (attention_gain[None], feed_gain[None])
    route, route_leave = (router_weight.T, router_leave.T)
    adapters = (gain_one, qkv_weight, qkv_enter, qkv_leave)
    named_all = named.reshape(1, 1, local)
    named_all = jnp.concatenate([named_all, swap(named_all, "ep", 1)])
    kept = project(docs, 0, scal, gather_near(tokens, "ep"), *adapters, None, named_all)
    token_parts = gather_far(tokens, "ep", kept[4])
    bit = 2
    while bit < members:
        named_all = jnp.concatenate([named_all, swap(named_all, "ep", bit)])
        bit *= 2
    kept = project(docs, 1, scal, token_parts, *adapters, kept)
    normed_all, low_all, projected, values, squares = kept
    late = fence(scal, values)
    ends, starts = (late[1 : 1 + docs], late[1 + 2 * docs :])
    rows = (jnp.stack(blocks)[:, None] * local + jnp.arange(local, dtype=jnp.int32)[None, :]).reshape(-1)
    begin = starts[0]
    for k in range(1, docs):
        begin = jnp.where(rows >= ends[k - 1], starts[k], begin)
    cosine, sine = angles(rows - begin)
    upstream_far = gather_near(swap(fence(cotangent, token_parts[0], named_all), "ep", members // 2), "ep")
    upstream_parts = gather_near(cotangent, "ep") + upstream_far
    squares = sum_relative(squares, "ep", local)
    own_gain = lambda gain: lax.dynamic_slice_in_dim(gain, own_cols, slice_width, 0)
    gains = jnp.stack([own_gain(query_gain), own_gain(key_gain)]).astype(f32)
    queries, keys = prepare(width, projected, squares, gains, cosine, sine, local, upstream_parts[-1], named_all)
    heads = [None] * members

    def attend_place(place, addend, *deps):
        heads[place] = attend(docs, place, local, scal, queries, keys, values, out_weight, out_enter, addend, *deps)
        return heads[place][1], heads[place][2]

    top = members // 2
    outs = reduce_scatter(attend_place, "ep")
    upstream_rows = run_upstream(scal, named_all, upstream_parts, down_weight, down_leave, heads[0][2])
    hidden_state, normed_two, low_router, probs = middle(
        docs, scal, tokens, outs, out_leave, gain_two, route, router_enter, route_leave, upstream_rows[0]
    )

    ranks, _, *backs = upstream_rows
    routers = (route, router_enter, route_leave)
    normed_two_parts = gather_near(normed_two, "ep")
    ahead = ()
    if members <= 4:
        ahead = run_near(
            docs, scal, ranks, *backs, *routers, normed_two_parts, gate_weight, up_weight, gate_enter, gate_leave, up_enter, up_leave,
            down_enter
        )
    normed_two_parts = normed_two_parts + gather_far(normed_two, "ep", *ahead[3:])
    inner = packs // LINE
    chunk_ids = jnp.arange(packs, dtype=jnp.int32)
    place = jnp.stack([(chunk_ids // inner - pack // inner) % LINE, (chunk_ids % inner - pack % inner) % inner])
    mixed_rows, grad_rows, scores, *expert_sums = run_experts(
        docs,
        scal,
        *upstream_rows,
        *routers,
        ahead,
        normed_two_parts,
        place,
        inner,
        gate_weight,
        up_weight,
        down_weight,
        gate_enter,
        gate_leave,
        up_enter,
        up_leave,
        down_enter,
        down_leave,
    )
    mixed = []

    def combine_place(place, addend, *deps):
        if place:
            part = combine(scal, ranks, scores, grad_rows, place, addend, *deps)
        else:
            *parts, part = combine_last(scal, ranks, scores, grad_rows, mixed_rows, addend, *deps)
            mixed.extend(parts)
        return part, part

    grads = reduce_scatter(combine_place, "ep")
    grad_hidden, grad_branch, grad_router_leave = middle_back(
        docs, scal, grads, probs, hidden_state, cotangent, low_router, gain_two, route, router_enter, route_leave
    )
    pair = lambda a, b: (a.astype(f32) + b.astype(f32)).astype(bf16)
    mixed = [pair(mixed[j], swap(mixed[j + 1], "ep", 1)) for j in range(0, members, 2)]
    mixed_near, mixed_far = (scatter_even(mixed[: top // 2], "ep"), scatter_even(mixed[top // 2 :], "ep"))

    inside = (queries, keys, values, out_weight, out_enter, out_leave)

    def attend_half_back(half, branch, before, *deps):
        part = slice(half * count, (half + 1) * count)
        atts, logs = ([head[i] for head in heads[part]] for i in (0, 2))
        return attend_back(docs, half, scal, *inside, branch, atts, logs, normed_two_parts[part], before, *deps)

    near = attend_half_back(0, gather_near(grad_branch, "ep"), ())
    branch_far = gather_far(grad_branch, "ep", near[6])
    other_sets = other[local + docs : local + 2 * docs]
    line_sums = sum_experts(docs, other_sets, expert_sums, near[6])
    far = attend_half_back(1, branch_far, near[1:6], line_sums[0])
    mixed_got = swap(fence(mixed_far, branch_far[0]), "ep", top)
    grad_keys, grad_values, *low_grads = far[1:6]
    terms = jnp.concatenate([jnp.concatenate([near[6], far[6]], axis=1), far[7]])
    line = LineSum(line_sums, "grp", LINE, inner)
    got = line.send(1)
    terms = sum_relative(fence(terms, *got, mixed_got), "ep", local)
    line.add(1, got)
    leave_rows = low // members
    leave_parts = jnp.stack([lax.dynamic_slice_in_dim(grad_router_leave, b * leave_rows, leave_rows, 1) for b in blocks])
    leave_parts = jnp.pad(leave_parts.astype(bf16), ((0, 0), (0, 0), (0, slice_width - leave_rows)))
    shared = (projected, squares, terms, gains, cosine, sine, normed_all, low_all, qkv_weight, qkv_enter, qkv_leave)
    ready = line.ready(2)
    *far_parts, enter_sums, leave_sums, projected_grads, low_grad = project_back(
        docs, local, scal, near[0], far[0], grad_keys, grad_values, *shared, leave_parts, *ready
    )
    got = line.send(2, ready)
    line.add(2, got)
    *far_parts, enter_sums, leave_sums = (fence(value, *got) for value in (*far_parts, enter_sums, leave_sums))
    input_far = scatter_even([pair(far_parts[j], swap(far_parts[j + 1], "ep", 1)) for j in range(0, count, 2)], "ep")
    near_parts = project_near(local, projected_grads, low_grad, qkv_weight, qkv_enter, input_far)
    input_got = swap(input_far, "ep", top)
    if count == 2:
        inputs = (near_parts[0], swap(near_parts[1], "ep", 1), input_got)
    else:
        inputs = [pair(near_parts[j], swap(near_parts[j + 1], "ep", 1)) for j in range(0, count, 2)]
        inputs = (scatter_even(inputs, "ep"), input_got)
    grad_input = finish(inputs, grad_hidden, tokens, gain_one)
    layer_out = (hidden_state + (mixed_near.astype(f32) + mixed_got.astype(f32))).astype(bf16)

    got = [fence(value, input_got) for value in line.send(3)]
    line.add(3, got)
    expert_sum = line.total[0]
    by_rows = lambda value: value.astype(bf16).reshape(-1, packs, value.shape[-2] // packs, slice_width).transpose(1, 0, 2, 3)
    joined = jnp.concatenate([by_rows(value) for value in (*low_grads, leave_sums)], axis=1)
    joined = sum_packs(by_place(fence(joined, input_far)), input_got)
    enter_sums = fence(enter_sums, input_far)
    enter_sums = [pair(enter_sums[j], swap(enter_sums[j + 1], "ep", 1)) for j in range(0, members, 2)]
    enter_far = swap(scatter_even(enter_sums[top // 2 :], "ep"), "ep", top)
    enter_sum = fence(pair(scatter_even(enter_sums[: top // 2], "ep"), enter_far), input_got, *got, joined)
    enter_chunks = by_rows(enter_sum[: 3 * low].reshape(3, low, slice_width)).reshape(packs, -1, slice_width)
    leave_chunks = by_rows(enter_sum[3 * low :]).reshape(packs, -1, slice_width)
    enter_sum = sum_packs(by_place(jnp.concatenate([enter_chunks, leave_chunks], axis=1)))
    enter_rows = 3 * low // packs
    wide = width // packs
    turn = lambda value: jnp.swapaxes(value, -1, -2)
    return (
        layer_out,
        grad_input,
        turn(enter_sum[:enter_rows].reshape(3, -1, slice_width)),
        joined[3:],
        turn(joined[0]),
        joined[1],
        turn(joined[2]),
        turn(enter_sum[enter_rows:, :leave_rows]),
        turn(expert_sum[:, :low, :wide]),
        expert_sum[:, :low, wide:],
        turn(expert_sum[:, low : 2 * low, :wide]),
        expert_sum[:, low : 2 * low, wide:],
        turn(expert_sum[:, 2 * low :, wide:]),
        expert_sum[:, 2 * low :, :wide],
    )


def solution(mesh):
    in_specs = (
        P(("grp", "ep"), None),
        P(("grp", "ep"), None),
        P(),
        P("grp", None),
        P("grp", None),
        P(("grp", "ep"), None),
        P(),
        P(),
        P(),
        P(),
        P(None, None, "ep"),
        P("ep", None),
        P(),
        P("ep", None, None),
        P("ep", None, None),
        P("ep", None, None),
        P(),
        P(None, None, "ep"),
        P("ep", None),
        P(),
        P(),
        P(),
        P("ep", None, None),
        P("ep", None, None),
        P("ep", None, None),
        P("ep", None, None),
        P("ep", None, None),
        P("ep", None, None),
    )
    out_specs = (
        P(("grp", "ep"), None),
        P(("grp", "ep"), None),
        P(None, "ep", "grp"),
        P(None, "grp", "ep"),
        P("ep", "grp"),
        P("grp", "ep"),
        P("ep", "grp"),
        P("ep", "grp"),
        P("ep", "grp", None),
        P("ep", None, "grp"),
        P("ep", "grp", None),
        P("ep", None, "grp"),
        P("ep", "grp", None),
        P("ep", None, "grp"),
    )
    return jax.shard_map(
        per_device, mesh=mesh, in_specs=in_specs, out_specs=out_specs, check_vma=False
    )
```

```python
import functools

import jax
import jax.numpy as jnp
from jax import lax
from jax.experimental import pallas as pl
from jax.experimental.pallas import tpu as pltpu
from jax.sharding import PartitionSpec as P

HEAD_DIM = 128
EXPERTS = 16
TOP = 8
SETS = 8
RANK = 16
CAP = 144


EPS = 1e-05
SCALE = 2.0
THETA = 10000.0
NEG = -1e30


def rms_scale(value):
    return lax.rsqrt(jnp.mean(value * value, axis=-1, keepdims=True) + EPS)


def angles(position):
    half = HEAD_DIM // 2
    freq = THETA ** (-(jnp.arange(half, dtype=jnp.float32) * 2.0) / HEAD_DIM)
    phase = position.astype(jnp.float32)[:, None] * freq[None, :]
    cosine, sine = (jnp.cos(phase), jnp.sin(phase))
    return (jnp.concatenate([cosine, cosine], axis=-1), jnp.concatenate([-sine, sine], axis=-1))


LINE = 4
VMEM = 62 * 1024 * 1024


def swap(value, axis, bit):
    count = lax.axis_size(axis)
    return lax.ppermute(value, axis, [(i, i ^ bit) for i in range(count)])


def gather_parts(value, axis, bit=None):
    parts, bit = ({0: value}, (bit or lax.axis_size(axis)) // 2)
    while bit >= 1:
        for j in list(parts):
            parts[j ^ bit] = swap(parts[j], axis, bit)
        bit //= 2
    return [parts[j] for j in range(len(parts))]


def gather_near(value, axis):
    return gather_parts(value, axis, lax.axis_size(axis) // 2)


def gather_far(value, axis, *deps):
    far = swap(value, axis, lax.axis_size(axis) // 2)
    return gather_near(fence(far, *deps) if deps else far, axis)


def scatter_even(parts, axis):
    parts, bit = ({2 * i: part for i, part in enumerate(parts)}, 2)
    while bit < lax.axis_size(axis) // 2:
        got = {j: swap(parts[j ^ bit], axis, bit) for j in parts if not j & bit}
        parts = {j: (parts[j].astype(jnp.float32) + got[j].astype(jnp.float32)).astype(jnp.bfloat16) for j in got}
        bit *= 2
    return parts[0]


def reduce_scatter(make, axis, *deps):
    members = lax.axis_size(axis)
    top = members // 2
    odd = {}
    for j in range(members - 1, 0, -2):
        part, mark = make(j, None, *deps)
        odd[j - 1], deps = (swap(part, axis, 1), (mark,))
    sums = {}
    for j in range(members - 2, top - 1, -2):
        sums[j], mark = make(j, odd[j], *deps)
        deps = (mark,)
    far = scatter_even([sums[j] for j in range(top, members, 2)], axis)
    deps = (far,)
    for j in range(top - 2, -1, -2):
        sums[j], mark = make(j, odd[j], *deps)
        deps = (mark,)
    return scatter_even([sums[j] for j in range(0, top, 2)], axis), swap(far, axis, top)


def fence_kernel(*refs):
    pass


def fence(value, *deps):
    return pl.pallas_call(
        fence_kernel,
        out_shape=jax.ShapeDtypeStruct(value.shape, value.dtype),
        in_specs=[pl.BlockSpec(memory_space=pl.ANY)] * (1 + len(deps)),
        out_specs=pl.BlockSpec(memory_space=pl.ANY),
        input_output_aliases={0: 0},
        name="fence",
    )(value, *deps)


def sum_relative(value, axis, local):
    count, bit = (lax.axis_size(axis), 1)
    while bit < count:
        got = swap(value, axis, bit)
        got = [got[..., (j ^ bit) * local : ((j ^ bit) + 1) * local] for j in range(count)]
        value = value + jnp.concatenate(got, axis=-1)
        bit *= 2
    return value


class LineSum:
    def __init__(self, parts, axis, length, stride):
        count = lax.axis_size(axis)
        place = lambda i: i // stride % length
        self.axis, self.length, self.at = (axis, length, place(lax.axis_index(axis)))
        self.up = [(i, i + stride) for i in range(count) if place(i) + 1 < length]
        self.down = [(i + stride, i) for i in range(count) if place(i) + 1 < length]
        self.total = [part.astype(jnp.float32) for part in parts]

    def ready(self, step):
        return [self.total[p].astype(jnp.bfloat16) for p in (self.length - step, step)]

    def send(self, step, ready=None):
        up, down = ready or self.ready(step)
        return lax.ppermute(up, self.axis, self.up), lax.ppermute(down, self.axis, self.down)

    def add(self, step, got):
        left = self.length - step - 1
        below, above = (value.astype(jnp.float32) for value in got)
        good = (self.at >= 1) & (self.at + left < self.length)
        self.total[left] = self.total[left] + jnp.where(good, below, 0.0)
        good = (self.at + 1 < self.length) & (self.at - left >= 0)
        high = (step + 1) % self.length
        self.total[high] = self.total[high] + jnp.where(good, above, 0.0)


def line_scatter(parts, axis, length, stride):
    line = LineSum(parts, axis, length, stride)
    for step in range(1, length):
        line.add(step, line.send(step))
    return line.total[0]


def direct_scatter(parts, axis, length, stride, *deps):
    count = lax.axis_size(axis)
    got = []
    for p in range(1, length):
        moves = [(i, i + ((i // stride % length + p) % length - i // stride % length) * stride) for i in range(count)]
        got.append(lax.ppermute(parts[p], axis, moves))
    total = (fence(parts[0], *deps) if deps else parts[0]).astype(jnp.float32)
    for value in got:
        total = total + value.astype(jnp.float32)
    return total


def by_place(chunks):
    inner = chunks.shape[0] // LINE
    index = lax.axis_index("grp")
    parts = []
    for q in range(inner):
        group = []
        for p in range(LINE):
            chunk = (index // inner + p) % LINE * inner + (index % inner + q) % inner
            group.append(lax.dynamic_index_in_dim(chunks, chunk, 0, keepdims=False))
        parts.append(jnp.stack(group))
    return parts


def sum_packs(parts, *deps, last=None):
    inner = len(parts)
    mine = direct_scatter(parts, "grp", inner, 1).astype(jnp.bfloat16) if inner > 1 else parts[0]
    if last is not None:
        mine = fence(mine, last)
    return direct_scatter([mine[p] for p in range(LINE)], "grp", LINE, inner, *deps)


def widen_kernel(docs, line, sets_ref, kept_ref, got_ref, *refs):
    f32 = jnp.float32
    out_refs = refs[-line:]
    experts, rows = got_ref.shape[1:3]
    for p in range(line):
        out_refs[p][...] = kept_ref[p]
        for e in range(experts):
            for g in range(rows // (docs * RANK)):
                for d in range(docs):
                    there = pl.ds(pl.multiple_of(g * SETS * RANK + sets_ref[d] * RANK, RANK), RANK)
                    piece = got_ref[p, e, (g * docs + d) * RANK : (g * docs + d + 1) * RANK]
                    out_refs[p][e, there] = (out_refs[p][e, there].astype(f32) + piece.astype(f32)).astype(kept_ref.dtype)


def widen(docs, sets, kept, got, *deps):
    line = kept.shape[0]
    return pl.pallas_call(
        functools.partial(widen_kernel, docs, line),
        out_shape=(jax.ShapeDtypeStruct(kept.shape[1:], kept.dtype),) * line,
        in_specs=[full(SMEM), full(), full()] + [full(pl.ANY)] * len(deps),
        out_specs=(full(),) * line,
        compiler_params=params(),
        name="widen",
    )(sets, kept, got, *deps)


def sum_experts(docs, sets, parts, *deps):
    inner = len(parts)
    if inner == 2:
        return widen(docs, sets, parts[0], swap(parts[1], "grp", 1), *deps)
    mine = line_scatter(parts, "grp", inner, 1).astype(jnp.bfloat16) if inner > 1 else parts[0]
    return [mine[p] for p in range(LINE)]


def dot_nn(a, b):
    return jnp.dot(a, b, preferred_element_type=jnp.float32)


def dot_nt(a, b):
    return lax.dot_general(a, b, (((1,), (1,)), ((), ())), preferred_element_type=jnp.float32)


def dot_tn(a, b):
    return lax.dot_general(a, b, (((0,), (0,)), ((), ())), preferred_element_type=jnp.float32)


def column(row):
    return jnp.broadcast_to(row, (128, row.shape[1])).T


def as_row(value):
    return jnp.broadcast_to(value, (value.shape[0], 128)).T[:1]


def doc_sum(scal_ref, rows, docs, at):
    value = jnp.full(rows.shape, scal_ref[at], jnp.int32)
    for k in range(1, docs):
        value = jnp.where(rows >= scal_ref[k], scal_ref[at + k], value)
    return value


def block_marks(scal_ref, docs, block, local):
    rows = block * local + lax.broadcasted_iota(jnp.int32, (local, SETS * RANK), 0)
    lanes = lax.broadcasted_iota(jnp.int32, (local, SETS * RANK), 1) // RANK
    return (doc_sum(scal_ref, rows, docs, 1 + docs) == lanes).astype(jnp.float32)


def params(**kinds):
    return pltpu.CompilerParams(vmem_limit_bytes=VMEM, **kinds)


def cost(flops, moved, exps=0):
    return pl.CostEstimate(flops=int(flops) // 8, bytes_accessed=int(moved) // 8, transcendentals=int(exps) // 8)


def full(memory=pltpu.VMEM):
    return pl.BlockSpec(memory_space=memory)


SMEM = pltpu.SMEM


def project_kernel(docs, half, parts, scal_ref, *refs):
    f32, bf16 = (jnp.float32, jnp.bfloat16)
    x_refs, (gain_ref, w_ref, enter_ref, leave_ref) = (refs[:parts], refs[parts : parts + 4])
    normed_ref, low_ref, p_ref, v_ref, square_ref = refs[-5:]
    local = x_refs[0].shape[0]
    rank = SETS * RANK
    which = pl.program_id(0)

    @pl.when(which == 0)
    def _():
        enter = jnp.concatenate([enter_ref[i] for i in range(3)], axis=1)
        for b in range(parts):
            x = x_refs[b][...].astype(f32)
            here = slice(b * local, (b + 1) * local)
            normed_ref[here] = (x * rms_scale(x) * gain_ref[...].astype(f32)).astype(bf16)
            mark = block_marks(scal_ref, docs, scal_ref[0] ^ (half * parts + b), local)
            low = dot_nn(normed_ref[here], enter)
            for i in range(3):
                low_ref[i, here] = (low[:, i * rank : (i + 1) * rank] * mark).astype(bf16) * SCALE

    value = dot_nn(normed_ref[...], w_ref[0]) + dot_nn(low_ref[which], leave_ref[0])

    @pl.when(which < 2)
    def _():
        p_ref[0] = value
        square_ref[pl.ds(which, 1)] = as_row(jnp.sum(value * value, axis=1, keepdims=True))

    @pl.when(which == 2)
    def _():
        v_ref[...] = value.astype(bf16)


def project(docs, half, scal, x_parts, gain, weight, enter, leave, kept, *deps):
    parts = len(x_parts)
    local, width = x_parts[0].shape
    slice_width = weight.shape[2]
    rows, rank = (parts * local, enter.shape[2])
    f32, bf16 = (jnp.float32, jnp.bfloat16)
    outs = (
        jax.ShapeDtypeStruct((2 * rows, width), bf16),
        jax.ShapeDtypeStruct((3, 2 * rows, rank), bf16),
        jax.ShapeDtypeStruct((2, 2 * rows, slice_width), f32),
        jax.ShapeDtypeStruct((2 * rows, slice_width), bf16),
        jax.ShapeDtypeStruct((2, 2 * rows), f32),
    )
    extra = () if kept is None else kept
    first = 5 + parts
    return pl.pallas_call(
        functools.partial(project_kernel, docs, half, parts),
        grid=(3,),
        out_shape=outs,
        in_specs=[full(SMEM)]
        + [full()] * parts
        + [
            full(),
            pl.BlockSpec((1, width, slice_width), lambda i: (i, 0, 0)),
            full(),
            pl.BlockSpec((1, rank, slice_width), lambda i: (i, 0, 0)),
        ]
        + [full(pl.ANY)] * (len(extra) + len(deps)),
        out_specs=(
            pl.BlockSpec((rows, width), lambda i: (half, 0)),
            pl.BlockSpec((3, rows, rank), lambda i: (0, half, 0)),
            pl.BlockSpec((1, rows, slice_width), lambda i: (jnp.minimum(i, 1), half, 0)),
            pl.BlockSpec((rows, slice_width), lambda i: (half, 0)),
            pl.BlockSpec((2, rows), lambda i: (0, half)),
        ),
        input_output_aliases={first + i: i for i in range(len(extra))},
        compiler_params=params(),
        cost_estimate=cost(2 * rows * width * (3 * slice_width + 3 * rank), 14_000_000),
        name="project",
    )(scal, *x_parts, gain, weight, enter, leave, *extra, *deps)


def prepare_kernel(width, p_ref, square_ref, gains_ref, cos_ref, sin_ref, q_ref, k_ref):
    inverse = lax.rsqrt(square_ref[...] / width + EPS)
    for i, out_ref in ((0, q_ref), (1, k_ref)):
        scale = column(inverse[i : i + 1])
        for at in range(0, p_ref.shape[2], HEAD_DIM):
            cut = slice(at, at + HEAD_DIM)
            value = p_ref[i, :, cut] * scale * gains_ref[i : i + 1, cut]
            value = value * cos_ref[...] + pltpu.roll(value, HEAD_DIM // 2, 1) * sin_ref[...]
            out_ref[:, cut] = value.astype(jnp.bfloat16)


def prepare(width, p, squares, gains, cosine, sine, local, *deps):
    _, rows, slice_width = p.shape
    out = jax.ShapeDtypeStruct((rows, slice_width), jnp.bfloat16)
    return pl.pallas_call(
        lambda *refs: prepare_kernel(width, *refs[:5], *refs[5 + len(deps) :]),
        grid=(rows // local,),
        out_shape=(out, out),
        in_specs=[
            pl.BlockSpec((2, local, slice_width), lambda i: (0, i, 0)),
            pl.BlockSpec((2, local), lambda i: (0, i)),
            full(),
            pl.BlockSpec((local, HEAD_DIM), lambda i: (i, 0)),
            pl.BlockSpec((local, HEAD_DIM), lambda i: (i, 0)),
        ]
        + [full(pl.ANY)] * len(deps),
        out_specs=(pl.BlockSpec((local, slice_width), lambda i: (i, 0)),) * 2,
        compiler_params=params(),
        cost_estimate=cost(10 * p.size, 8 * p.size),
        name="prepare",
    )(p, squares, gains, cosine, sine, *deps)


def attend_kernel(docs, place, local, added, scal_ref, q_ref, k_ref, v_ref, w_ref, enter_ref, *refs):
    f32, bf16 = (jnp.float32, jnp.bfloat16)
    att_ref, part_ref, log_ref = refs[-3:]
    members = q_ref.shape[0] // local
    heads = q_ref.shape[1] // HEAD_DIM
    width = w_ref.shape[1]
    member = scal_ref[0]
    block = member ^ place
    queries = slice(place * local, (place + 1) * local)

    def run(last):
        rows = last * local + lax.broadcasted_iota(jnp.int32, (local, local), 0)
        begin = doc_sum(scal_ref, rows, docs, 1 + 2 * docs)
        lanes = lax.broadcasted_iota(jnp.int32, (local, local), 1)
        logs = jnp.zeros((8, local), f32)
        for h in range(heads):
            cut = slice(h * HEAD_DIM, (h + 1) * HEAD_DIM)
            query = q_ref[queries, cut]
            scores, values = ([], [])
            for b in range(last + 1):
                there = pl.ds(pl.multiple_of((member ^ b) * local, local), local)
                score = dot_nt(query, k_ref[there, cut]) * HEAD_DIM ** (-0.5)
                good = lanes + b * local >= begin
                if b == last:
                    good = good & (lanes + b * local <= rows)
                scores.append(jnp.where(good, score, NEG))
                values.append(v_ref[there, cut])
            peak = functools.reduce(jnp.maximum, [jnp.max(score, axis=1, keepdims=True) for score in scores])
            expo = [jnp.exp(score - peak) for score in scores]
            total = functools.reduce(jnp.add, [jnp.sum(e, axis=1, keepdims=True) for e in expo])
            share = 1.0 / total
            mixed = functools.reduce(jnp.add, [dot_nn((e * share).astype(bf16), v) for e, v in zip(expo, values)])
            att_ref[:, cut] = mixed.astype(bf16)
            head_row = lax.broadcasted_iota(jnp.int32, (8, local), 0) == h
            logs = jnp.where(head_row, as_row(peak + jnp.log(total)), logs)
        log_ref[...] = logs

    for last in range(members):
        pl.when(block == last)(functools.partial(run, last))
    for cut, value_ref in ((slice(0, width), w_ref), (slice(width, None), enter_ref)):
        value = dot_nn(att_ref[...], value_ref[...])
        if added:
            value = value + refs[0][:, cut].astype(f32)
        part_ref[:, cut] = value.astype(bf16)


def attend(docs, place, local, scal, q, k, v, weight, enter, addend, *deps):
    slice_width = q.shape[1]
    width, rank = (weight.shape[1], enter.shape[1])
    f32, bf16 = (jnp.float32, jnp.bfloat16)
    assert slice_width // HEAD_DIM <= 8
    return pl.pallas_call(
        functools.partial(attend_kernel, docs, place, local, addend is not None),
        out_shape=(
            jax.ShapeDtypeStruct((local, slice_width), bf16),
            jax.ShapeDtypeStruct((local, width + rank), bf16),
            jax.ShapeDtypeStruct((8, local), f32),
        ),
        in_specs=[full(SMEM)] + [full()] * (5 + (addend is not None)) + [full(pl.ANY)] * len(deps),
        out_specs=(full(),) * 3,
        compiler_params=params(),
        cost_estimate=cost(2_200_000_000, 4_000_000, 350_000),
        name="attend",
    )(scal, q, k, v, weight, enter, *(() if addend is None else (addend,)), *deps)


def middle_kernel(
    docs, scal_ref, x_ref, oa_ref, ob_ref, leave_ref, gain_ref, route_ref, route_enter, route_leave, h_ref, normed_ref, route_low, probs_ref
):
    f32, bf16 = (jnp.float32, jnp.bfloat16)
    width = x_ref.shape[1]
    mark = block_marks(scal_ref, docs, scal_ref[0], x_ref.shape[0])
    low = ((oa_ref[:, width:].astype(f32) + ob_ref[:, width:].astype(f32)) * mark).astype(bf16)
    normed_ref[:, width:] = low
    h = x_ref[...].astype(f32) + (oa_ref[:, :width].astype(f32) + ob_ref[:, :width].astype(f32))
    h = h + SCALE * dot_nn(low, leave_ref[...])
    h_ref[...] = h
    normed = (h * rms_scale(h) * gain_ref[...].astype(f32)).astype(bf16)
    normed_ref[:, :width] = normed
    low, probs = router(normed, mark, route_ref, route_enter, route_leave)
    route_low[...] = low
    probs_ref[...] = probs


def router(normed, mark, route_ref, route_enter, route_leave):
    low = (dot_nn(normed, route_enter[...]) * mark).astype(jnp.bfloat16)
    logits = dot_nt(route_ref[...], normed) + SCALE * dot_nt(route_leave[...], low)
    expo = jnp.exp(logits - jnp.max(logits, axis=0, keepdims=True))
    return low, expo / jnp.sum(expo, axis=0, keepdims=True)


def middle(docs, scal, x, outs, leave, gain, route, route_enter, route_leave, *deps):
    local, width = x.shape
    rank = leave.shape[0]
    f32, bf16 = (jnp.float32, jnp.bfloat16)
    return pl.pallas_call(
        lambda *refs: middle_kernel(docs, *refs[:9], *refs[9 + len(deps) :]),
        out_shape=(
            jax.ShapeDtypeStruct((local, width), f32),
            jax.ShapeDtypeStruct((local, width + rank), bf16),
            jax.ShapeDtypeStruct((local, rank), bf16),
            jax.ShapeDtypeStruct((route.shape[0], local), f32),
        ),
        in_specs=[full(SMEM)] + [full()] * 8 + [full(pl.ANY)] * len(deps),
        out_specs=(full(),) * 4,
        compiler_params=params(),
        cost_estimate=cost(4 * local * width * rank, 8_000_000),
        name="middle",
    )(scal, x, *outs, leave, gain, route, route_enter, route_leave, *deps)


def middle_back_kernel(
    docs, scal_ref, ga_ref, gb_ref, probs_ref, h_ref, up_ref, route_low, gain_ref, route_ref, route_enter, route_leave, dh_ref, dhb_ref, leave_ref
):
    f32, bf16 = (jnp.float32, jnp.bfloat16)
    width = h_ref.shape[1]
    mark = block_marks(scal_ref, docs, scal_ref[0], h_ref.shape[0])
    probs = probs_ref[...]
    experts = probs.shape[0]
    scores = (ga_ref[:, width:].astype(f32) + gb_ref[:, width:].astype(f32)).T
    dprobs = scores[:experts] + scores[experts : 2 * experts]
    dlogits = (probs * (dprobs - jnp.sum(probs * dprobs, axis=0, keepdims=True))).astype(bf16)
    dlow = (dot_tn(dlogits, route_leave[...]) * SCALE * mark).astype(bf16)
    dhb_ref[:, width:] = dlow
    leave_ref[...] = SCALE * dot_nn(dlogits, route_low[...])
    back = ga_ref[:, :width].astype(f32) + gb_ref[:, :width].astype(f32)
    back = back + dot_tn(dlogits, route_ref[...]) + dot_nt(dlow, route_enter[...])
    back = back * gain_ref[...].astype(f32)
    h = h_ref[...]
    scale = rms_scale(h)
    dh = up_ref[...].astype(f32) + scale * back - h * scale**3 * jnp.mean(h * back, axis=-1, keepdims=True)
    dh_ref[...] = dh
    dhb_ref[:, :width] = dh.astype(bf16)


def middle_back(docs, scal, grads, probs, h, upstream, route_low, gain, route, route_enter, route_leave):
    local, width = h.shape
    rank = route_enter.shape[1]
    f32, bf16 = (jnp.float32, jnp.bfloat16)
    return pl.pallas_call(
        functools.partial(middle_back_kernel, docs),
        out_shape=(
            jax.ShapeDtypeStruct((local, width), f32),
            jax.ShapeDtypeStruct((local, width + rank), bf16),
            jax.ShapeDtypeStruct((route.shape[0], rank), f32),
        ),
        in_specs=[full(SMEM)] + [full()] * 10,
        out_specs=(full(),) * 3,
        compiler_params=params(),
        cost_estimate=cost(4 * local * width * rank, 10_000_000),
        name="middle_back",
    )(scal, *grads, probs, h, upstream, route_low, gain, route, route_enter, route_leave)


def attend_back_kernel(docs, half, local, scal_ref, *refs):
    f32, bf16 = (jnp.float32, jnp.bfloat16)
    q_ref = refs[0]
    members = q_ref.shape[0] // local
    count = members // 2
    heads = q_ref.shape[1] // HEAD_DIM
    q_ref, k_ref, v_ref, w_ref, enter_ref, leave_ref = refs[:6]
    refs = refs[6:]
    grad_refs, att_refs, log_refs, normed_refs, refs = (*(refs[i * count : (i + 1) * count] for i in range(4)), refs[4 * count :])
    before, refs = (refs[: 5 * half], refs[5 * half + half :])
    dq_ref, dk_ref, dv_ref, enter_grad, leave_grad, route_grad, *rest = refs
    term_refs, (grad, datt, att, logs, normed) = (rest[:-5], rest[-5:])
    width = w_ref.shape[1]
    step = pl.program_id(0)
    place = half * count + step
    member = scal_ref[0]
    block = member ^ place
    queries = pl.ds(pl.multiple_of(place * local, local), local)
    mine = pl.ds(pl.multiple_of(member * q_ref.shape[1], 128), q_ref.shape[1])

    @pl.when(step == 0)
    def _():
        for i, ref in enumerate((dk_ref, dv_ref, enter_grad, leave_grad, route_grad)):
            ref[...] = before[i][...] if half else jnp.zeros_like(ref)

    for i in range(count):

        @pl.when(step == i)
        def _():
            grad[...] = grad_refs[i][...]
            att[...] = att_refs[i][...]
            logs[...] = log_refs[i][...]
            normed[:, : mine.size] = normed_refs[i][:, mine]
            normed[:, mine.size :] = normed_refs[i][:, width:]

    mark = block_marks(scal_ref, docs, block, local)
    low = (dot_nt(grad[:, :width], leave_ref[...]) * SCALE * mark).astype(bf16)
    datt[...] = (dot_nt(grad[:, :width], w_ref[...]) + dot_nt(low, enter_ref[...])).astype(bf16)
    enter_grad[...] += dot_tn(low, att[...])
    leave_grad[...] += SCALE * dot_tn(normed[:, mine.size :], grad[:, mine])
    route_grad[...] += dot_tn(grad[:, width:], normed[:, : mine.size])

    def run(last):
        rows = last * local + lax.broadcasted_iota(jnp.int32, (local, local), 1)
        begin = doc_sum(scal_ref, rows, docs, 1 + 2 * docs)
        down = lax.broadcasted_iota(jnp.int32, (local, local), 0)
        term = jnp.zeros((local, 1), f32)
        for h in range(heads):
            cut = slice(h * HEAD_DIM, (h + 1) * HEAD_DIM)
            query, dout = (q_ref[queries, cut], datt[:, cut])
            log = logs[h : h + 1]
            shares, pushes = ([], [])
            for b in range(last + 1):
                there = pl.ds(pl.multiple_of((member ^ b) * local, local), local)
                score = dot_nt(k_ref[there, cut], query) * HEAD_DIM ** (-0.5)
                good = down + b * local >= begin
                if b == last:
                    good = good & (down + b * local <= rows)
                share = jnp.where(good, jnp.exp(score - log), 0.0)
                shares.append(share)
                pushes.append(dot_nt(v_ref[there, cut], dout))
            inner = functools.reduce(jnp.add, [jnp.sum(s * d, axis=0, keepdims=True) for s, d in zip(shares, pushes)])
            dquery = jnp.zeros((local, HEAD_DIM), f32)
            for b in range(last + 1):
                there = pl.ds(pl.multiple_of((member ^ b) * local, local), local)
                dscore = (shares[b] * (pushes[b] - inner) * HEAD_DIM ** (-0.5)).astype(bf16)
                dquery = dquery + dot_tn(dscore, k_ref[there, cut])
                dk_ref[there, cut] += dot_nn(dscore, query)
                dv_ref[there, cut] += dot_nn(shares[b].astype(bf16), dout)
            dq_ref[:, cut] = dquery
            term = term + jnp.sum(dquery * query.astype(f32), axis=1, keepdims=True)
        term_refs[0][...] = as_row(term)

    for last in range(members):
        pl.when(block == last)(functools.partial(run, last))

    if half:

        @pl.when(step == count - 1)
        def _():
            for b in range(members):
                here = slice(b * local, (b + 1) * local)
                value = jnp.sum(dk_ref[here] * k_ref[here].astype(f32), axis=1, keepdims=True)
                term_refs[1][:, here] = as_row(value)


def attend_back(docs, half, scal, q, k, v, weight, enter, leave, grads, atts, logs, normed, before, *deps):
    group_len, slice_width = q.shape
    local = grads[0].shape[0]
    width, rank = (weight.shape[1], enter.shape[1])
    count = len(grads)
    f32, bf16 = (jnp.float32, jnp.bfloat16)
    low_grad = jax.ShapeDtypeStruct((rank, slice_width), f32)
    outs = (
        jax.ShapeDtypeStruct((count * local, slice_width), f32),
        jax.ShapeDtypeStruct((group_len, slice_width), f32),
        jax.ShapeDtypeStruct((group_len, slice_width), f32),
        low_grad,
        low_grad,
        low_grad,
        jax.ShapeDtypeStruct((1, count * local), f32),
    ) + ((jax.ShapeDtypeStruct((1, group_len), f32),) if half else ())
    return pl.pallas_call(
        functools.partial(attend_back_kernel, docs, half, local),
        grid=(count,),
        out_shape=outs,
        in_specs=[full(SMEM)] + [full()] * (6 + 4 * count + len(before)) + [full(pl.ANY)] * len(deps),
        out_specs=(pl.BlockSpec((local, slice_width), lambda i: (i, 0)),)
        + (full(),) * 5
        + (pl.BlockSpec((1, local), lambda i: (0, i)),)
        + ((full(),) if half else ()),
        scratch_shapes=[
            pltpu.VMEM((local, width + rank), bf16),
            pltpu.VMEM((local, slice_width), bf16),
            pltpu.VMEM((local, slice_width), bf16),
            pltpu.VMEM((8, local), f32),
            pltpu.VMEM((local, slice_width + rank), bf16),
        ],
        compiler_params=params(),
        cost_estimate=cost(8_000_000_000, 14_000_000, 700_000),
        name="attend_back",
    )(scal, q, k, v, weight, enter, leave, *grads, *atts, *logs, *normed, *before, *deps)


def project_back_kernel(docs, local, scal_ref, *refs):
    f32, bf16 = (jnp.float32, jnp.bfloat16)
    near_ref, far_ref, dk_ref, dv_ref, p_ref, square_ref, term_ref, gains_ref, cos_ref, sin_ref, normed_ref, low_ref = refs[:12]
    w_ref, enter_ref, leave_ref, route_ref, *refs = refs[12:]
    *dx_refs, enter_grad, leave_grad, dp_ref, dlow_ref, turned = refs
    rows, slice_width = near_ref.shape
    rank = SETS * RANK
    member = scal_ref[0]
    step = pl.program_id(0)
    members = pl.num_programs(0)
    width = slice_width * members
    count = rows // local

    @pl.when(step == 0)
    def _():
        inverse = lax.rsqrt(square_ref[...] / width + EPS)
        biases = inverse * inverse * term_ref[...] / width
        for i in range(2):
            for half in range(2):
                here = slice(half * rows, (half + 1) * rows)
                scale, bias = (column(inverse[i : i + 1, here]), column(biases[i : i + 1, here]))
                for at in range(0, slice_width, HEAD_DIM):
                    cut = slice(at, at + HEAD_DIM)
                    value = dk_ref[here, cut] if i else (far_ref if half else near_ref)[:, cut]
                    value = value * cos_ref[here] - pltpu.roll(value, HEAD_DIM // 2, 1) * sin_ref[here]
                    value = value * gains_ref[i : i + 1, cut] * scale - p_ref[i, here, cut] * bias
                    dp_ref[i, here, cut] = value.astype(bf16)
        dp_ref[2] = dv_ref[...].astype(bf16)
        for b in range(2 * count):
            here = slice(b * local, (b + 1) * local)
            mark = block_marks(scal_ref, docs, member ^ b, local)
            for i in range(3):
                value = dot_nt(dp_ref[i, here], leave_ref[i]) * SCALE * mark
                dlow_ref[here, i * rank : (i + 1) * rank] = value.astype(bf16)
                turned[i * rank : (i + 1) * rank, here] = value.T.astype(bf16)
        for i in range(3):
            leave_grad[i] = dot_tn(low_ref[i], dp_ref[i])

    enter_grad[0, : 3 * rank] = dot_nn(turned[...], normed_ref[...]).astype(bf16)
    enter_grad[0, 3 * rank :] = route_ref[0]
    spread_back(dx_refs, [dp_ref[i, rows:] for i in range(3)], dlow_ref[rows:], w_ref, enter_ref)


def spread_back(dx_refs, grads, low, w_ref, enter_ref):
    value = dot_nt(grads[0], w_ref[0]) + dot_nt(grads[1], w_ref[1]) + dot_nt(grads[2], w_ref[2])
    value = value + dot_nt(low, jnp.concatenate([enter_ref[i] for i in range(3)], axis=1))
    value = value.astype(jnp.bfloat16)
    local = dx_refs[0].shape[0]
    for b, dx_ref in enumerate(dx_refs):
        dx_ref[...] = value[b * local : (b + 1) * local]


def project_back(docs, local, scal, near, far, dk, dv, p, squares, terms, gains, cosine, sine, normed, low, weight, enter, leave, route_grad, *deps):
    rows, slice_width = near.shape
    width, rank = (normed.shape[1], enter.shape[2])
    members, count = (2 * rows // local, rows // local)
    tall = 3 * rank + route_grad.shape[1]
    f32, bf16 = (jnp.float32, jnp.bfloat16)
    pick = lambda i, scal: scal[0] ^ i
    sums = pl.BlockSpec((1, tall, slice_width), lambda i, scal: (i, 0, 0))
    in_specs = [full()] * 10 + [
        pl.BlockSpec((2 * rows, slice_width), lambda i, scal: (0, pick(i, scal))),
        full(),
        pl.BlockSpec((3, slice_width, slice_width), lambda i, scal: (0, pick(i, scal), 0)),
        pl.BlockSpec((3, slice_width, rank), lambda i, scal: (0, pick(i, scal), 0)),
        full(),
        pl.BlockSpec((1, tall - 3 * rank, slice_width), lambda i, scal: (i, 0, 0)),
    ] + [full(pl.ANY)] * len(deps)
    return pl.pallas_call(
        lambda *refs: project_back_kernel(docs, local, *refs[:17], *refs[17 + len(deps) :]),
        out_shape=(jax.ShapeDtypeStruct((local, width), bf16),) * count
        + (
            jax.ShapeDtypeStruct((members, tall, slice_width), bf16),
            jax.ShapeDtypeStruct((3, rank, slice_width), f32),
            jax.ShapeDtypeStruct((3, 2 * rows, slice_width), bf16),
            jax.ShapeDtypeStruct((2 * rows, 3 * rank), bf16),
        ),
        grid_spec=pltpu.PrefetchScalarGridSpec(
            num_scalar_prefetch=1,
            grid=(members,),
            in_specs=in_specs,
            out_specs=(pl.BlockSpec((local, slice_width), lambda i, scal: (0, pick(i, scal))),) * count
            + (sums, full(), full(), full()),
            scratch_shapes=[pltpu.VMEM((3 * rank, 2 * rows), bf16)],
        ),
        compiler_params=params(),
        cost_estimate=cost(2 * rows * (width * 3 * slice_width + 6 * rank * width), 20_000_000),
        name="project_back",
    )(scal, near, far, dk, dv, p, squares, terms, gains, cosine, sine, normed, low, weight, enter, leave, route_grad, *deps)


def project_near(local, grads, low, weight, enter, *deps):
    _, group_len, slice_width = grads.shape
    rows, width, rank = (group_len // 2, weight.shape[1], enter.shape[2])
    count = rows // local
    step = slice_width
    out = jax.ShapeDtypeStruct((local, width), jnp.bfloat16)

    def kernel(grads_ref, low_ref, w_ref, enter_ref, *refs):
        spread_back(refs[-count:], [grads_ref[i] for i in range(3)], low_ref[...], w_ref, enter_ref)

    return pl.pallas_call(
        kernel,
        grid=(width // step,),
        out_shape=(out,) * count,
        in_specs=[
            pl.BlockSpec((3, rows, slice_width), lambda i: (0, 0, 0)),
            pl.BlockSpec((rows, 3 * rank), lambda i: (0, 0)),
            pl.BlockSpec((3, step, slice_width), lambda i: (0, i, 0)),
            pl.BlockSpec((3, step, rank), lambda i: (0, i, 0)),
        ]
        + [full(pl.ANY)] * len(deps),
        out_specs=(pl.BlockSpec((local, step), lambda i: (0, i)),) * count,
        compiler_params=params(),
        cost_estimate=cost(2 * rows * (width * 3 * slice_width), 10_000_000),
        name="project_near",
    )(grads, low, weight, enter, *deps)


def finish_kernel(*refs):
    f32 = jnp.float32
    *parts, dh_ref, x_ref, gain_ref, out_ref = refs
    x = x_ref[...].astype(f32)
    back = functools.reduce(jnp.add, [part[...].astype(f32) for part in parts]) * gain_ref[...].astype(f32)
    scale = rms_scale(x)
    out = dh_ref[...] + scale * back - x * scale**3 * jnp.mean(x * back, axis=-1, keepdims=True)
    out_ref[...] = out.astype(out_ref.dtype)


def finish(grads, dh, x, gain):
    return pl.pallas_call(
        finish_kernel,
        out_shape=jax.ShapeDtypeStruct(x.shape, jnp.bfloat16),
        in_specs=[full()] * (3 + len(grads)),
        out_specs=full(),
        compiler_params=params(),
        cost_estimate=cost(10 * x.size, 12 * x.size),
        name="finish",
    )(*grads, dh, x, gain)


def upstream_kernel(scal_ref, named_ref, *refs):
    blocks = named_ref.shape[0]
    f32, bf16 = (jnp.float32, jnp.bfloat16)
    upstream_refs, (down_w, down_leave, rank_ref, rows_ref, back_ref, low_ref, places) = (refs[:blocks], refs[-7:])
    experts, local = places.shape[1:]
    cap = rows_ref.shape[1] // blocks

    @pl.when((pl.program_id(0) == 0) | (pl.num_programs(1) > 1))
    def _():
        earlier = lax.broadcasted_iota(jnp.int32, (local, local), 0) < lax.broadcasted_iota(jnp.int32, (local, local), 1)
        bits = lax.broadcasted_iota(jnp.int32, (experts, local), 0)
        for b in range(blocks):
            hot = (jnp.right_shift(named_ref[b], bits) & 1).astype(f32)
            rank = dot_nn(hot.astype(bf16), earlier.astype(f32).astype(bf16))
            places[b] = jnp.where(hot > 0.0, rank, -1.0)

    mine = pl.ds(scal_ref[0] * pl.num_programs(0) + pl.program_id(0), 1)
    slots = lax.broadcasted_iota(jnp.int32, (cap, local), 0).astype(f32)
    for b in range(blocks):
        rank_ref[0, b] = places[b, mine]
        pick = (places[b, mine] == slots).astype(bf16)
        rows_ref[0, b * cap : (b + 1) * cap] = dot_nn(pick, upstream_refs[b][...]).astype(bf16)
    back_ref[0] = dot_nt(rows_ref[0], down_w[0]).astype(bf16)
    low_ref[0] = dot_nt(rows_ref[0], down_leave[0])


def run_upstream(scal, named, upstream, down, down_leave, *deps):
    members, _, local = named.shape
    experts, ff, width = down.shape
    low = down_leave.shape[1]
    blocks = min(members, 4)
    turns = members // blocks
    count = blocks * CAP
    f32, bf16 = (jnp.float32, jnp.bfloat16)
    rows = lambda wide: pl.BlockSpec((1, count, wide), lambda e, r: (e, r, 0))
    return pl.pallas_call(
        lambda *refs: upstream_kernel(*refs[: 4 + blocks], *refs[4 + blocks + len(deps) :]),
        grid=(experts, turns),
        out_shape=(
            jax.ShapeDtypeStruct((experts, members, 1, local), f32),
            jax.ShapeDtypeStruct((experts, members * CAP, width), bf16),
            jax.ShapeDtypeStruct((experts, members * CAP, ff), bf16),
            jax.ShapeDtypeStruct((experts, members * CAP, low), f32),
        ),
        in_specs=[full(SMEM), pl.BlockSpec((blocks, 1, local), lambda e, r: (r, 0, 0))]
        + [pl.BlockSpec((local, width), lambda e, r: (r, 0), pipeline_mode=pl.Buffered(1))] * blocks
        + [pl.BlockSpec((1, ff, width), lambda e, r: (e, 0, 0)), pl.BlockSpec((1, low, width), lambda e, r: (e, 0, 0))]
        + [full(pl.ANY)] * len(deps),
        out_specs=(pl.BlockSpec((1, blocks, 1, local), lambda e, r: (e, r, 0, 0)), rows(width), rows(ff), rows(low)),
        scratch_shapes=[pltpu.VMEM((blocks, EXPERTS, local), f32)],
        compiler_params=params(),
        cost_estimate=cost(2 * experts * members * CAP * width * ff, 40_000_000),
        name="upstream",
    )(scal, named, *by_block(upstream, blocks), down, down_leave, *deps)


def by_block(parts, blocks):
    return [jnp.concatenate(parts[b::blocks]) if len(parts) > blocks else parts[b] for b in range(blocks)]


def dispatch(docs, scal_ref, place, rank_rows, weight_rows, normed_refs, rows_in, marks):
    local, low = (rank_rows[0].shape[1], marks.shape[1])
    cap = rows_in.shape[0] // len(rank_rows)
    slots = lax.broadcasted_iota(jnp.int32, (cap, local), 0).astype(jnp.float32)
    weights = []
    for b, rank_row in enumerate(rank_rows):
        hit = rank_row == slots
        pick = hit.astype(jnp.bfloat16)
        weights.append(jnp.sum(jnp.where(hit, weight_rows[b], 0.0), axis=1, keepdims=True))
        here = slice(b * cap, (b + 1) * cap)
        mark = block_marks(scal_ref, docs, scal_ref[0] ^ (place + b), local).astype(jnp.bfloat16)
        rows_in[here, :] = dot_nn(pick, normed_refs[b][:, : rows_in.shape[1]]).astype(jnp.bfloat16)
        marks[here, :] = dot_nn(pick, mark)
    return jnp.concatenate(weights, axis=0)


def inner_rows(
    first, rows_in, mark, weight, low_in, back_in, gate_w, up_w, gate_enter, gate_leave, up_enter, up_leave, down_enter, hidden, grad_gate, grad_up
):
    f32, bf16 = (jnp.float32, jnp.bfloat16)
    rank, ff = (mark.shape[1], hidden.shape[1])
    rows = rows_in[first:]
    low = dot_nn(rows, jnp.concatenate([gate_enter[0], up_enter[0]], axis=1))
    low_gate = (low[:, :rank] * mark).astype(bf16) * SCALE
    low_up = (low[:, rank:] * mark).astype(bf16) * SCALE
    grad_low_down = (low_in[...] * (SCALE * weight) * mark).astype(bf16)
    step = min(256, ff)
    for at in range(0, ff, step):
        cut = slice(at, at + step)
        gate = dot_nn(rows, gate_w[0, :, cut]) + dot_nn(low_gate, gate_leave[0, :, cut])
        up = dot_nn(rows, up_w[0, :, cut]) + dot_nn(low_up, up_leave[0, :, cut])
        back = back_in[:, cut].astype(f32) * weight + dot_nt(grad_low_down, down_enter[0, cut, :])
        sigma = 1.0 / (1.0 + jnp.exp(-gate))
        silu = gate * sigma
        hidden[first:, cut] = (silu * up).astype(bf16)
        grad_gate[first:, cut] = (back * up * sigma * (1.0 + gate * (1.0 - sigma))).astype(bf16)
        grad_up[first:, cut] = (back * silu).astype(bf16)
    return low_gate, low_up, grad_low_down


def near_kernel(docs, scal_ref, rank_ref, back_ref, low_ref, route_ref, route_enter, route_leave, *refs):
    count = len(refs) - 14
    normed_refs, refs = (refs[:count], refs[count:])
    weights, (hidden, grad_gate, grad_up, lows, rows_in, marks, probs) = (refs[:7], refs[7:])
    width = rows_in.shape[1]
    local = rank_ref.shape[3]

    @pl.when(pl.program_id(0) == 0)
    def _():
        for b in range(count):
            mark = block_marks(scal_ref, docs, scal_ref[0] ^ b, local)
            probs[b] = router(normed_refs[b][:, :width], mark, route_ref, route_enter, route_leave)[1]

    mine = pl.ds(scal_ref[0] * pl.num_programs(0) + pl.program_id(0), 1)
    rank_rows, weight_rows = ([rank_ref[0, b] for b in range(count)], [probs[b, mine] for b in range(count)])
    weight = dispatch(docs, scal_ref, 0, rank_rows, weight_rows, normed_refs, rows_in, marks)
    made = inner_rows(
        0, rows_in, marks[...], weight, low_ref.at[0], back_ref.at[0], *weights, hidden.at[0], grad_gate.at[0], grad_up.at[0]
    )
    lows[0] = jnp.concatenate(made, axis=1)


def run_near(docs, scal, ranks, back, low_back, route, route_enter, route_leave, normed, *weights):
    experts, members, _, local = ranks.shape
    ff, low = (back.shape[2], low_back.shape[2])
    width = normed[0].shape[1] - low
    rows = len(normed) * CAP
    bf16 = jnp.bfloat16
    near = lambda wide: pl.BlockSpec((1, rows, wide), lambda e: (e, 0, 0))
    hidden = jax.ShapeDtypeStruct((experts, rows, ff), bf16)
    return pl.pallas_call(
        functools.partial(near_kernel, docs),
        grid=(experts,),
        out_shape=(hidden, hidden, hidden, jax.ShapeDtypeStruct((experts, rows, 3 * low), bf16)),
        in_specs=[full(SMEM), pl.BlockSpec((1, members, 1, local), lambda e: (e, 0, 0, 0)), near(ff), near(low)]
        + [full()] * (3 + len(normed))
        + [pl.BlockSpec((1,) + value.shape[1:], lambda e: (e, 0, 0)) for value in weights],
        out_specs=(near(ff), near(ff), near(ff), near(3 * low)),
        scratch_shapes=[
            pltpu.VMEM((rows, width), bf16),
            pltpu.VMEM((rows, low), jnp.float32),
            pltpu.VMEM((len(normed), EXPERTS, local), jnp.float32),
        ],
        compiler_params=params(),
        cost_estimate=cost(4 * experts * rows * width * ff, 40_000_000),
        name="near",
    )(scal, ranks, back, low_back, route, route_enter, route_leave, *normed, *weights)


def expert_kernel(line, docs, made, scal_ref, rank_ref, grads_ref, back_ref, low_ref, route_ref, route_enter, route_leave, *refs):
    blocks = rank_ref.shape[1]
    ahead, refs = (refs[:made], refs[made:])
    normed_refs, refs, probs = (refs[:blocks], refs[blocks:-1], refs[-1])
    width = grads_ref.shape[2]
    turn = pl.program_id(1)
    local = rank_ref.shape[3]

    @pl.when((pl.program_id(0) == 0) | (pl.num_programs(1) > 1))
    def _():
        for b in range(blocks):
            mark = block_marks(scal_ref, docs, scal_ref[0] ^ (turn * blocks + b), local)
            probs[b] = router(normed_refs[b][:, :width], mark, route_ref, route_enter, route_leave)[1]

    mine = pl.ds(scal_ref[0] * pl.num_programs(0) + pl.program_id(0), 1)
    weights = [probs[b, mine] for b in range(blocks)]
    expert_rows(line, docs, ahead, scal_ref, rank_ref, weights, normed_refs, grads_ref.at[0], back_ref.at[0], low_ref.at[0], *refs)


def expert_rows(
    line,
    docs,
    ahead,
    scal_ref,
    rank_ref,
    weight_rows,
    normed_refs,
    grads_in,
    back_in,
    low_in,
    gate_w,
    up_w,
    down_w,
    gate_enter,
    gate_leave,
    up_enter,
    up_leave,
    down_enter,
    down_leave,
    place_ref,
    mixed_ref,
    grad_ref,
    score_ref,
    *rest,
):
    inner = len(rest) - 9
    sums, (rows_in, hidden, grad_gate, grad_up, marks, out_tile, back_tile, done, full_rows) = (rest[:inner], rest[inner:])
    f32, bf16 = (jnp.float32, jnp.bfloat16)
    blocks, local, width = (rank_ref.shape[1], rank_ref.shape[3], grads_in.shape[1])
    cap = mixed_ref.shape[2]
    expert, turn = (pl.program_id(0), pl.program_id(1))
    count = blocks * cap
    ff = hidden.shape[1]
    slots = lax.broadcasted_iota(jnp.int32, (cap, local), 0).astype(f32)
    rank_rows = [rank_ref[0, b] for b in range(blocks)]
    weight = dispatch(docs, scal_ref, turn * blocks, rank_rows, weight_rows, normed_refs, rows_in, marks)
    mark = marks[...]
    rank = mark.shape[1]
    first = ahead[0].shape[1] if ahead else 0
    lows = inner_rows(
        first, rows_in, mark[first:], weight[first:], low_in, back_in, gate_w, up_w, gate_enter, gate_leave, up_enter, up_leave, down_enter,
        hidden, grad_gate, grad_up
    )
    if ahead:
        for to, of in zip((hidden, grad_gate, grad_up), ahead):
            to[:first] = of[0]
        lows = [jnp.concatenate([ahead[3][0, :, i * rank : (i + 1) * rank], value], axis=0) for i, value in enumerate(lows)]
    low_gate, low_up, grad_low_down = lows
    low_down = (dot_nn(hidden[...], down_enter[0]) * mark).astype(bf16) * SCALE
    grad_low_gate = (dot_nt(grad_gate[...], gate_leave[0]) * SCALE * mark).astype(bf16)
    grad_low_up = (dot_nt(grad_up[...], up_leave[0]) * SCALE * mark).astype(bf16)
    grad_low = jnp.concatenate([grad_low_gate, grad_low_up], axis=1)
    step = out_tile.shape[3]
    sent = []

    def send(slot, cut):
        there = pl.ds(turn * blocks, blocks)
        copies = [
            pltpu.make_async_copy(out_tile.at[slot], mixed_ref.at[there, expert, :, cut], done.at[0, slot]),
            pltpu.make_async_copy(back_tile.at[slot], grad_ref.at[there, expert, :, cut], done.at[1, slot]),
        ]
        for copy in copies:
            copy.start()
        sent.append(copies)

    score = jnp.zeros((count, 1), f32)
    for at in range(0, width, step):
        cut = slice(at, at + step)
        out = dot_nn(hidden[...], down_w[0, :, cut]) + dot_nn(low_down, down_leave[0, :, cut])
        score = score + jnp.sum(out * grads_in[:, cut].astype(f32), axis=1, keepdims=True)
        back = dot_nt(grad_gate[...], gate_w[0, cut, :]) + dot_nt(grad_up[...], up_w[0, cut, :])
        back = back + dot_nt(grad_low, jnp.concatenate([gate_enter[0, cut, :], up_enter[0, cut, :]], axis=1))
        out = (out * weight).astype(bf16)
        back = back.astype(bf16)
        slot = len(sent) % 2
        if len(sent) >= 2:
            for copy in sent[-2]:
                copy.wait()
        for b in range(blocks):
            out_tile[slot, b] = out[b * cap : (b + 1) * cap]
            back_tile[slot, b] = back[b * cap : (b + 1) * cap]
        send(slot, pl.ds(at, step))
    for b in range(blocks):
        hit = rank_ref[0, b] == slots
        score_ref[0, b] = jnp.sum(jnp.where(hit, score[b * cap : (b + 1) * cap], 0.0), axis=0, keepdims=True)

    def keep(value, row, ref_at):
        piece = value.shape[1] // (line * inner)
        value = value.astype(bf16)
        full_rows[: value.shape[0], : value.shape[1]] = value
        columns = slice(ref_at, ref_at + piece)
        for c in range(line * inner):
            part = slice(c * piece, (c + 1) * piece)
            for q in range(inner):

                @pl.when(place_ref[1, c] == q)
                def _():
                    for at in range(0, value.shape[0], rank):
                        if inner != 2 or q == 0:
                            source = full_rows[at : at + rank, part]
                            target = sums[q].at[place_ref[0, c], 0, slice(row + at, row + at + rank), columns]
                            if pl.num_programs(1) > 1:
                                old = jnp.where(turn > 0, target[...].astype(f32), 0.0)
                                source = (old + source.astype(f32)).astype(bf16)
                            target[...] = source
                            continue
                        for d in range(docs):
                            there = pl.ds(pl.multiple_of(at + scal_ref[1 + docs + d] * RANK, RANK), RANK)
                            source = full_rows[there, part]
                            for d2 in range(d):
                                repeated = scal_ref[1 + docs + d2] == scal_ref[1 + docs + d]
                                source = jnp.where(repeated, jnp.zeros_like(source), source)
                            to = ((row + at) // rank * docs + d) * RANK
                            target = sums[q].at[place_ref[0, c], 0, slice(to, to + RANK), columns]
                            if pl.num_programs(1) > 1:
                                old = jnp.where(turn > 0, target[...].astype(f32), 0.0)
                                source = (old + source.astype(f32)).astype(bf16)
                            target[...] = source

    wide = width // (line * inner)
    keep(dot_tn(grad_low, rows_in[...]), 0, 0)
    keep(dot_tn((low_down.astype(f32) * weight).astype(bf16), grads_in[...]), 2 * rank, 0)
    keep(dot_tn(low_gate, grad_gate[...]), 0, wide)
    keep(dot_tn(low_up, grad_up[...]), rank, wide)
    keep(dot_tn(grad_low_down, hidden[...]), 2 * rank, wide)
    for copies in sent[-2:]:
        for copy in copies:
            copy.wait()


def run_experts(docs, scal, ranks, grads, back, low_back, route, route_enter, route_leave, ahead, normed, place, inner, *weights):
    experts, members, _, local = ranks.shape
    width = grads.shape[2]
    ff = back.shape[2]
    low = SETS * RANK
    blocks = min(members, 4)
    turns = members // blocks
    packs = place.shape[1]
    line = packs // inner
    bf16 = jnp.bfloat16
    count = blocks * CAP
    tile = min(512, width)
    by_turn = lambda e, r: (e, r, 0, 0)
    rows = lambda wide: pl.BlockSpec((1, count, wide), lambda e, r: (e, r, 0))
    half = count // 2
    back_rows = lambda wide: pl.BlockSpec((1, half, wide), lambda e, r: (e, 1, 0)) if ahead else rows(wide)
    once = lambda wide: [pl.BlockSpec((local, wide), lambda e, r: (r, 0), pipeline_mode=pl.Buffered(1))] * blocks
    per_expert = lambda value: pl.BlockSpec((1,) + value.shape[1:], lambda e, r: (e, 0, 0))
    packed = docs * RANK if inner == 2 else low
    sums = [jax.ShapeDtypeStruct((line, experts, 3 * (packed if q else low), (width + ff) // packs), bf16) for q in range(inner)]
    rows_out = jax.ShapeDtypeStruct((members, experts, CAP, width), bf16)
    return pl.pallas_call(
        functools.partial(expert_kernel, line, docs, len(ahead)),
        grid=(experts, turns),
        out_shape=(rows_out, rows_out, jax.ShapeDtypeStruct(ranks.shape, jnp.float32), *sums),
        in_specs=[full(SMEM), pl.BlockSpec((1, blocks, 1, local), by_turn), rows(width), back_rows(ff), back_rows(low)]
        + [full()] * 3
        + [pl.BlockSpec((1,) + value.shape[1:], lambda e, r: (e, 0, 0)) for value in ahead]
        + once(width + low)
        + [per_expert(value) for value in weights]
        + [full(SMEM)],
        out_specs=(full(pl.ANY), full(pl.ANY), pl.BlockSpec((1, blocks, 1, local), by_turn))
        + tuple(pl.BlockSpec((line, 1) + value.shape[2:], lambda e, r: (0, e, 0, 0)) for value in sums),
        scratch_shapes=[
            pltpu.VMEM((count, width), bf16),
            pltpu.VMEM((count, ff), bf16),
            pltpu.VMEM((count, ff), bf16),
            pltpu.VMEM((count, ff), bf16),
            pltpu.VMEM((count, low), jnp.float32),
            pltpu.VMEM((2, blocks, CAP, tile), bf16),
            pltpu.VMEM((2, blocks, CAP, tile), bf16),
            pltpu.SemaphoreType.DMA((2, 2)),
            pltpu.VMEM((2 * low, width), bf16),
            pltpu.VMEM((blocks, EXPERTS, local), jnp.float32),
        ],
        compiler_params=params(),
        cost_estimate=cost(2 * experts * members * CAP * (width * ff * 5 + 9 * low * (width + ff)), 60_000_000),
        name="experts",
    )(scal, ranks, grads, back, low_back, route, route_enter, route_leave, *ahead, *by_block(normed, blocks), *weights, place)


def mix(rank_ref, rows_ref, pick_ref, step):
    experts, cap, local = (rows_ref.shape[1], rows_ref.shape[2], rank_ref.shape[3])

    @pl.when(step == 0)
    def _():
        slots = lax.broadcasted_iota(jnp.int32, (cap, local), 0).astype(jnp.float32)
        pick = jnp.concatenate([(rank_ref[e, 0] == slots).astype(jnp.float32) for e in range(experts)], axis=0)
        pick_ref[...] = pick.T.astype(jnp.bfloat16)

    rows = jnp.concatenate([rows_ref[0, e] for e in range(experts)], axis=0)
    return dot_nn(pick_ref[...], rows)


def mix_grads(scal_ref, rank_ref, score_ref, rows_ref, added_ref, back_ref, pick_ref, step):
    f32, bf16 = (jnp.float32, jnp.bfloat16)
    experts, local = (rows_ref.shape[1], rank_ref.shape[3])
    piece, low = (rows_ref.shape[3], SETS * RANK)
    width = back_ref.shape[1] - low
    columns = pl.ds(pl.multiple_of(step * piece, 128), piece)
    value = mix(rank_ref, rows_ref, pick_ref, step)
    if added_ref is not None:
        value = value + added_ref[:, columns].astype(f32)
    back_ref[:, columns] = value.astype(bf16)

    @pl.when(step == 0)
    def _():
        lines = lax.broadcasted_iota(jnp.int32, (low, local), 0)
        table = jnp.zeros((low, local), f32)
        for e in range(experts):
            score = score_ref[e, 0]
            whole = score.astype(bf16).astype(f32)
            at = scal_ref[0] * experts + e
            table = jnp.where(lines == at, whole, table)
            table = jnp.where(lines == at + EXPERTS, score - whole, table)
        table = table.T
        if added_ref is not None:
            table = table + added_ref[:, width:].astype(f32)
        back_ref[:, width:] = table.astype(bf16)


def combine_kernel(added, scal_ref, rank_ref, score_ref, rows_ref, *refs):
    back_ref, pick_ref = refs[-2:]
    mix_grads(scal_ref, rank_ref, score_ref, rows_ref, refs[0] if added else None, back_ref, pick_ref, pl.program_id(0))


def combine(scal, ranks, scores, rows, place, addend, *deps):
    experts, members, _, local = ranks.shape
    width = rows.shape[3]
    piece = width // 2
    low = SETS * RANK
    one = pl.BlockSpec((experts, 1, 1, local), lambda n: (0, place, 0, 0))
    more = () if addend is None else (addend,)
    return pl.pallas_call(
        functools.partial(combine_kernel, addend is not None),
        grid=(2,),
        out_shape=jax.ShapeDtypeStruct((local, width + low), jnp.bfloat16),
        in_specs=[full(SMEM), one, one, pl.BlockSpec((1, experts, CAP, piece), lambda n: (place, 0, 0, n))]
        + [full()] * len(more)
        + [full(pl.ANY)] * len(deps),
        out_specs=full(),
        scratch_shapes=[pltpu.VMEM((local, experts * CAP), jnp.bfloat16)],
        compiler_params=params(),
        cost_estimate=cost(2 * local * experts * CAP * width, 2 * experts * CAP * width),
        name="combine",
    )(scal, ranks, scores, rows, *more, *deps)


def combine_last_kernel(scal_ref, rank_ref, score_ref, grads_ref, rows_ref, added_ref, *refs):
    members = pl.num_programs(0)
    out_refs, (back_ref, pick_ref) = (refs[-2 - members : -2], refs[-2:])
    block, step = (pl.program_id(0), pl.program_id(1))
    piece = rows_ref.shape[3]
    columns = pl.ds(pl.multiple_of(step * piece, 128), piece)
    value = mix(rank_ref, rows_ref, pick_ref, step).astype(jnp.bfloat16)
    for b in range(members):

        @pl.when(block == b)
        def _():
            out_refs[b][:, columns] = value

    @pl.when(block == 0)
    def _():
        mix_grads(scal_ref, rank_ref, score_ref, grads_ref, added_ref, back_ref, pick_ref, step)


def combine_last(scal, ranks, scores, grads, mixed, addend, *deps):
    experts, members, _, local = ranks.shape
    width = grads.shape[3]
    piece = width // 2
    low = SETS * RANK
    out = jax.ShapeDtypeStruct((local, width), jnp.bfloat16)
    one = pl.BlockSpec((experts, 1, 1, local), lambda b, n: (0, b, 0, 0))
    first = lambda b, n: (0, 0, 0, jnp.where(b == 0, n, 1))
    return pl.pallas_call(
        lambda *refs: combine_last_kernel(*refs[:6], *refs[6 + len(deps) :]),
        grid=(members, 2),
        out_shape=(out,) * members + (jax.ShapeDtypeStruct((local, width + low), jnp.bfloat16),),
        in_specs=[full(SMEM), one, one]
        + [pl.BlockSpec((1, experts, CAP, piece), first), pl.BlockSpec((1, experts, CAP, piece), lambda b, n: (b, 0, 0, n))]
        + [full()]
        + [full(pl.ANY)] * len(deps),
        out_specs=(full(),) * (members + 1),
        scratch_shapes=[pltpu.VMEM((local, experts * CAP), jnp.bfloat16)],
        compiler_params=params(),
        cost_estimate=cost(2 * 5 * local * experts * CAP * width, 10 * experts * CAP * width),
        name="combine_last",
    )(scal, ranks, scores, grads, mixed, addend, *deps)


def per_device(
    tokens,
    cotangent,
    pack_order,
    doc_lengths,
    doc_sets,
    routes,
    attention_gain,
    query_gain,
    key_gain,
    feed_gain,
    qkv_weight,
    out_weight,
    router_weight,
    gate_weight,
    up_weight,
    down_weight,
    qkv_enter,
    qkv_leave,
    out_enter,
    out_leave,
    router_enter,
    router_leave,
    gate_enter,
    gate_leave,
    up_enter,
    up_leave,
    down_enter,
    down_leave,
):
    members = lax.axis_size("ep")
    packs = lax.axis_size("grp")
    pack = lax.axis_index("grp")
    member = lax.axis_index("ep")
    local, width = tokens.shape
    slice_width = width // members
    experts_here = gate_weight.shape[0]
    own_cols = member * slice_width
    count = members // 2
    low = SETS * RANK
    f32, bf16 = (jnp.float32, jnp.bfloat16)
    slot = jnp.sum(jnp.where(pack_order == pack, jnp.arange(packs, dtype=jnp.int32), 0))
    named = jnp.sum(jnp.left_shift(jnp.int32(1), routes), axis=1)
    documents_here = jnp.concatenate([doc_lengths[0], doc_sets[0]])
    info = jnp.concatenate([named, jnp.pad(documents_here, (0, 128 - documents_here.shape[0]))])
    info = jnp.stack(gather_parts(info, "grp"))
    other = jnp.sum(jnp.where(pack_order == pack ^ 1, jnp.arange(packs, dtype=jnp.int32), 0))
    other = lax.dynamic_index_in_dim(info, other ^ pack, 0, keepdims=False)
    info = lax.dynamic_index_in_dim(info, slot ^ pack, 0, keepdims=False)
    blocks = [member ^ j for j in range(members)]
    named = info[:local]
    docs = doc_lengths.shape[1]
    lengths, sets = (info[local : local + docs], info[local + docs : local + 2 * docs])
    ends = jnp.cumsum(lengths)
    starts = ends - lengths
    scal = jnp.concatenate([member[None].astype(jnp.int32), ends, sets, starts])
    gain_one, gain_two = (attention_gain[None], feed_gain[None])
    route, route_leave = (router_weight.T, router_leave.T)
    adapters = (gain_one, qkv_weight, qkv_enter, qkv_leave)
    named_all = named.reshape(1, 1, local)
    named_all = jnp.concatenate([named_all, swap(named_all, "ep", 1)])
    kept = project(docs, 0, scal, gather_near(tokens, "ep"), *adapters, None, named_all)
    token_parts = gather_far(tokens, "ep", kept[4])
    bit = 2
    while bit < members:
        named_all = jnp.concatenate([named_all, swap(named_all, "ep", bit)])
        bit *= 2
    kept = project(docs, 1, scal, token_parts, *adapters, kept)
    normed_all, low_all, projected, values, squares = kept
    late = fence(scal, values)
    ends, starts = (late[1 : 1 + docs], late[1 + 2 * docs :])
    rows = (jnp.stack(blocks)[:, None] * local + jnp.arange(local, dtype=jnp.int32)[None, :]).reshape(-1)
    begin = starts[0]
    for k in range(1, docs):
        begin = jnp.where(rows >= ends[k - 1], starts[k], begin)
    cosine, sine = angles(rows - begin)
    upstream_far = gather_near(swap(fence(cotangent, token_parts[0], named_all), "ep", members // 2), "ep")
    upstream_parts = gather_near(cotangent, "ep") + upstream_far
    squares = sum_relative(squares, "ep", local)
    own_gain = lambda gain: lax.dynamic_slice_in_dim(gain, own_cols, slice_width, 0)
    gains = jnp.stack([own_gain(query_gain), own_gain(key_gain)]).astype(f32)
    queries, keys = prepare(width, projected, squares, gains, cosine, sine, local, upstream_parts[-1], named_all)
    heads = [None] * members

    def attend_place(place, addend, *deps):
        heads[place] = attend(docs, place, local, scal, queries, keys, values, out_weight, out_enter, addend, *deps)
        return heads[place][1], heads[place][2]

    top = members // 2
    outs = reduce_scatter(attend_place, "ep")
    upstream_rows = run_upstream(scal, named_all, upstream_parts, down_weight, down_leave, heads[0][2])
    hidden_state, normed_two, low_router, probs = middle(
        docs, scal, tokens, outs, out_leave, gain_two, route, router_enter, route_leave, upstream_rows[0]
    )

    ranks, _, *backs = upstream_rows
    routers = (route, router_enter, route_leave)
    normed_two_parts = gather_near(normed_two, "ep")
    ahead = ()
    if members <= 4:
        ahead = run_near(
            docs, scal, ranks, *backs, *routers, normed_two_parts, gate_weight, up_weight, gate_enter, gate_leave, up_enter, up_leave,
            down_enter
        )
    normed_two_parts = normed_two_parts + gather_far(normed_two, "ep", *ahead[3:])
    inner = packs // LINE
    chunk_ids = jnp.arange(packs, dtype=jnp.int32)
    place = jnp.stack([(chunk_ids // inner - pack // inner) % LINE, (chunk_ids % inner - pack % inner) % inner])
    mixed_rows, grad_rows, scores, *expert_sums = run_experts(
        docs,
        scal,
        *upstream_rows,
        *routers,
        ahead,
        normed_two_parts,
        place,
        inner,
        gate_weight,
        up_weight,
        down_weight,
        gate_enter,
        gate_leave,
        up_enter,
        up_leave,
        down_enter,
        down_leave,
    )
    mixed = []

    def combine_place(place, addend, *deps):
        if place:
            part = combine(scal, ranks, scores, grad_rows, place, addend, *deps)
        else:
            *parts, part = combine_last(scal, ranks, scores, grad_rows, mixed_rows, addend, *deps)
            mixed.extend(parts)
        return part, part

    grads = reduce_scatter(combine_place, "ep")
    grad_hidden, grad_branch, grad_router_leave = middle_back(
        docs, scal, grads, probs, hidden_state, cotangent, low_router, gain_two, route, router_enter, route_leave
    )
    pair = lambda a, b: (a.astype(f32) + b.astype(f32)).astype(bf16)
    mixed = [pair(mixed[j], swap(mixed[j + 1], "ep", 1)) for j in range(0, members, 2)]
    mixed_near, mixed_far = (scatter_even(mixed[: top // 2], "ep"), scatter_even(mixed[top // 2 :], "ep"))

    inside = (queries, keys, values, out_weight, out_enter, out_leave)

    def attend_half_back(half, branch, before, *deps):
        part = slice(half * count, (half + 1) * count)
        atts, logs = ([head[i] for head in heads[part]] for i in (0, 2))
        return attend_back(docs, half, scal, *inside, branch, atts, logs, normed_two_parts[part], before, *deps)

    near = attend_half_back(0, gather_near(grad_branch, "ep"), ())
    branch_far = gather_far(grad_branch, "ep", near[6])
    other_sets = other[local + docs : local + 2 * docs]
    line_sums = sum_experts(docs, other_sets, expert_sums, near[6])
    far = attend_half_back(1, branch_far, near[1:6], line_sums[0])
    mixed_got = swap(fence(mixed_far, branch_far[0]), "ep", top)
    grad_keys, grad_values, *low_grads = far[1:6]
    terms = jnp.concatenate([jnp.concatenate([near[6], far[6]], axis=1), far[7]])
    line = LineSum(line_sums, "grp", LINE, inner)
    got = line.send(1)
    terms = sum_relative(fence(terms, *got, mixed_got), "ep", local)
    line.add(1, got)
    leave_rows = low // members
    leave_parts = jnp.stack([lax.dynamic_slice_in_dim(grad_router_leave, b * leave_rows, leave_rows, 1) for b in blocks])
    leave_parts = jnp.pad(leave_parts.astype(bf16), ((0, 0), (0, 0), (0, slice_width - leave_rows)))
    shared = (projected, squares, terms, gains, cosine, sine, normed_all, low_all, qkv_weight, qkv_enter, qkv_leave)
    ready = line.ready(2)
    *far_parts, enter_sums, leave_sums, projected_grads, low_grad = project_back(
        docs, local, scal, near[0], far[0], grad_keys, grad_values, *shared, leave_parts, *ready
    )
    got = line.send(2, ready)
    *far_parts, enter_sums, leave_sums = (fence(value, *got) for value in (*far_parts, enter_sums, leave_sums))
    input_far = scatter_even([pair(far_parts[j], swap(far_parts[j + 1], "ep", 1)) for j in range(0, count, 2)], "ep")
    input_got = swap(input_far, "ep", top)
    line.add(2, [fence(value, input_far) for value in got])
    ready = line.ready(3)
    enter_sums = fence(enter_sums, input_far)
    enter_sums = [pair(enter_sums[j], swap(enter_sums[j + 1], "ep", 1)) for j in range(0, members, 2)]
    enter_far = scatter_even(enter_sums[top // 2 :], "ep")
    near_parts = project_near(local, projected_grads, low_grad, qkv_weight, qkv_enter, input_far, *ready, enter_far)
    if count == 2:
        inputs = (near_parts[0], swap(near_parts[1], "ep", 1), input_got)
    else:
        inputs = [pair(near_parts[j], swap(near_parts[j + 1], "ep", 1)) for j in range(0, count, 2)]
        inputs = (scatter_even(inputs, "ep"), input_got)
    grad_input = finish(inputs, grad_hidden, tokens, gain_one)
    layer_out = (hidden_state + (mixed_near.astype(f32) + mixed_got.astype(f32))).astype(bf16)

    got = [fence(value, input_got) for value in line.send(3, ready)]
    line.add(3, got)
    expert_sum = line.total[0]
    by_rows = lambda value: value.astype(bf16).reshape(-1, packs, value.shape[-2] // packs, slice_width).transpose(1, 0, 2, 3)
    joined = jnp.concatenate([by_rows(value) for value in (*low_grads, leave_sums)], axis=1)
    joined = sum_packs(by_place(fence(joined, input_far)), input_got)
    enter_far = swap(enter_far, "ep", top)
    enter_sum = fence(pair(scatter_even(enter_sums[: top // 2], "ep"), enter_far), input_got, *got, joined)
    enter_chunks = by_rows(enter_sum[: 3 * low].reshape(3, low, slice_width)).reshape(packs, -1, slice_width)
    leave_chunks = by_rows(enter_sum[3 * low :]).reshape(packs, -1, slice_width)
    enter_sum = sum_packs(by_place(jnp.concatenate([enter_chunks, leave_chunks], axis=1)), last=grad_input)
    enter_rows = 3 * low // packs
    wide = width // packs
    turn = lambda value: jnp.swapaxes(value, -1, -2)
    return (
        layer_out,
        grad_input,
        turn(enter_sum[:enter_rows].reshape(3, -1, slice_width)),
        joined[3:],
        turn(joined[0]),
        joined[1],
        turn(joined[2]),
        turn(enter_sum[enter_rows:, :leave_rows]),
        turn(expert_sum[:, :low, :wide]),
        expert_sum[:, :low, wide:],
        turn(expert_sum[:, low : 2 * low, :wide]),
        expert_sum[:, low : 2 * low, wide:],
        turn(expert_sum[:, 2 * low :, wide:]),
        expert_sum[:, 2 * low :, :wide],
    )


def solution(mesh):
    in_specs = (
        P(("grp", "ep"), None),
        P(("grp", "ep"), None),
        P(),
        P("grp", None),
        P("grp", None),
        P(("grp", "ep"), None),
        P(),
        P(),
        P(),
        P(),
        P(None, None, "ep"),
        P("ep", None),
        P(),
        P("ep", None, None),
        P("ep", None, None),
        P("ep", None, None),
        P(),
        P(None, None, "ep"),
        P("ep", None),
        P(),
        P(),
        P(),
        P("ep", None, None),
        P("ep", None, None),
        P("ep", None, None),
        P("ep", None, None),
        P("ep", None, None),
        P("ep", None, None),
    )
    out_specs = (
        P(("grp", "ep"), None),
        P(("grp", "ep"), None),
        P(None, "ep", "grp"),
        P(None, "grp", "ep"),
        P("ep", "grp"),
        P("grp", "ep"),
        P("ep", "grp"),
        P("ep", "grp"),
        P("ep", "grp", None),
        P("ep", None, "grp"),
        P("ep", "grp", None),
        P("ep", None, "grp"),
        P("ep", "grp", None),
        P("ep", None, "grp"),
    )
    return jax.shard_map(
        per_device, mesh=mesh, in_specs=in_specs, out_specs=out_specs, check_vma=False
    )
```

```python
import functools

import jax
import jax.numpy as jnp
from jax import lax
from jax.experimental import pallas as pl
from jax.experimental.pallas import tpu as pltpu
from jax.sharding import PartitionSpec as P

HEAD_DIM = 128
EXPERTS = 16
TOP = 8
SETS = 8
RANK = 16
CAP = 144


EPS = 1e-05
SCALE = 2.0
THETA = 10000.0
NEG = -1e30


def rms_scale(value):
    return lax.rsqrt(jnp.mean(value * value, axis=-1, keepdims=True) + EPS)


def angles(position):
    half = HEAD_DIM // 2
    freq = THETA ** (-(jnp.arange(half, dtype=jnp.float32) * 2.0) / HEAD_DIM)
    phase = position.astype(jnp.float32)[:, None] * freq[None, :]
    cosine, sine = (jnp.cos(phase), jnp.sin(phase))
    return (jnp.concatenate([cosine, cosine], axis=-1), jnp.concatenate([-sine, sine], axis=-1))


LINE = 4
VMEM = 62 * 1024 * 1024


def swap(value, axis, bit):
    count = lax.axis_size(axis)
    return lax.ppermute(value, axis, [(i, i ^ bit) for i in range(count)])


def gather_parts(value, axis, bit=None):
    parts, bit = ({0: value}, (bit or lax.axis_size(axis)) // 2)
    while bit >= 1:
        for j in list(parts):
            parts[j ^ bit] = swap(parts[j], axis, bit)
        bit //= 2
    return [parts[j] for j in range(len(parts))]


def gather_near(value, axis):
    return gather_parts(value, axis, lax.axis_size(axis) // 2)


def gather_far(value, axis, *deps):
    far = swap(value, axis, lax.axis_size(axis) // 2)
    return gather_near(fence(far, *deps) if deps else far, axis)


def scatter_even(parts, axis):
    parts, bit = ({2 * i: part for i, part in enumerate(parts)}, 2)
    while bit < lax.axis_size(axis) // 2:
        got = {j: swap(parts[j ^ bit], axis, bit) for j in parts if not j & bit}
        parts = {j: (parts[j].astype(jnp.float32) + got[j].astype(jnp.float32)).astype(jnp.bfloat16) for j in got}
        bit *= 2
    return parts[0]


def reduce_scatter(make, axis, *deps):
    members = lax.axis_size(axis)
    top = members // 2
    odd = {}
    for j in range(members - 1, 0, -2):
        part, mark = make(j, None, *deps)
        odd[j - 1], deps = (swap(part, axis, 1), (mark,))
    sums = {}
    for j in range(members - 2, top - 1, -2):
        sums[j], mark = make(j, odd[j], *deps)
        deps = (mark,)
    far = scatter_even([sums[j] for j in range(top, members, 2)], axis)
    deps = (far,)
    for j in range(top - 2, -1, -2):
        sums[j], mark = make(j, odd[j], *deps)
        deps = (mark,)
    return scatter_even([sums[j] for j in range(0, top, 2)], axis), swap(far, axis, top)


def fence_kernel(*refs):
    pass


def fence(value, *deps):
    return pl.pallas_call(
        fence_kernel,
        out_shape=jax.ShapeDtypeStruct(value.shape, value.dtype),
        in_specs=[pl.BlockSpec(memory_space=pl.ANY)] * (1 + len(deps)),
        out_specs=pl.BlockSpec(memory_space=pl.ANY),
        input_output_aliases={0: 0},
        name="fence",
    )(value, *deps)


def sum_relative(value, axis, local):
    count, bit = (lax.axis_size(axis), 1)
    while bit < count:
        got = swap(value, axis, bit)
        got = [got[..., (j ^ bit) * local : ((j ^ bit) + 1) * local] for j in range(count)]
        value = value + jnp.concatenate(got, axis=-1)
        bit *= 2
    return value


class LineSum:
    def __init__(self, parts, axis, length, stride):
        count = lax.axis_size(axis)
        place = lambda i: i // stride % length
        self.axis, self.length, self.at = (axis, length, place(lax.axis_index(axis)))
        self.up = [(i, i + stride) for i in range(count) if place(i) + 1 < length]
        self.down = [(i + stride, i) for i in range(count) if place(i) + 1 < length]
        self.total = [part.astype(jnp.float32) for part in parts]

    def ready(self, step):
        return [self.total[p].astype(jnp.bfloat16) for p in (self.length - step, step)]

    def send(self, step, ready=None):
        up, down = ready or self.ready(step)
        return lax.ppermute(up, self.axis, self.up), lax.ppermute(down, self.axis, self.down)

    def add(self, step, got):
        left = self.length - step - 1
        below, above = (value.astype(jnp.float32) for value in got)
        good = (self.at >= 1) & (self.at + left < self.length)
        self.total[left] = self.total[left] + jnp.where(good, below, 0.0)
        good = (self.at + 1 < self.length) & (self.at - left >= 0)
        high = (step + 1) % self.length
        self.total[high] = self.total[high] + jnp.where(good, above, 0.0)


def line_scatter(parts, axis, length, stride):
    line = LineSum(parts, axis, length, stride)
    for step in range(1, length):
        line.add(step, line.send(step))
    return line.total[0]


def direct_scatter(parts, axis, length, stride, *deps):
    count = lax.axis_size(axis)
    got = []
    for p in range(1, length):
        moves = [(i, i + ((i // stride % length + p) % length - i // stride % length) * stride) for i in range(count)]
        got.append(lax.ppermute(parts[p], axis, moves))
    total = (fence(parts[0], *deps) if deps else parts[0]).astype(jnp.float32)
    for value in got:
        total = total + value.astype(jnp.float32)
    return total


def by_place(chunks):
    inner = chunks.shape[0] // LINE
    index = lax.axis_index("grp")
    parts = []
    for q in range(inner):
        group = []
        for p in range(LINE):
            chunk = (index // inner + p) % LINE * inner + (index % inner + q) % inner
            group.append(lax.dynamic_index_in_dim(chunks, chunk, 0, keepdims=False))
        parts.append(jnp.stack(group))
    return parts


def sum_packs(parts, *deps, last=None):
    inner = len(parts)
    mine = direct_scatter(parts, "grp", inner, 1).astype(jnp.bfloat16) if inner > 1 else parts[0]
    if last is not None:
        mine = fence(mine, last)
    return direct_scatter([mine[p] for p in range(LINE)], "grp", LINE, inner, *deps)


def widen_kernel(docs, line, sets_ref, kept_ref, got_ref, *refs):
    f32 = jnp.float32
    out_refs = refs[-line:]
    experts, rows = got_ref.shape[1:3]
    for p in range(line):
        out_refs[p][...] = kept_ref[p]
        for e in range(experts):
            for g in range(rows // (docs * RANK)):
                for d in range(docs):
                    there = pl.ds(pl.multiple_of(g * SETS * RANK + sets_ref[d] * RANK, RANK), RANK)
                    piece = got_ref[p, e, (g * docs + d) * RANK : (g * docs + d + 1) * RANK]
                    out_refs[p][e, there] = (out_refs[p][e, there].astype(f32) + piece.astype(f32)).astype(kept_ref.dtype)


def widen(docs, sets, kept, got, *deps):
    line = kept.shape[0]
    return pl.pallas_call(
        functools.partial(widen_kernel, docs, line),
        out_shape=(jax.ShapeDtypeStruct(kept.shape[1:], kept.dtype),) * line,
        in_specs=[full(SMEM), full(), full()] + [full(pl.ANY)] * len(deps),
        out_specs=(full(),) * line,
        compiler_params=params(),
        name="widen",
    )(sets, kept, got, *deps)


def sum_experts(docs, sets, parts, *deps):
    inner = len(parts)
    if inner == 2:
        return widen(docs, sets, parts[0], swap(parts[1], "grp", 1), *deps)
    mine = line_scatter(parts, "grp", inner, 1).astype(jnp.bfloat16) if inner > 1 else parts[0]
    return [mine[p] for p in range(LINE)]


def dot_nn(a, b):
    return jnp.dot(a, b, preferred_element_type=jnp.float32)


def dot_nt(a, b):
    return lax.dot_general(a, b, (((1,), (1,)), ((), ())), preferred_element_type=jnp.float32)


def dot_tn(a, b):
    return lax.dot_general(a, b, (((0,), (0,)), ((), ())), preferred_element_type=jnp.float32)


def column(row):
    return jnp.broadcast_to(row, (128, row.shape[1])).T


def as_row(value):
    return jnp.broadcast_to(value, (value.shape[0], 128)).T[:1]


def doc_sum(scal_ref, rows, docs, at):
    value = jnp.full(rows.shape, scal_ref[at], jnp.int32)
    for k in range(1, docs):
        value = jnp.where(rows >= scal_ref[k], scal_ref[at + k], value)
    return value


def block_marks(scal_ref, docs, block, local):
    rows = block * local + lax.broadcasted_iota(jnp.int32, (local, SETS * RANK), 0)
    lanes = lax.broadcasted_iota(jnp.int32, (local, SETS * RANK), 1) // RANK
    return (doc_sum(scal_ref, rows, docs, 1 + docs) == lanes).astype(jnp.float32)


def params(**kinds):
    return pltpu.CompilerParams(vmem_limit_bytes=VMEM, **kinds)


def cost(flops, moved, exps=0):
    return pl.CostEstimate(flops=int(flops) // 8, bytes_accessed=int(moved) // 8, transcendentals=int(exps) // 8)


def full(memory=pltpu.VMEM):
    return pl.BlockSpec(memory_space=memory)


SMEM = pltpu.SMEM


def project_kernel(docs, half, parts, scal_ref, *refs):
    f32, bf16 = (jnp.float32, jnp.bfloat16)
    x_refs, (gain_ref, w_ref, enter_ref, leave_ref) = (refs[:parts], refs[parts : parts + 4])
    normed_ref, low_ref, p_ref, v_ref, square_ref = refs[-5:]
    local = x_refs[0].shape[0]
    rank = SETS * RANK
    which = pl.program_id(0)

    @pl.when(which == 0)
    def _():
        enter = jnp.concatenate([enter_ref[i] for i in range(3)], axis=1)
        for b in range(parts):
            x = x_refs[b][...].astype(f32)
            here = slice(b * local, (b + 1) * local)
            normed_ref[here] = (x * rms_scale(x) * gain_ref[...].astype(f32)).astype(bf16)
            mark = block_marks(scal_ref, docs, scal_ref[0] ^ (half * parts + b), local)
            low = dot_nn(normed_ref[here], enter)
            for i in range(3):
                low_ref[i, here] = (low[:, i * rank : (i + 1) * rank] * mark).astype(bf16) * SCALE

    value = dot_nn(normed_ref[...], w_ref[0]) + dot_nn(low_ref[which], leave_ref[0])

    @pl.when(which < 2)
    def _():
        p_ref[0] = value
        square_ref[pl.ds(which, 1)] = as_row(jnp.sum(value * value, axis=1, keepdims=True))

    @pl.when(which == 2)
    def _():
        v_ref[...] = value.astype(bf16)


def project(docs, half, scal, x_parts, gain, weight, enter, leave, kept, *deps):
    parts = len(x_parts)
    local, width = x_parts[0].shape
    slice_width = weight.shape[2]
    rows, rank = (parts * local, enter.shape[2])
    f32, bf16 = (jnp.float32, jnp.bfloat16)
    outs = (
        jax.ShapeDtypeStruct((2 * rows, width), bf16),
        jax.ShapeDtypeStruct((3, 2 * rows, rank), bf16),
        jax.ShapeDtypeStruct((2, 2 * rows, slice_width), f32),
        jax.ShapeDtypeStruct((2 * rows, slice_width), bf16),
        jax.ShapeDtypeStruct((2, 2 * rows), f32),
    )
    extra = () if kept is None else kept
    first = 5 + parts
    return pl.pallas_call(
        functools.partial(project_kernel, docs, half, parts),
        grid=(3,),
        out_shape=outs,
        in_specs=[full(SMEM)]
        + [full()] * parts
        + [
            full(),
            pl.BlockSpec((1, width, slice_width), lambda i: (i, 0, 0)),
            full(),
            pl.BlockSpec((1, rank, slice_width), lambda i: (i, 0, 0)),
        ]
        + [full(pl.ANY)] * (len(extra) + len(deps)),
        out_specs=(
            pl.BlockSpec((rows, width), lambda i: (half, 0)),
            pl.BlockSpec((3, rows, rank), lambda i: (0, half, 0)),
            pl.BlockSpec((1, rows, slice_width), lambda i: (jnp.minimum(i, 1), half, 0)),
            pl.BlockSpec((rows, slice_width), lambda i: (half, 0)),
            pl.BlockSpec((2, rows), lambda i: (0, half)),
        ),
        input_output_aliases={first + i: i for i in range(len(extra))},
        compiler_params=params(),
        cost_estimate=cost(2 * rows * width * (3 * slice_width + 3 * rank), 14_000_000),
        name="project",
    )(scal, *x_parts, gain, weight, enter, leave, *extra, *deps)


def prepare_kernel(width, p_ref, square_ref, gains_ref, cos_ref, sin_ref, q_ref, k_ref):
    inverse = lax.rsqrt(square_ref[...] / width + EPS)
    for i, out_ref in ((0, q_ref), (1, k_ref)):
        scale = column(inverse[i : i + 1])
        for at in range(0, p_ref.shape[2], HEAD_DIM):
            cut = slice(at, at + HEAD_DIM)
            value = p_ref[i, :, cut] * scale * gains_ref[i : i + 1, cut]
            value = value * cos_ref[...] + pltpu.roll(value, HEAD_DIM // 2, 1) * sin_ref[...]
            out_ref[:, cut] = value.astype(jnp.bfloat16)


def prepare(width, p, squares, gains, cosine, sine, local, *deps):
    _, rows, slice_width = p.shape
    out = jax.ShapeDtypeStruct((rows, slice_width), jnp.bfloat16)
    return pl.pallas_call(
        lambda *refs: prepare_kernel(width, *refs[:5], *refs[5 + len(deps) :]),
        grid=(rows // local,),
        out_shape=(out, out),
        in_specs=[
            pl.BlockSpec((2, local, slice_width), lambda i: (0, i, 0)),
            pl.BlockSpec((2, local), lambda i: (0, i)),
            full(),
            pl.BlockSpec((local, HEAD_DIM), lambda i: (i, 0)),
            pl.BlockSpec((local, HEAD_DIM), lambda i: (i, 0)),
        ]
        + [full(pl.ANY)] * len(deps),
        out_specs=(pl.BlockSpec((local, slice_width), lambda i: (i, 0)),) * 2,
        compiler_params=params(),
        cost_estimate=cost(10 * p.size, 8 * p.size),
        name="prepare",
    )(p, squares, gains, cosine, sine, *deps)


def attend_kernel(docs, place, local, added, scal_ref, q_ref, k_ref, v_ref, w_ref, enter_ref, *refs):
    f32, bf16 = (jnp.float32, jnp.bfloat16)
    att_ref, part_ref, log_ref = refs[-3:]
    members = q_ref.shape[0] // local
    heads = q_ref.shape[1] // HEAD_DIM
    width = w_ref.shape[1]
    member = scal_ref[0]
    block = member ^ place
    queries = slice(place * local, (place + 1) * local)

    def run(last):
        rows = last * local + lax.broadcasted_iota(jnp.int32, (local, local), 0)
        begin = doc_sum(scal_ref, rows, docs, 1 + 2 * docs)
        lanes = lax.broadcasted_iota(jnp.int32, (local, local), 1)
        logs = jnp.zeros((8, local), f32)
        for h in range(heads):
            cut = slice(h * HEAD_DIM, (h + 1) * HEAD_DIM)
            query = q_ref[queries, cut]
            scores, values = ([], [])
            for b in range(last + 1):
                there = pl.ds(pl.multiple_of((member ^ b) * local, local), local)
                score = dot_nt(query, k_ref[there, cut]) * HEAD_DIM ** (-0.5)
                good = lanes + b * local >= begin
                if b == last:
                    good = good & (lanes + b * local <= rows)
                scores.append(jnp.where(good, score, NEG))
                values.append(v_ref[there, cut])
            peak = functools.reduce(jnp.maximum, [jnp.max(score, axis=1, keepdims=True) for score in scores])
            expo = [jnp.exp(score - peak) for score in scores]
            total = functools.reduce(jnp.add, [jnp.sum(e, axis=1, keepdims=True) for e in expo])
            share = 1.0 / total
            mixed = functools.reduce(jnp.add, [dot_nn((e * share).astype(bf16), v) for e, v in zip(expo, values)])
            att_ref[:, cut] = mixed.astype(bf16)
            head_row = lax.broadcasted_iota(jnp.int32, (8, local), 0) == h
            logs = jnp.where(head_row, as_row(peak + jnp.log(total)), logs)
        log_ref[...] = logs

    for last in range(members):
        pl.when(block == last)(functools.partial(run, last))
    for cut, value_ref in ((slice(0, width), w_ref), (slice(width, None), enter_ref)):
        value = dot_nn(att_ref[...], value_ref[...])
        if added:
            value = value + refs[0][:, cut].astype(f32)
        part_ref[:, cut] = value.astype(bf16)


def attend(docs, place, local, scal, q, k, v, weight, enter, addend, *deps):
    slice_width = q.shape[1]
    width, rank = (weight.shape[1], enter.shape[1])
    f32, bf16 = (jnp.float32, jnp.bfloat16)
    assert slice_width // HEAD_DIM <= 8
    return pl.pallas_call(
        functools.partial(attend_kernel, docs, place, local, addend is not None),
        out_shape=(
            jax.ShapeDtypeStruct((local, slice_width), bf16),
            jax.ShapeDtypeStruct((local, width + rank), bf16),
            jax.ShapeDtypeStruct((8, local), f32),
        ),
        in_specs=[full(SMEM)] + [full()] * (5 + (addend is not None)) + [full(pl.ANY)] * len(deps),
        out_specs=(full(),) * 3,
        compiler_params=params(),
        cost_estimate=cost(2_200_000_000, 4_000_000, 350_000),
        name="attend",
    )(scal, q, k, v, weight, enter, *(() if addend is None else (addend,)), *deps)


def middle_kernel(
    docs, scal_ref, x_ref, oa_ref, ob_ref, leave_ref, gain_ref, route_ref, route_enter, route_leave, h_ref, normed_ref, route_low, probs_ref
):
    f32, bf16 = (jnp.float32, jnp.bfloat16)
    width = x_ref.shape[1]
    mark = block_marks(scal_ref, docs, scal_ref[0], x_ref.shape[0])
    low = ((oa_ref[:, width:].astype(f32) + ob_ref[:, width:].astype(f32)) * mark).astype(bf16)
    normed_ref[:, width:] = low
    h = x_ref[...].astype(f32) + (oa_ref[:, :width].astype(f32) + ob_ref[:, :width].astype(f32))
    h = h + SCALE * dot_nn(low, leave_ref[...])
    h_ref[...] = h
    normed = (h * rms_scale(h) * gain_ref[...].astype(f32)).astype(bf16)
    normed_ref[:, :width] = normed
    low, probs = router(normed, mark, route_ref, route_enter, route_leave)
    route_low[...] = low
    probs_ref[...] = probs


def router(normed, mark, route_ref, route_enter, route_leave):
    low = (dot_nn(normed, route_enter[...]) * mark).astype(jnp.bfloat16)
    logits = dot_nt(route_ref[...], normed) + SCALE * dot_nt(route_leave[...], low)
    expo = jnp.exp(logits - jnp.max(logits, axis=0, keepdims=True))
    return low, expo / jnp.sum(expo, axis=0, keepdims=True)


def middle(docs, scal, x, outs, leave, gain, route, route_enter, route_leave, *deps):
    local, width = x.shape
    rank = leave.shape[0]
    f32, bf16 = (jnp.float32, jnp.bfloat16)
    return pl.pallas_call(
        lambda *refs: middle_kernel(docs, *refs[:9], *refs[9 + len(deps) :]),
        out_shape=(
            jax.ShapeDtypeStruct((local, width), f32),
            jax.ShapeDtypeStruct((local, width + rank), bf16),
            jax.ShapeDtypeStruct((local, rank), bf16),
            jax.ShapeDtypeStruct((route.shape[0], local), f32),
        ),
        in_specs=[full(SMEM)] + [full()] * 8 + [full(pl.ANY)] * len(deps),
        out_specs=(full(),) * 4,
        compiler_params=params(),
        cost_estimate=cost(4 * local * width * rank, 8_000_000),
        name="middle",
    )(scal, x, *outs, leave, gain, route, route_enter, route_leave, *deps)


def middle_back_kernel(
    docs, scal_ref, ga_ref, gb_ref, probs_ref, h_ref, up_ref, route_low, gain_ref, route_ref, route_enter, route_leave, dh_ref, dhb_ref, leave_ref
):
    f32, bf16 = (jnp.float32, jnp.bfloat16)
    width = h_ref.shape[1]
    mark = block_marks(scal_ref, docs, scal_ref[0], h_ref.shape[0])
    probs = probs_ref[...]
    experts = probs.shape[0]
    scores = (ga_ref[:, width:].astype(f32) + gb_ref[:, width:].astype(f32)).T
    dprobs = scores[:experts] + scores[experts : 2 * experts]
    dlogits = (probs * (dprobs - jnp.sum(probs * dprobs, axis=0, keepdims=True))).astype(bf16)
    dlow = (dot_tn(dlogits, route_leave[...]) * SCALE * mark).astype(bf16)
    dhb_ref[:, width:] = dlow
    leave_ref[...] = SCALE * dot_nn(dlogits, route_low[...])
    back = ga_ref[:, :width].astype(f32) + gb_ref[:, :width].astype(f32)
    back = back + dot_tn(dlogits, route_ref[...]) + dot_nt(dlow, route_enter[...])
    back = back * gain_ref[...].astype(f32)
    h = h_ref[...]
    scale = rms_scale(h)
    dh = up_ref[...].astype(f32) + scale * back - h * scale**3 * jnp.mean(h * back, axis=-1, keepdims=True)
    dh_ref[...] = dh
    dhb_ref[:, :width] = dh.astype(bf16)


def middle_back(docs, scal, grads, probs, h, upstream, route_low, gain, route, route_enter, route_leave):
    local, width = h.shape
    rank = route_enter.shape[1]
    f32, bf16 = (jnp.float32, jnp.bfloat16)
    return pl.pallas_call(
        functools.partial(middle_back_kernel, docs),
        out_shape=(
            jax.ShapeDtypeStruct((local, width), f32),
            jax.ShapeDtypeStruct((local, width + rank), bf16),
            jax.ShapeDtypeStruct((route.shape[0], rank), f32),
        ),
        in_specs=[full(SMEM)] + [full()] * 10,
        out_specs=(full(),) * 3,
        compiler_params=params(),
        cost_estimate=cost(4 * local * width * rank, 10_000_000),
        name="middle_back",
    )(scal, *grads, probs, h, upstream, route_low, gain, route, route_enter, route_leave)


def attend_back_kernel(docs, half, local, scal_ref, *refs):
    f32, bf16 = (jnp.float32, jnp.bfloat16)
    q_ref = refs[0]
    members = q_ref.shape[0] // local
    count = members // 2
    heads = q_ref.shape[1] // HEAD_DIM
    q_ref, k_ref, v_ref, w_ref, enter_ref, leave_ref = refs[:6]
    refs = refs[6:]
    grad_refs, att_refs, log_refs, normed_refs, refs = (*(refs[i * count : (i + 1) * count] for i in range(4)), refs[4 * count :])
    before, refs = (refs[: 5 * half], refs[5 * half + half :])
    dq_ref, dk_ref, dv_ref, enter_grad, leave_grad, route_grad, *rest = refs
    term_refs, (grad, datt, att, logs, normed) = (rest[:-5], rest[-5:])
    width = w_ref.shape[1]
    step = pl.program_id(0)
    place = half * count + step
    member = scal_ref[0]
    block = member ^ place
    queries = pl.ds(pl.multiple_of(place * local, local), local)
    mine = pl.ds(pl.multiple_of(member * q_ref.shape[1], 128), q_ref.shape[1])

    @pl.when(step == 0)
    def _():
        for i, ref in enumerate((dk_ref, dv_ref, enter_grad, leave_grad, route_grad)):
            ref[...] = before[i][...] if half else jnp.zeros_like(ref)

    for i in range(count):

        @pl.when(step == i)
        def _():
            grad[...] = grad_refs[i][...]
            att[...] = att_refs[i][...]
            logs[...] = log_refs[i][...]
            normed[:, : mine.size] = normed_refs[i][:, mine]
            normed[:, mine.size :] = normed_refs[i][:, width:]

    mark = block_marks(scal_ref, docs, block, local)
    low = (dot_nt(grad[:, :width], leave_ref[...]) * SCALE * mark).astype(bf16)
    datt[...] = (dot_nt(grad[:, :width], w_ref[...]) + dot_nt(low, enter_ref[...])).astype(bf16)
    enter_grad[...] += dot_tn(low, att[...])
    leave_grad[...] += SCALE * dot_tn(normed[:, mine.size :], grad[:, mine])
    route_grad[...] += dot_tn(grad[:, width:], normed[:, : mine.size])

    def run(last):
        rows = last * local + lax.broadcasted_iota(jnp.int32, (local, local), 1)
        begin = doc_sum(scal_ref, rows, docs, 1 + 2 * docs)
        down = lax.broadcasted_iota(jnp.int32, (local, local), 0)
        term = jnp.zeros((local, 1), f32)
        for h in range(heads):
            cut = slice(h * HEAD_DIM, (h + 1) * HEAD_DIM)
            query, dout = (q_ref[queries, cut], datt[:, cut])
            log = logs[h : h + 1]
            shares, pushes = ([], [])
            for b in range(last + 1):
                there = pl.ds(pl.multiple_of((member ^ b) * local, local), local)
                score = dot_nt(k_ref[there, cut], query) * HEAD_DIM ** (-0.5)
                good = down + b * local >= begin
                if b == last:
                    good = good & (down + b * local <= rows)
                share = jnp.where(good, jnp.exp(score - log), 0.0)
                shares.append(share)
                pushes.append(dot_nt(v_ref[there, cut], dout))
            inner = functools.reduce(jnp.add, [jnp.sum(s * d, axis=0, keepdims=True) for s, d in zip(shares, pushes)])
            dquery = jnp.zeros((local, HEAD_DIM), f32)
            for b in range(last + 1):
                there = pl.ds(pl.multiple_of((member ^ b) * local, local), local)
                dscore = (shares[b] * (pushes[b] - inner) * HEAD_DIM ** (-0.5)).astype(bf16)
                dquery = dquery + dot_tn(dscore, k_ref[there, cut])
                dk_ref[there, cut] += dot_nn(dscore, query)
                dv_ref[there, cut] += dot_nn(shares[b].astype(bf16), dout)
            dq_ref[:, cut] = dquery
            term = term + jnp.sum(dquery * query.astype(f32), axis=1, keepdims=True)
        term_refs[0][...] = as_row(term)

    for last in range(members):
        pl.when(block == last)(functools.partial(run, last))

    if half:

        @pl.when(step == count - 1)
        def _():
            for b in range(members):
                here = slice(b * local, (b + 1) * local)
                value = jnp.sum(dk_ref[here] * k_ref[here].astype(f32), axis=1, keepdims=True)
                term_refs[1][:, here] = as_row(value)


def attend_back(docs, half, scal, q, k, v, weight, enter, leave, grads, atts, logs, normed, before, *deps):
    group_len, slice_width = q.shape
    local = grads[0].shape[0]
    width, rank = (weight.shape[1], enter.shape[1])
    count = len(grads)
    f32, bf16 = (jnp.float32, jnp.bfloat16)
    low_grad = jax.ShapeDtypeStruct((rank, slice_width), f32)
    outs = (
        jax.ShapeDtypeStruct((count * local, slice_width), f32),
        jax.ShapeDtypeStruct((group_len, slice_width), f32),
        jax.ShapeDtypeStruct((group_len, slice_width), f32),
        low_grad,
        low_grad,
        low_grad,
        jax.ShapeDtypeStruct((1, count * local), f32),
    ) + ((jax.ShapeDtypeStruct((1, group_len), f32),) if half else ())
    return pl.pallas_call(
        functools.partial(attend_back_kernel, docs, half, local),
        grid=(count,),
        out_shape=outs,
        in_specs=[full(SMEM)] + [full()] * (6 + 4 * count + len(before)) + [full(pl.ANY)] * len(deps),
        out_specs=(pl.BlockSpec((local, slice_width), lambda i: (i, 0)),)
        + (full(),) * 5
        + (pl.BlockSpec((1, local), lambda i: (0, i)),)
        + ((full(),) if half else ()),
        scratch_shapes=[
            pltpu.VMEM((local, width + rank), bf16),
            pltpu.VMEM((local, slice_width), bf16),
            pltpu.VMEM((local, slice_width), bf16),
            pltpu.VMEM((8, local), f32),
            pltpu.VMEM((local, slice_width + rank), bf16),
        ],
        compiler_params=params(),
        cost_estimate=cost(8_000_000_000, 14_000_000, 700_000),
        name="attend_back",
    )(scal, q, k, v, weight, enter, leave, *grads, *atts, *logs, *normed, *before, *deps)


def project_back_kernel(docs, local, scal_ref, *refs):
    f32, bf16 = (jnp.float32, jnp.bfloat16)
    near_ref, far_ref, dk_ref, dv_ref, p_ref, square_ref, term_ref, gains_ref, cos_ref, sin_ref, normed_ref, low_ref = refs[:12]
    w_ref, enter_ref, leave_ref, route_ref, *refs = refs[12:]
    *dx_refs, enter_grad, leave_grad, dp_ref, dlow_ref, turned = refs
    rows, slice_width = near_ref.shape
    rank = SETS * RANK
    member = scal_ref[0]
    step = pl.program_id(0)
    members = pl.num_programs(0)
    width = slice_width * members
    count = rows // local

    @pl.when(step == 0)
    def _():
        inverse = lax.rsqrt(square_ref[...] / width + EPS)
        biases = inverse * inverse * term_ref[...] / width
        for i in range(2):
            for half in range(2):
                here = slice(half * rows, (half + 1) * rows)
                scale, bias = (column(inverse[i : i + 1, here]), column(biases[i : i + 1, here]))
                for at in range(0, slice_width, HEAD_DIM):
                    cut = slice(at, at + HEAD_DIM)
                    value = dk_ref[here, cut] if i else (far_ref if half else near_ref)[:, cut]
                    value = value * cos_ref[here] - pltpu.roll(value, HEAD_DIM // 2, 1) * sin_ref[here]
                    value = value * gains_ref[i : i + 1, cut] * scale - p_ref[i, here, cut] * bias
                    dp_ref[i, here, cut] = value.astype(bf16)
        dp_ref[2] = dv_ref[...].astype(bf16)
        for b in range(2 * count):
            here = slice(b * local, (b + 1) * local)
            mark = block_marks(scal_ref, docs, member ^ b, local)
            for i in range(3):
                value = dot_nt(dp_ref[i, here], leave_ref[i]) * SCALE * mark
                dlow_ref[here, i * rank : (i + 1) * rank] = value.astype(bf16)
                turned[i * rank : (i + 1) * rank, here] = value.T.astype(bf16)
        for i in range(3):
            leave_grad[i] = dot_tn(low_ref[i], dp_ref[i])

    enter_grad[0, : 3 * rank] = dot_nn(turned[...], normed_ref[...]).astype(bf16)
    enter_grad[0, 3 * rank :] = route_ref[0]
    spread_back(dx_refs, [dp_ref[i, rows:] for i in range(3)], dlow_ref[rows:], w_ref, enter_ref)


def spread_back(dx_refs, grads, low, w_ref, enter_ref):
    value = dot_nt(grads[0], w_ref[0]) + dot_nt(grads[1], w_ref[1]) + dot_nt(grads[2], w_ref[2])
    value = value + dot_nt(low, jnp.concatenate([enter_ref[i] for i in range(3)], axis=1))
    value = value.astype(jnp.bfloat16)
    local = dx_refs[0].shape[0]
    for b, dx_ref in enumerate(dx_refs):
        dx_ref[...] = value[b * local : (b + 1) * local]


def project_back(docs, local, scal, near, far, dk, dv, p, squares, terms, gains, cosine, sine, normed, low, weight, enter, leave, route_grad, *deps):
    rows, slice_width = near.shape
    width, rank = (normed.shape[1], enter.shape[2])
    members, count = (2 * rows // local, rows // local)
    tall = 3 * rank + route_grad.shape[1]
    f32, bf16 = (jnp.float32, jnp.bfloat16)
    pick = lambda i, scal: scal[0] ^ i
    sums = pl.BlockSpec((1, tall, slice_width), lambda i, scal: (i, 0, 0))
    in_specs = [full()] * 10 + [
        pl.BlockSpec((2 * rows, slice_width), lambda i, scal: (0, pick(i, scal))),
        full(),
        pl.BlockSpec((3, slice_width, slice_width), lambda i, scal: (0, pick(i, scal), 0)),
        pl.BlockSpec((3, slice_width, rank), lambda i, scal: (0, pick(i, scal), 0)),
        full(),
        pl.BlockSpec((1, tall - 3 * rank, slice_width), lambda i, scal: (i, 0, 0)),
    ] + [full(pl.ANY)] * len(deps)
    return pl.pallas_call(
        lambda *refs: project_back_kernel(docs, local, *refs[:17], *refs[17 + len(deps) :]),
        out_shape=(jax.ShapeDtypeStruct((local, width), bf16),) * count
        + (
            jax.ShapeDtypeStruct((members, tall, slice_width), bf16),
            jax.ShapeDtypeStruct((3, rank, slice_width), f32),
            jax.ShapeDtypeStruct((3, 2 * rows, slice_width), bf16),
            jax.ShapeDtypeStruct((2 * rows, 3 * rank), bf16),
        ),
        grid_spec=pltpu.PrefetchScalarGridSpec(
            num_scalar_prefetch=1,
            grid=(members,),
            in_specs=in_specs,
            out_specs=(pl.BlockSpec((local, slice_width), lambda i, scal: (0, pick(i, scal))),) * count
            + (sums, full(), full(), full()),
            scratch_shapes=[pltpu.VMEM((3 * rank, 2 * rows), bf16)],
        ),
        compiler_params=params(),
        cost_estimate=cost(2 * rows * (width * 3 * slice_width + 6 * rank * width), 20_000_000),
        name="project_back",
    )(scal, near, far, dk, dv, p, squares, terms, gains, cosine, sine, normed, low, weight, enter, leave, route_grad, *deps)


def project_near(local, grads, low, weight, enter, *deps):
    _, group_len, slice_width = grads.shape
    rows, width, rank = (group_len // 2, weight.shape[1], enter.shape[2])
    count = rows // local
    step = slice_width
    out = jax.ShapeDtypeStruct((local, width), jnp.bfloat16)

    def kernel(grads_ref, low_ref, w_ref, enter_ref, *refs):
        spread_back(refs[-count:], [grads_ref[i] for i in range(3)], low_ref[...], w_ref, enter_ref)

    return pl.pallas_call(
        kernel,
        grid=(width // step,),
        out_shape=(out,) * count,
        in_specs=[
            pl.BlockSpec((3, rows, slice_width), lambda i: (0, 0, 0)),
            pl.BlockSpec((rows, 3 * rank), lambda i: (0, 0)),
            pl.BlockSpec((3, step, slice_width), lambda i: (0, i, 0)),
            pl.BlockSpec((3, step, rank), lambda i: (0, i, 0)),
        ]
        + [full(pl.ANY)] * len(deps),
        out_specs=(pl.BlockSpec((local, step), lambda i: (0, i)),) * count,
        compiler_params=params(),
        cost_estimate=cost(2 * rows * (width * 3 * slice_width), 10_000_000),
        name="project_near",
    )(grads, low, weight, enter, *deps)


def finish_kernel(*refs):
    f32 = jnp.float32
    *parts, dh_ref, x_ref, gain_ref, out_ref = refs
    x = x_ref[...].astype(f32)
    back = functools.reduce(jnp.add, [part[...].astype(f32) for part in parts]) * gain_ref[...].astype(f32)
    scale = rms_scale(x)
    out = dh_ref[...] + scale * back - x * scale**3 * jnp.mean(x * back, axis=-1, keepdims=True)
    out_ref[...] = out.astype(out_ref.dtype)


def finish(grads, dh, x, gain):
    return pl.pallas_call(
        finish_kernel,
        out_shape=jax.ShapeDtypeStruct(x.shape, jnp.bfloat16),
        in_specs=[full()] * (3 + len(grads)),
        out_specs=full(),
        compiler_params=params(),
        cost_estimate=cost(10 * x.size, 12 * x.size),
        name="finish",
    )(*grads, dh, x, gain)


def upstream_kernel(scal_ref, named_ref, *refs):
    blocks = named_ref.shape[0]
    f32, bf16 = (jnp.float32, jnp.bfloat16)
    upstream_refs, (down_w, down_leave, rank_ref, rows_ref, back_ref, low_ref, places) = (refs[:blocks], refs[-7:])
    experts, local = places.shape[1:]
    cap = rows_ref.shape[1] // blocks

    @pl.when((pl.program_id(0) == 0) | (pl.num_programs(1) > 1))
    def _():
        earlier = lax.broadcasted_iota(jnp.int32, (local, local), 0) < lax.broadcasted_iota(jnp.int32, (local, local), 1)
        bits = lax.broadcasted_iota(jnp.int32, (experts, local), 0)
        for b in range(blocks):
            hot = (jnp.right_shift(named_ref[b], bits) & 1).astype(f32)
            rank = dot_nn(hot.astype(bf16), earlier.astype(f32).astype(bf16))
            places[b] = jnp.where(hot > 0.0, rank, -1.0)

    mine = pl.ds(scal_ref[0] * pl.num_programs(0) + pl.program_id(0), 1)
    slots = lax.broadcasted_iota(jnp.int32, (cap, local), 0).astype(f32)
    for b in range(blocks):
        rank_ref[0, b] = places[b, mine]
        pick = (places[b, mine] == slots).astype(bf16)
        rows_ref[0, b * cap : (b + 1) * cap] = dot_nn(pick, upstream_refs[b][...]).astype(bf16)
    back_ref[0] = dot_nt(rows_ref[0], down_w[0]).astype(bf16)
    low_ref[0] = dot_nt(rows_ref[0], down_leave[0])


def run_upstream(scal, named, upstream, down, down_leave, *deps):
    members, _, local = named.shape
    experts, ff, width = down.shape
    low = down_leave.shape[1]
    blocks = min(members, 4)
    turns = members // blocks
    count = blocks * CAP
    f32, bf16 = (jnp.float32, jnp.bfloat16)
    rows = lambda wide: pl.BlockSpec((1, count, wide), lambda e, r: (e, r, 0))
    return pl.pallas_call(
        lambda *refs: upstream_kernel(*refs[: 4 + blocks], *refs[4 + blocks + len(deps) :]),
        grid=(experts, turns),
        out_shape=(
            jax.ShapeDtypeStruct((experts, members, 1, local), f32),
            jax.ShapeDtypeStruct((experts, members * CAP, width), bf16),
            jax.ShapeDtypeStruct((experts, members * CAP, ff), bf16),
            jax.ShapeDtypeStruct((experts, members * CAP, low), f32),
        ),
        in_specs=[full(SMEM), pl.BlockSpec((blocks, 1, local), lambda e, r: (r, 0, 0))]
        + [pl.BlockSpec((local, width), lambda e, r: (r, 0), pipeline_mode=pl.Buffered(1))] * blocks
        + [pl.BlockSpec((1, ff, width), lambda e, r: (e, 0, 0)), pl.BlockSpec((1, low, width), lambda e, r: (e, 0, 0))]
        + [full(pl.ANY)] * len(deps),
        out_specs=(pl.BlockSpec((1, blocks, 1, local), lambda e, r: (e, r, 0, 0)), rows(width), rows(ff), rows(low)),
        scratch_shapes=[pltpu.VMEM((blocks, EXPERTS, local), f32)],
        compiler_params=params(),
        cost_estimate=cost(2 * experts * members * CAP * width * ff, 40_000_000),
        name="upstream",
    )(scal, named, *by_block(upstream, blocks), down, down_leave, *deps)


def by_block(parts, blocks):
    return [jnp.concatenate(parts[b::blocks]) if len(parts) > blocks else parts[b] for b in range(blocks)]


def dispatch(docs, scal_ref, place, rank_rows, weight_rows, normed_refs, rows_in, marks):
    local, low = (rank_rows[0].shape[1], marks.shape[1])
    cap = rows_in.shape[0] // len(rank_rows)
    slots = lax.broadcasted_iota(jnp.int32, (cap, local), 0).astype(jnp.float32)
    weights = []
    for b, rank_row in enumerate(rank_rows):
        hit = rank_row == slots
        pick = hit.astype(jnp.bfloat16)
        weights.append(jnp.sum(jnp.where(hit, weight_rows[b], 0.0), axis=1, keepdims=True))
        here = slice(b * cap, (b + 1) * cap)
        mark = block_marks(scal_ref, docs, scal_ref[0] ^ (place + b), local).astype(jnp.bfloat16)
        rows_in[here, :] = dot_nn(pick, normed_refs[b][:, : rows_in.shape[1]]).astype(jnp.bfloat16)
        marks[here, :] = dot_nn(pick, mark)
    return jnp.concatenate(weights, axis=0)


def inner_rows(
    first, rows_in, mark, weight, low_in, back_in, gate_w, up_w, gate_enter, gate_leave, up_enter, up_leave, down_enter, hidden, grad_gate, grad_up
):
    f32, bf16 = (jnp.float32, jnp.bfloat16)
    rank, ff = (mark.shape[1], hidden.shape[1])
    rows = rows_in[first:]
    low = dot_nn(rows, jnp.concatenate([gate_enter[0], up_enter[0]], axis=1))
    low_gate = (low[:, :rank] * mark).astype(bf16) * SCALE
    low_up = (low[:, rank:] * mark).astype(bf16) * SCALE
    grad_low_down = (low_in[...] * (SCALE * weight) * mark).astype(bf16)
    step = min(256, ff)
    for at in range(0, ff, step):
        cut = slice(at, at + step)
        gate = dot_nn(rows, gate_w[0, :, cut]) + dot_nn(low_gate, gate_leave[0, :, cut])
        up = dot_nn(rows, up_w[0, :, cut]) + dot_nn(low_up, up_leave[0, :, cut])
        back = back_in[:, cut].astype(f32) * weight + dot_nt(grad_low_down, down_enter[0, cut, :])
        sigma = 1.0 / (1.0 + jnp.exp(-gate))
        silu = gate * sigma
        hidden[first:, cut] = (silu * up).astype(bf16)
        grad_gate[first:, cut] = (back * up * sigma * (1.0 + gate * (1.0 - sigma))).astype(bf16)
        grad_up[first:, cut] = (back * silu).astype(bf16)
    return low_gate, low_up, grad_low_down


def near_kernel(docs, scal_ref, rank_ref, back_ref, low_ref, route_ref, route_enter, route_leave, *refs):
    count = len(refs) - 14
    normed_refs, refs = (refs[:count], refs[count:])
    weights, (hidden, grad_gate, grad_up, lows, rows_in, marks, probs) = (refs[:7], refs[7:])
    width = rows_in.shape[1]
    local = rank_ref.shape[3]

    @pl.when(pl.program_id(0) == 0)
    def _():
        for b in range(count):
            mark = block_marks(scal_ref, docs, scal_ref[0] ^ b, local)
            probs[b] = router(normed_refs[b][:, :width], mark, route_ref, route_enter, route_leave)[1]

    mine = pl.ds(scal_ref[0] * pl.num_programs(0) + pl.program_id(0), 1)
    rank_rows, weight_rows = ([rank_ref[0, b] for b in range(count)], [probs[b, mine] for b in range(count)])
    weight = dispatch(docs, scal_ref, 0, rank_rows, weight_rows, normed_refs, rows_in, marks)
    made = inner_rows(
        0, rows_in, marks[...], weight, low_ref.at[0], back_ref.at[0], *weights, hidden.at[0], grad_gate.at[0], grad_up.at[0]
    )
    lows[0] = jnp.concatenate(made, axis=1)


def run_near(docs, scal, ranks, back, low_back, route, route_enter, route_leave, normed, *weights):
    experts, members, _, local = ranks.shape
    ff, low = (back.shape[2], low_back.shape[2])
    width = normed[0].shape[1] - low
    rows = len(normed) * CAP
    bf16 = jnp.bfloat16
    near = lambda wide: pl.BlockSpec((1, rows, wide), lambda e: (e, 0, 0))
    hidden = jax.ShapeDtypeStruct((experts, rows, ff), bf16)
    return pl.pallas_call(
        functools.partial(near_kernel, docs),
        grid=(experts,),
        out_shape=(hidden, hidden, hidden, jax.ShapeDtypeStruct((experts, rows, 3 * low), bf16)),
        in_specs=[full(SMEM), pl.BlockSpec((1, members, 1, local), lambda e: (e, 0, 0, 0)), near(ff), near(low)]
        + [full()] * (3 + len(normed))
        + [pl.BlockSpec((1,) + value.shape[1:], lambda e: (e, 0, 0)) for value in weights],
        out_specs=(near(ff), near(ff), near(ff), near(3 * low)),
        scratch_shapes=[
            pltpu.VMEM((rows, width), bf16),
            pltpu.VMEM((rows, low), jnp.float32),
            pltpu.VMEM((len(normed), EXPERTS, local), jnp.float32),
        ],
        compiler_params=params(),
        cost_estimate=cost(4 * experts * rows * width * ff, 40_000_000),
        name="near",
    )(scal, ranks, back, low_back, route, route_enter, route_leave, *normed, *weights)


def expert_kernel(line, docs, made, scal_ref, rank_ref, grads_ref, back_ref, low_ref, route_ref, route_enter, route_leave, *refs):
    blocks = rank_ref.shape[1]
    ahead, refs = (refs[:made], refs[made:])
    normed_refs, refs, probs = (refs[:blocks], refs[blocks:-1], refs[-1])
    width = grads_ref.shape[2]
    turn = pl.program_id(1)
    local = rank_ref.shape[3]

    @pl.when((pl.program_id(0) == 0) | (pl.num_programs(1) > 1))
    def _():
        for b in range(blocks):
            mark = block_marks(scal_ref, docs, scal_ref[0] ^ (turn * blocks + b), local)
            probs[b] = router(normed_refs[b][:, :width], mark, route_ref, route_enter, route_leave)[1]

    mine = pl.ds(scal_ref[0] * pl.num_programs(0) + pl.program_id(0), 1)
    weights = [probs[b, mine] for b in range(blocks)]
    expert_rows(line, docs, ahead, scal_ref, rank_ref, weights, normed_refs, grads_ref.at[0], back_ref.at[0], low_ref.at[0], *refs)


def expert_rows(
    line,
    docs,
    ahead,
    scal_ref,
    rank_ref,
    weight_rows,
    normed_refs,
    grads_in,
    back_in,
    low_in,
    gate_w,
    up_w,
    down_w,
    gate_enter,
    gate_leave,
    up_enter,
    up_leave,
    down_enter,
    down_leave,
    place_ref,
    mixed_ref,
    grad_ref,
    score_ref,
    *rest,
):
    inner = len(rest) - 9
    sums, (rows_in, hidden, grad_gate, grad_up, marks, out_tile, back_tile, done, full_rows) = (rest[:inner], rest[inner:])
    f32, bf16 = (jnp.float32, jnp.bfloat16)
    blocks, local, width = (rank_ref.shape[1], rank_ref.shape[3], grads_in.shape[1])
    cap = mixed_ref.shape[2]
    expert, turn = (pl.program_id(0), pl.program_id(1))
    count = blocks * cap
    ff = hidden.shape[1]
    slots = lax.broadcasted_iota(jnp.int32, (cap, local), 0).astype(f32)
    rank_rows = [rank_ref[0, b] for b in range(blocks)]
    weight = dispatch(docs, scal_ref, turn * blocks, rank_rows, weight_rows, normed_refs, rows_in, marks)
    mark = marks[...]
    rank = mark.shape[1]
    first = ahead[0].shape[1] if ahead else 0
    lows = inner_rows(
        first, rows_in, mark[first:], weight[first:], low_in, back_in, gate_w, up_w, gate_enter, gate_leave, up_enter, up_leave, down_enter,
        hidden, grad_gate, grad_up
    )
    if ahead:
        for to, of in zip((hidden, grad_gate, grad_up), ahead):
            to[:first] = of[0]
        lows = [jnp.concatenate([ahead[3][0, :, i * rank : (i + 1) * rank], value], axis=0) for i, value in enumerate(lows)]
    low_gate, low_up, grad_low_down = lows
    low_down = (dot_nn(hidden[...], down_enter[0]) * mark).astype(bf16) * SCALE
    grad_low_gate = (dot_nt(grad_gate[...], gate_leave[0]) * SCALE * mark).astype(bf16)
    grad_low_up = (dot_nt(grad_up[...], up_leave[0]) * SCALE * mark).astype(bf16)
    grad_low = jnp.concatenate([grad_low_gate, grad_low_up], axis=1)
    step = out_tile.shape[3]
    sent = []

    def send(slot, cut):
        there = pl.ds(turn * blocks, blocks)
        copies = [
            pltpu.make_async_copy(out_tile.at[slot], mixed_ref.at[there, expert, :, cut], done.at[0, slot]),
            pltpu.make_async_copy(back_tile.at[slot], grad_ref.at[there, expert, :, cut], done.at[1, slot]),
        ]
        for copy in copies:
            copy.start()
        sent.append(copies)

    score = jnp.zeros((count, 1), f32)
    for at in range(0, width, step):
        cut = slice(at, at + step)
        out = dot_nn(hidden[...], down_w[0, :, cut]) + dot_nn(low_down, down_leave[0, :, cut])
        score = score + jnp.sum(out * grads_in[:, cut].astype(f32), axis=1, keepdims=True)
        back = dot_nt(grad_gate[...], gate_w[0, cut, :]) + dot_nt(grad_up[...], up_w[0, cut, :])
        back = back + dot_nt(grad_low, jnp.concatenate([gate_enter[0, cut, :], up_enter[0, cut, :]], axis=1))
        out = (out * weight).astype(bf16)
        back = back.astype(bf16)
        slot = len(sent) % 2
        if len(sent) >= 2:
            for copy in sent[-2]:
                copy.wait()
        for b in range(blocks):
            out_tile[slot, b] = out[b * cap : (b + 1) * cap]
            back_tile[slot, b] = back[b * cap : (b + 1) * cap]
        send(slot, pl.ds(at, step))
    for b in range(blocks):
        hit = rank_ref[0, b] == slots
        score_ref[0, b] = jnp.sum(jnp.where(hit, score[b * cap : (b + 1) * cap], 0.0), axis=0, keepdims=True)

    def keep(value, row, ref_at):
        piece = value.shape[1] // (line * inner)
        value = value.astype(bf16)
        full_rows[: value.shape[0], : value.shape[1]] = value
        columns = slice(ref_at, ref_at + piece)
        for c in range(line * inner):
            part = slice(c * piece, (c + 1) * piece)
            for q in range(inner):

                @pl.when(place_ref[1, c] == q)
                def _():
                    for at in range(0, value.shape[0], rank):
                        if inner != 2 or q == 0:
                            source = full_rows[at : at + rank, part]
                            target = sums[q].at[place_ref[0, c], 0, slice(row + at, row + at + rank), columns]
                            if pl.num_programs(1) > 1:
                                old = jnp.where(turn > 0, target[...].astype(f32), 0.0)
                                source = (old + source.astype(f32)).astype(bf16)
                            target[...] = source
                            continue
                        for d in range(docs):
                            there = pl.ds(pl.multiple_of(at + scal_ref[1 + docs + d] * RANK, RANK), RANK)
                            source = full_rows[there, part]
                            for d2 in range(d):
                                repeated = scal_ref[1 + docs + d2] == scal_ref[1 + docs + d]
                                source = jnp.where(repeated, jnp.zeros_like(source), source)
                            to = ((row + at) // rank * docs + d) * RANK
                            target = sums[q].at[place_ref[0, c], 0, slice(to, to + RANK), columns]
                            if pl.num_programs(1) > 1:
                                old = jnp.where(turn > 0, target[...].astype(f32), 0.0)
                                source = (old + source.astype(f32)).astype(bf16)
                            target[...] = source

    wide = width // (line * inner)
    keep(dot_tn(grad_low, rows_in[...]), 0, 0)
    keep(dot_tn((low_down.astype(f32) * weight).astype(bf16), grads_in[...]), 2 * rank, 0)
    keep(dot_tn(low_gate, grad_gate[...]), 0, wide)
    keep(dot_tn(low_up, grad_up[...]), rank, wide)
    keep(dot_tn(grad_low_down, hidden[...]), 2 * rank, wide)
    for copies in sent[-2:]:
        for copy in copies:
            copy.wait()


def run_experts(docs, scal, ranks, grads, back, low_back, route, route_enter, route_leave, ahead, normed, place, inner, *weights):
    experts, members, _, local = ranks.shape
    width = grads.shape[2]
    ff = back.shape[2]
    low = SETS * RANK
    blocks = min(members, 4)
    turns = members // blocks
    packs = place.shape[1]
    line = packs // inner
    bf16 = jnp.bfloat16
    count = blocks * CAP
    tile = min(512, width)
    by_turn = lambda e, r: (e, r, 0, 0)
    rows = lambda wide: pl.BlockSpec((1, count, wide), lambda e, r: (e, r, 0))
    half = count // 2
    back_rows = lambda wide: pl.BlockSpec((1, half, wide), lambda e, r: (e, 1, 0)) if ahead else rows(wide)
    once = lambda wide: [pl.BlockSpec((local, wide), lambda e, r: (r, 0), pipeline_mode=pl.Buffered(1))] * blocks
    per_expert = lambda value: pl.BlockSpec((1,) + value.shape[1:], lambda e, r: (e, 0, 0))
    packed = docs * RANK if inner == 2 else low
    sums = [jax.ShapeDtypeStruct((line, experts, 3 * (packed if q else low), (width + ff) // packs), bf16) for q in range(inner)]
    rows_out = jax.ShapeDtypeStruct((members, experts, CAP, width), bf16)
    return pl.pallas_call(
        functools.partial(expert_kernel, line, docs, len(ahead)),
        grid=(experts, turns),
        out_shape=(rows_out, rows_out, jax.ShapeDtypeStruct(ranks.shape, jnp.float32), *sums),
        in_specs=[full(SMEM), pl.BlockSpec((1, blocks, 1, local), by_turn), rows(width), back_rows(ff), back_rows(low)]
        + [full()] * 3
        + [pl.BlockSpec((1,) + value.shape[1:], lambda e, r: (e, 0, 0)) for value in ahead]
        + once(width + low)
        + [per_expert(value) for value in weights]
        + [full(SMEM)],
        out_specs=(full(pl.ANY), full(pl.ANY), pl.BlockSpec((1, blocks, 1, local), by_turn))
        + tuple(pl.BlockSpec((line, 1) + value.shape[2:], lambda e, r: (0, e, 0, 0)) for value in sums),
        scratch_shapes=[
            pltpu.VMEM((count, width), bf16),
            pltpu.VMEM((count, ff), bf16),
            pltpu.VMEM((count, ff), bf16),
            pltpu.VMEM((count, ff), bf16),
            pltpu.VMEM((count, low), jnp.float32),
            pltpu.VMEM((2, blocks, CAP, tile), bf16),
            pltpu.VMEM((2, blocks, CAP, tile), bf16),
            pltpu.SemaphoreType.DMA((2, 2)),
            pltpu.VMEM((2 * low, width), bf16),
            pltpu.VMEM((blocks, EXPERTS, local), jnp.float32),
        ],
        compiler_params=params(),
        cost_estimate=cost(2 * experts * members * CAP * (width * ff * 5 + 9 * low * (width + ff)), 60_000_000),
        name="experts",
    )(scal, ranks, grads, back, low_back, route, route_enter, route_leave, *ahead, *by_block(normed, blocks), *weights, place)


def mix(rank_ref, rows_ref, pick_ref, step):
    experts, cap, local = (rows_ref.shape[1], rows_ref.shape[2], rank_ref.shape[3])

    @pl.when(step == 0)
    def _():
        slots = lax.broadcasted_iota(jnp.int32, (cap, local), 0).astype(jnp.float32)
        pick = jnp.concatenate([(rank_ref[e, 0] == slots).astype(jnp.float32) for e in range(experts)], axis=0)
        pick_ref[...] = pick.T.astype(jnp.bfloat16)

    rows = jnp.concatenate([rows_ref[0, e] for e in range(experts)], axis=0)
    return dot_nn(pick_ref[...], rows)


def mix_grads(scal_ref, rank_ref, score_ref, rows_ref, added_ref, back_ref, pick_ref, step):
    f32, bf16 = (jnp.float32, jnp.bfloat16)
    experts, local = (rows_ref.shape[1], rank_ref.shape[3])
    piece, low = (rows_ref.shape[3], SETS * RANK)
    width = back_ref.shape[1] - low
    columns = pl.ds(pl.multiple_of(step * piece, 128), piece)
    value = mix(rank_ref, rows_ref, pick_ref, step)
    if added_ref is not None:
        value = value + added_ref[:, columns].astype(f32)
    back_ref[:, columns] = value.astype(bf16)

    @pl.when(step == 0)
    def _():
        lines = lax.broadcasted_iota(jnp.int32, (low, local), 0)
        table = jnp.zeros((low, local), f32)
        for e in range(experts):
            score = score_ref[e, 0]
            whole = score.astype(bf16).astype(f32)
            at = scal_ref[0] * experts + e
            table = jnp.where(lines == at, whole, table)
            table = jnp.where(lines == at + EXPERTS, score - whole, table)
        table = table.T
        if added_ref is not None:
            table = table + added_ref[:, width:].astype(f32)
        back_ref[:, width:] = table.astype(bf16)


def combine_kernel(added, scal_ref, rank_ref, score_ref, rows_ref, *refs):
    back_ref, pick_ref = refs[-2:]
    mix_grads(scal_ref, rank_ref, score_ref, rows_ref, refs[0] if added else None, back_ref, pick_ref, pl.program_id(0))


def combine(scal, ranks, scores, rows, place, addend, *deps):
    experts, members, _, local = ranks.shape
    width = rows.shape[3]
    piece = width // 2
    low = SETS * RANK
    one = pl.BlockSpec((experts, 1, 1, local), lambda n: (0, place, 0, 0))
    more = () if addend is None else (addend,)
    return pl.pallas_call(
        functools.partial(combine_kernel, addend is not None),
        grid=(2,),
        out_shape=jax.ShapeDtypeStruct((local, width + low), jnp.bfloat16),
        in_specs=[full(SMEM), one, one, pl.BlockSpec((1, experts, CAP, piece), lambda n: (place, 0, 0, n))]
        + [full()] * len(more)
        + [full(pl.ANY)] * len(deps),
        out_specs=full(),
        scratch_shapes=[pltpu.VMEM((local, experts * CAP), jnp.bfloat16)],
        compiler_params=params(),
        cost_estimate=cost(2 * local * experts * CAP * width, 2 * experts * CAP * width),
        name="combine",
    )(scal, ranks, scores, rows, *more, *deps)


def combine_last_kernel(scal_ref, rank_ref, score_ref, grads_ref, rows_ref, added_ref, *refs):
    members = pl.num_programs(0)
    out_refs, (back_ref, pick_ref) = (refs[-2 - members : -2], refs[-2:])
    block, step = (pl.program_id(0), pl.program_id(1))
    piece = rows_ref.shape[3]
    columns = pl.ds(pl.multiple_of(step * piece, 128), piece)
    value = mix(rank_ref, rows_ref, pick_ref, step).astype(jnp.bfloat16)
    for b in range(members):

        @pl.when(block == b)
        def _():
            out_refs[b][:, columns] = value

    @pl.when(block == 0)
    def _():
        mix_grads(scal_ref, rank_ref, score_ref, grads_ref, added_ref, back_ref, pick_ref, step)


def combine_last(scal, ranks, scores, grads, mixed, addend, *deps):
    experts, members, _, local = ranks.shape
    width = grads.shape[3]
    piece = width // 2
    low = SETS * RANK
    out = jax.ShapeDtypeStruct((local, width), jnp.bfloat16)
    one = pl.BlockSpec((experts, 1, 1, local), lambda b, n: (0, b, 0, 0))
    first = lambda b, n: (0, 0, 0, jnp.where(b == 0, n, 1))
    return pl.pallas_call(
        lambda *refs: combine_last_kernel(*refs[:6], *refs[6 + len(deps) :]),
        grid=(members, 2),
        out_shape=(out,) * members + (jax.ShapeDtypeStruct((local, width + low), jnp.bfloat16),),
        in_specs=[full(SMEM), one, one]
        + [pl.BlockSpec((1, experts, CAP, piece), first), pl.BlockSpec((1, experts, CAP, piece), lambda b, n: (b, 0, 0, n))]
        + [full()]
        + [full(pl.ANY)] * len(deps),
        out_specs=(full(),) * (members + 1),
        scratch_shapes=[pltpu.VMEM((local, experts * CAP), jnp.bfloat16)],
        compiler_params=params(),
        cost_estimate=cost(2 * 5 * local * experts * CAP * width, 10 * experts * CAP * width),
        name="combine_last",
    )(scal, ranks, scores, grads, mixed, addend, *deps)


def per_device(
    tokens,
    cotangent,
    pack_order,
    doc_lengths,
    doc_sets,
    routes,
    attention_gain,
    query_gain,
    key_gain,
    feed_gain,
    qkv_weight,
    out_weight,
    router_weight,
    gate_weight,
    up_weight,
    down_weight,
    qkv_enter,
    qkv_leave,
    out_enter,
    out_leave,
    router_enter,
    router_leave,
    gate_enter,
    gate_leave,
    up_enter,
    up_leave,
    down_enter,
    down_leave,
):
    members = lax.axis_size("ep")
    packs = lax.axis_size("grp")
    pack = lax.axis_index("grp")
    member = lax.axis_index("ep")
    local, width = tokens.shape
    slice_width = width // members
    experts_here = gate_weight.shape[0]
    own_cols = member * slice_width
    count = members // 2
    low = SETS * RANK
    f32, bf16 = (jnp.float32, jnp.bfloat16)
    slot = jnp.sum(jnp.where(pack_order == pack, jnp.arange(packs, dtype=jnp.int32), 0))
    named = jnp.sum(jnp.left_shift(jnp.int32(1), routes), axis=1)
    documents_here = jnp.concatenate([doc_lengths[0], doc_sets[0]])
    info = jnp.concatenate([named, jnp.pad(documents_here, (0, 128 - documents_here.shape[0]))])
    info = jnp.stack(gather_parts(info, "grp"))
    other = jnp.sum(jnp.where(pack_order == pack ^ 1, jnp.arange(packs, dtype=jnp.int32), 0))
    other = lax.dynamic_index_in_dim(info, other ^ pack, 0, keepdims=False)
    info = lax.dynamic_index_in_dim(info, slot ^ pack, 0, keepdims=False)
    blocks = [member ^ j for j in range(members)]
    named = info[:local]
    docs = doc_lengths.shape[1]
    lengths, sets = (info[local : local + docs], info[local + docs : local + 2 * docs])
    ends = jnp.cumsum(lengths)
    starts = ends - lengths
    scal = jnp.concatenate([member[None].astype(jnp.int32), ends, sets, starts])
    gain_one, gain_two = (attention_gain[None], feed_gain[None])
    route, route_leave = (router_weight.T, router_leave.T)
    adapters = (gain_one, qkv_weight, qkv_enter, qkv_leave)
    named_all = named.reshape(1, 1, local)
    named_all = jnp.concatenate([named_all, swap(named_all, "ep", 1)])
    kept = project(docs, 0, scal, gather_near(tokens, "ep"), *adapters, None, named_all)
    token_parts = gather_far(tokens, "ep", kept[4])
    bit = 2
    while bit < members:
        named_all = jnp.concatenate([named_all, swap(named_all, "ep", bit)])
        bit *= 2
    kept = project(docs, 1, scal, token_parts, *adapters, kept)
    normed_all, low_all, projected, values, squares = kept
    late = fence(scal, values)
    ends, starts = (late[1 : 1 + docs], late[1 + 2 * docs :])
    rows = (jnp.stack(blocks)[:, None] * local + jnp.arange(local, dtype=jnp.int32)[None, :]).reshape(-1)
    begin = starts[0]
    for k in range(1, docs):
        begin = jnp.where(rows >= ends[k - 1], starts[k], begin)
    cosine, sine = angles(rows - begin)
    upstream_far = gather_near(swap(fence(cotangent, token_parts[0], named_all), "ep", members // 2), "ep")
    upstream_parts = gather_near(cotangent, "ep") + upstream_far
    squares = sum_relative(squares, "ep", local)
    own_gain = lambda gain: lax.dynamic_slice_in_dim(gain, own_cols, slice_width, 0)
    gains = jnp.stack([own_gain(query_gain), own_gain(key_gain)]).astype(f32)
    queries, keys = prepare(width, projected, squares, gains, cosine, sine, local, upstream_parts[-1], named_all)
    heads = [None] * members

    def attend_place(place, addend, *deps):
        heads[place] = attend(docs, place, local, scal, queries, keys, values, out_weight, out_enter, addend, *deps)
        return heads[place][1], heads[place][2]

    top = members // 2
    outs = reduce_scatter(attend_place, "ep")
    upstream_rows = run_upstream(scal, named_all, upstream_parts, down_weight, down_leave, heads[0][2])
    hidden_state, normed_two, low_router, probs = middle(
        docs, scal, tokens, outs, out_leave, gain_two, route, router_enter, route_leave, upstream_rows[0]
    )

    ranks, _, *backs = upstream_rows
    routers = (route, router_enter, route_leave)
    normed_two_parts = gather_near(normed_two, "ep")
    ahead = ()
    if members <= 4:
        ahead = run_near(
            docs, scal, ranks, *backs, *routers, normed_two_parts, gate_weight, up_weight, gate_enter, gate_leave, up_enter, up_leave,
            down_enter
        )
    normed_two_parts = normed_two_parts + gather_far(normed_two, "ep", *ahead[3:])
    inner = packs // LINE
    chunk_ids = jnp.arange(packs, dtype=jnp.int32)
    place = jnp.stack([(chunk_ids // inner - pack // inner) % LINE, (chunk_ids % inner - pack % inner) % inner])
    mixed_rows, grad_rows, scores, *expert_sums = run_experts(
        docs,
        scal,
        *upstream_rows,
        *routers,
        ahead,
        normed_two_parts,
        place,
        inner,
        gate_weight,
        up_weight,
        down_weight,
        gate_enter,
        gate_leave,
        up_enter,
        up_leave,
        down_enter,
        down_leave,
    )
    mixed = []

    def combine_place(place, addend, *deps):
        if place:
            part = combine(scal, ranks, scores, grad_rows, place, addend, *deps)
        else:
            *parts, part = combine_last(scal, ranks, scores, grad_rows, mixed_rows, addend, *deps)
            mixed.extend(parts)
        return part, part

    grads = reduce_scatter(combine_place, "ep")
    grad_hidden, grad_branch, grad_router_leave = middle_back(
        docs, scal, grads, probs, hidden_state, cotangent, low_router, gain_two, route, router_enter, route_leave
    )
    pair = lambda a, b: (a.astype(f32) + b.astype(f32)).astype(bf16)
    mixed = [pair(mixed[j], swap(mixed[j + 1], "ep", 1)) for j in range(0, members, 2)]
    mixed_near, mixed_far = (scatter_even(mixed[: top // 2], "ep"), scatter_even(mixed[top // 2 :], "ep"))

    inside = (queries, keys, values, out_weight, out_enter, out_leave)

    def attend_half_back(half, branch, before, *deps):
        part = slice(half * count, (half + 1) * count)
        atts, logs = ([head[i] for head in heads[part]] for i in (0, 2))
        return attend_back(docs, half, scal, *inside, branch, atts, logs, normed_two_parts[part], before, *deps)

    near = attend_half_back(0, gather_near(grad_branch, "ep"), ())
    branch_far = gather_far(grad_branch, "ep", near[6])
    other_sets = other[local + docs : local + 2 * docs]
    line_sums = sum_experts(docs, other_sets, expert_sums, near[6])
    far = attend_half_back(1, branch_far, near[1:6], line_sums[0])
    mixed_got = swap(fence(mixed_far, branch_far[0]), "ep", top)
    grad_keys, grad_values, *low_grads = far[1:6]
    terms = jnp.concatenate([jnp.concatenate([near[6], far[6]], axis=1), far[7]])
    line = LineSum(line_sums, "grp", LINE, inner)
    got = line.send(1)
    terms = sum_relative(fence(terms, *got, mixed_got), "ep", local)
    line.add(1, got)
    leave_rows = low // members
    leave_parts = jnp.stack([lax.dynamic_slice_in_dim(grad_router_leave, b * leave_rows, leave_rows, 1) for b in blocks])
    leave_parts = jnp.pad(leave_parts.astype(bf16), ((0, 0), (0, 0), (0, slice_width - leave_rows)))
    shared = (projected, squares, terms, gains, cosine, sine, normed_all, low_all, qkv_weight, qkv_enter, qkv_leave)
    ready = line.ready(2)
    *far_parts, enter_sums, leave_sums, projected_grads, low_grad = project_back(
        docs, local, scal, near[0], far[0], grad_keys, grad_values, *shared, leave_parts, *ready
    )
    got = line.send(2, ready)
    line.add(2, got)
    *far_parts, enter_sums, leave_sums = (fence(value, *got) for value in (*far_parts, enter_sums, leave_sums))
    input_far = scatter_even([pair(far_parts[j], swap(far_parts[j + 1], "ep", 1)) for j in range(0, count, 2)], "ep")
    near_parts = project_near(local, projected_grads, low_grad, qkv_weight, qkv_enter, input_far)
    input_got = swap(input_far, "ep", top)
    if count == 2:
        inputs = (near_parts[0], swap(near_parts[1], "ep", 1), input_got)
    else:
        inputs = [pair(near_parts[j], swap(near_parts[j + 1], "ep", 1)) for j in range(0, count, 2)]
        inputs = (scatter_even(inputs, "ep"), input_got)
    grad_input = finish(inputs, grad_hidden, tokens, gain_one)
    layer_out = (hidden_state + (mixed_near.astype(f32) + mixed_got.astype(f32))).astype(bf16)

    got = [fence(value, input_got) for value in line.send(3)]
    line.add(3, got)
    expert_sum = line.total[0]
    by_rows = lambda value: value.astype(bf16).reshape(-1, packs, value.shape[-2] // packs, slice_width).transpose(1, 0, 2, 3)
    joined = jnp.concatenate([by_rows(value) for value in (*low_grads, leave_sums)], axis=1)
    joined = sum_packs(by_place(fence(joined, input_far)), input_got)
    enter_sums = fence(enter_sums, input_far)
    enter_sums = [pair(enter_sums[j], swap(enter_sums[j + 1], "ep", 1)) for j in range(0, members, 2)]
    enter_far = swap(scatter_even(enter_sums[top // 2 :], "ep"), "ep", top)
    enter_sum = fence(pair(scatter_even(enter_sums[: top // 2], "ep"), enter_far), input_got, *got, joined)
    enter_chunks = by_rows(enter_sum[: 3 * low].reshape(3, low, slice_width)).reshape(packs, -1, slice_width)
    leave_chunks = by_rows(enter_sum[3 * low :]).reshape(packs, -1, slice_width)
    enter_sum = sum_packs(by_place(jnp.concatenate([enter_chunks, leave_chunks], axis=1)), last=grad_input)
    enter_rows = 3 * low // packs
    wide = width // packs
    turn = lambda value: jnp.swapaxes(value, -1, -2)
    return (
        layer_out,
        grad_input,
        turn(enter_sum[:enter_rows].reshape(3, -1, slice_width)),
        joined[3:],
        turn(joined[0]),
        joined[1],
        turn(joined[2]),
        turn(enter_sum[enter_rows:, :leave_rows]),
        turn(expert_sum[:, :low, :wide]),
        expert_sum[:, :low, wide:],
        turn(expert_sum[:, low : 2 * low, :wide]),
        expert_sum[:, low : 2 * low, wide:],
        turn(expert_sum[:, 2 * low :, wide:]),
        expert_sum[:, 2 * low :, :wide],
    )


def solution(mesh):
    in_specs = (
        P(("grp", "ep"), None),
        P(("grp", "ep"), None),
        P(),
        P("grp", None),
        P("grp", None),
        P(("grp", "ep"), None),
        P(),
        P(),
        P(),
        P(),
        P(None, None, "ep"),
        P("ep", None),
        P(),
        P("ep", None, None),
        P("ep", None, None),
        P("ep", None, None),
        P(),
        P(None, None, "ep"),
        P("ep", None),
        P(),
        P(),
        P(),
        P("ep", None, None),
        P("ep", None, None),
        P("ep", None, None),
        P("ep", None, None),
        P("ep", None, None),
        P("ep", None, None),
    )
    out_specs = (
        P(("grp", "ep"), None),
        P(("grp", "ep"), None),
        P(None, "ep", "grp"),
        P(None, "grp", "ep"),
        P("ep", "grp"),
        P("grp", "ep"),
        P("ep", "grp"),
        P("ep", "grp"),
        P("ep", "grp", None),
        P("ep", None, "grp"),
        P("ep", "grp", None),
        P("ep", None, "grp"),
        P("ep", "grp", None),
        P("ep", None, "grp"),
    )
    return jax.shard_map(
        per_device, mesh=mesh, in_specs=in_specs, out_specs=out_specs, check_vma=False
    )
```
